32 devices in a mesh: dp: 4 (over x, core), fsdp: 8 (over z, y).
Axes of the slice: x: 2, y: 2, z: 4, core: 2. Of those that a mesh axis runs over, the one named last changes fastest.
Arguments:
- tokens: bfloat16 [256, 256, 384], P(('dp', 'fsdp')), may hold values from -6 to 6
- grid: int32 [256, 2], P(('dp', 'fsdp')), may hold values from 8 to 16
- w_expand: bfloat16 [384, 1536], P('fsdp'), may hold values from -0.3125 to 0.3125
- w_depth: bfloat16 [9, 1536], P(None, 'fsdp'), may hold values from -2 to 2
- w_project: bfloat16 [1536, 384], P('fsdp'), may hold values from -0.15625 to 0.15625
- gain_conv: bfloat16 [384], P('fsdp'), may hold values from 0.25 to 1.75
- bias_conv: bfloat16 [384], P('fsdp'), may hold values from -3 to 3
- gain_attend: bfloat16 [384], P('fsdp'), may hold values from 0.25 to 1.75
- bias_attend: bfloat16 [384], P('fsdp'), may hold values from -3 to 3
- w_qkv: bfloat16 [384, 1152], P('fsdp'), may hold values from -0.3125 to 0.3125
- w_out: bfloat16 [384, 384], P('fsdp'), may hold values from -1.25 to 1.25
- gain_mlp: bfloat16 [384], P('fsdp'), may hold values from 0.25 to 1.75
- bias_mlp: bfloat16 [384], P('fsdp'), may hold values from -3 to 3
- w_up: bfloat16 [384, 1536], P('fsdp'), may hold values from -0.3125 to 0.3125
- w_down: bfloat16 [1536, 384], P('fsdp'), may hold values from -0.15625 to 0.15625
- cotangent: bfloat16 [256, 256, 384], P(('dp', 'fsdp')), may hold values from -6 to 6
Outputs:
- layer_out: bfloat16 [256, 256, 384], P(('dp', 'fsdp'))
- input_grad: bfloat16 [256, 256, 384], P(('dp', 'fsdp'))
- grad_expand: float32 [384, 1536], P('fsdp')
- grad_depth: float32 [9, 1536], P(None, 'fsdp')
- grad_project: float32 [1536, 384], P('fsdp')
- grad_gain_conv: float32 [384], P('fsdp')
- grad_bias_conv: float32 [384], P('fsdp')
- grad_gain_attend: float32 [384], P('fsdp')
- grad_bias_attend: float32 [384], P('fsdp')
- grad_qkv: float32 [384, 1152], P('fsdp')
- grad_out: float32 [384, 384], P('fsdp')
- grad_gain_mlp: float32 [384], P('fsdp')
- grad_bias_mlp: float32 [384], P('fsdp')
- grad_up: float32 [384, 1536], P('fsdp')
- grad_down: float32 [1536, 384], P('fsdp')
The draws below stay inside these ranges and needn't reach their ends.
All inputs are finite; a program needn't handle non-finite values.
Results may differ from the reference program's by a relative error of at most 0.02.
Values may be sent and summed in bfloat16 or wider, within the bound.
A program may use at most 128 MiB of HBM per device.

```python
import jax
import jax.numpy as jnp
from jax import lax

D = 384
HID = 1536
HEADS = 6
HDIM = 64
GRID = 16
ROWS = 256
IMAGES = 256


def touch_ends(values, rng, low, largest):
    shape = values.shape
    index_at = [jax.random.randint(jax.random.fold_in(rng, axis), (), 0, shape[axis]) for axis in range(len(shape))]
    values = values.at[tuple(index_at)].set(low)
    longest = shape.index(max(shape))
    index_at[longest] = (index_at[longest] + 1) % shape[longest]
    return values.at[tuple(index_at)].set(largest)


def level_of(stream_key, shape, cuts, smallest, largest):
    def one(position, blocks):
        steps = jax.random.uniform(jax.random.fold_in(jax.random.fold_in(stream_key, 6), position), (blocks,), jnp.float32, smallest / len(cuts), largest / len(cuts))
        return jnp.repeat(jnp.exp(steps), shape[position] // blocks).reshape((-1,) + (1,) * (len(shape) - position - 1))

    level = one(*cuts[0])
    for cut in cuts[1:]:
        level = level * one(*cut)
    return level


def normal_values(stream_key, dims, scale, limit, shards=(), held_as=jnp.bfloat16):
    entries = jax.random.normal(stream_key, dims, jnp.float32) * scale
    if len(shards) > 0:
        entries = level_of(stream_key, dims, shards, -0.22, 0.18) * entries
    return jnp.clip(entries, min=-limit, max=limit).astype(held_as)


def setup_inputs(seed: int = 0) -> dict:
    streams_of = jax.random.split(jax.random.key(seed), 17)
    tokens = normal_values(streams_of[0], (IMAGES, ROWS, D), 1.0, 6.0, ((0, 32),))
    grid = touch_ends(jax.random.randint(streams_of[1], (IMAGES, 2), GRID // 2, GRID + 1), jax.random.fold_in(streams_of[1], 1), GRID // 2, GRID).astype(jnp.int32)
    w_expand = normal_values(streams_of[2], (D, HID), D ** -0.5, 0.3125, ((0, 8),))
    w_depth = normal_values(streams_of[3], (9, HID), 9 ** -0.5, 2.0, ((1, 8),))
    w_project = normal_values(streams_of[4], (HID, D), HID ** -0.5, 0.15625, ((0, 8),))
    gain_conv = jnp.clip(1.0 + 0.15 * jax.random.normal(streams_of[5], (D,), jnp.float32), 0.25, 1.75).astype(jnp.bfloat16)
    bias_conv = normal_values(streams_of[6], (D,), 0.5, 3.0, ((0, 8),))
    gain_attend = jnp.clip(1.0 + 0.15 * jax.random.normal(streams_of[7], (D,), jnp.float32), 0.25, 1.75).astype(jnp.bfloat16)
    bias_attend = normal_values(streams_of[8], (D,), 0.5, 3.0, ((0, 8),))
    w_qkv = normal_values(streams_of[9], (D, 3 * D), D ** -0.5, 0.3125, ((0, 8),))
    w_out = normal_values(streams_of[10], (D, D), (D // 16) ** -0.5, 1.25, ((0, 8),))
    gain_mlp = jnp.clip(1.0 + 0.15 * jax.random.normal(streams_of[11], (D,), jnp.float32), 0.25, 1.75).astype(jnp.bfloat16)
    bias_mlp = normal_values(streams_of[12], (D,), 0.5, 3.0, ((0, 8),))
    w_up = normal_values(streams_of[13], (D, HID), D ** -0.5, 0.3125, ((0, 8),))
    w_down = normal_values(streams_of[14], (HID, D), HID ** -0.5, 0.15625, ((0, 8),))
    cotangent = normal_values(streams_of[15], (IMAGES, ROWS, D), 1.0, 6.0, ((0, 32),))
    return {"tokens": tokens, "grid": grid, "w_expand": w_expand, "w_depth": w_depth, "w_project": w_project, "gain_conv": gain_conv, "bias_conv": bias_conv, "gain_attend": gain_attend, "bias_attend": bias_attend, "w_qkv": w_qkv, "w_out": w_out, "gain_mlp": gain_mlp, "bias_mlp": bias_mlp, "w_up": w_up, "w_down": w_down, "cotangent": cotangent}


@jax.custom_vjp
def low(v):
    return lax.optimization_barrier(v.astype(jnp.bfloat16)).astype(jnp.float32)

@jax.custom_vjp
def low_back(v):
    return v

def low_keep(v):
    return (low(v), None)

def low_pass(kept, grad):
    return (grad,)

def back_keep(v):
    return (v, None)

def back_low(kept, grad):
    return (low(grad),)
low.defvjp(low_keep, low_pass)
low_back.defvjp(back_keep, back_low)
epsilon = 1e-05

def layer_norm(values, gain, offset):
    center = lax.optimization_barrier(jnp.mean(values, axis=-1, keepdims=True))
    shifted = values - center
    spread = lax.optimization_barrier(jnp.mean(shifted * shifted, axis=-1, keepdims=True))
    return shifted * lax.rsqrt(spread + epsilon) * gain + offset

def depthwise(field, taps):
    side = field.shape[1]
    padded = jnp.pad(field, ((0, 0), (1, 1), (1, 1), (0, 0)))
    total = jnp.zeros_like(field)
    for row_shift in range(3):
        for col_shift in range(3):
            total = total + taps[3 * row_shift + col_shift] * padded[:, row_shift:row_shift + side, col_shift:col_shift + side, :]
    return total

def swish(values):
    return values * jax.nn.sigmoid(values)

def smooth_gelu(values):
    return 0.5 * values * (1.0 + jnp.tanh(0.7978845608028654 * (values + 0.044715 * values * values * values)))

def image_valid(grid):
    places = jnp.arange(GRID * GRID, dtype=jnp.int32)
    return (places[None, :] // GRID < grid[:, 0:1]) & (places[None, :] % GRID < grid[:, 1:2])

def mixing(left, right):
    return jnp.einsum('bri,io->bro', left, right, precision=lax.Precision.HIGHEST)

def layer(params, images, valid):
    w_expand, w_depth, w_project, gain_conv, bias_conv, gain_attend, bias_attend, w_qkv, w_out, gain_mlp, bias_mlp, w_up, w_down = params
    keeper = valid.astype(jnp.float32)[..., None]
    count, rows, width = images.shape
    expanded = low_back(mixing(images, w_expand)) * keeper
    convolved = depthwise(expanded.reshape(count, GRID, GRID, -1), w_depth).reshape(count, rows, -1)
    activated = low(swish(convolved))
    projected = low_back(mixing(activated, w_project))
    first = images + keeper * layer_norm(projected, gain_conv, bias_conv)
    normed = low(layer_norm(first, gain_attend, bias_attend))
    packed = low(low_back(mixing(normed, w_qkv)))
    query = packed[..., :width].reshape(count, rows, HEADS, HDIM)
    key_part = packed[..., width:2 * width].reshape(count, rows, HEADS, HDIM)
    value_part = packed[..., 2 * width:].reshape(count, rows, HEADS, HDIM)
    scores = jnp.einsum('bqhd,bkhd->bhqk', query, key_part, precision=lax.Precision.HIGHEST) * HDIM ** (-0.5)
    scores = low_back(jnp.where(valid[:, None, None, :], scores, -1000000000.0))
    highest = lax.optimization_barrier(jnp.max(scores, axis=-1, keepdims=True))
    expo = jnp.exp(scores - highest)
    probs = low(expo / lax.optimization_barrier(jnp.sum(expo, axis=-1, keepdims=True)))
    attended = jnp.einsum('bhqk,bkhd->bqhd', probs, value_part, precision=lax.Precision.HIGHEST).reshape(count, rows, width)
    attended = low(low_back(attended))
    second = first + keeper * low_back(mixing(attended, w_out))
    normed3 = low(layer_norm(second, gain_mlp, bias_mlp))
    hidden = low(smooth_gelu(low_back(mixing(normed3, w_up))))
    return second + keeper * low_back(mixing(hidden, w_down))

def reference(tokens, grid, w_expand, w_depth, w_project, gain_conv, bias_conv, gain_attend, bias_attend, w_qkv, w_out, gain_mlp, bias_mlp, w_up, w_down, cotangent):
    params = tuple((weight.astype(jnp.float32) for weight in (w_expand, w_depth, w_project, gain_conv, bias_conv, gain_attend, bias_attend, w_qkv, w_out, gain_mlp, bias_mlp, w_up, w_down)))
    valid = image_valid(grid)
    block = 16
    groups = tokens.shape[0] // block
    images = tokens.astype(jnp.float32).reshape(groups, block, ROWS, D)
    valids = valid.reshape(groups, block, ROWS)
    checked = jax.checkpoint(layer)

    def forward(weights, inputs):
        return lax.map(lambda pieces: checked(weights, pieces[0], pieces[1]), (inputs, valids))
    outputs, pullback = jax.vjp(forward, params, images)
    grads, d_images = pullback(cotangent.astype(jnp.float32).reshape(outputs.shape))
    return (outputs.reshape(tokens.shape).astype(jnp.bfloat16), d_images.reshape(tokens.shape).astype(jnp.bfloat16), grads[0], grads[1], grads[2], grads[3], grads[4], grads[5], grads[6], grads[7], grads[8], grads[9], grads[10], grads[11], grads[12])
```

```python
import functools

import jax
import jax.numpy as jnp
from jax import lax
from jax.experimental import pallas as pl
from jax.experimental.pallas import tpu as pltpu
from jax.sharding import PartitionSpec as P

HDIM = 64
GRID = 16
ROWS = GRID * GRID
CHUNK = 256
EPSILON = 1e-05
VMEM_BYTES = 60 * 1024 * 1024
F32 = jnp.float32
BF16 = jnp.bfloat16


def dot_nn(left, right):
    return jnp.dot(left, right, preferred_element_type=F32)


def dot_nt(left, right):
    return lax.dot_general(left, right, (((1,), (1,)), ((), ())), preferred_element_type=F32)


def dot_tn(left, right):
    return lax.dot_general(left, right, (((0,), (0,)), ((), ())), preferred_element_type=F32)


def valid_cells(high, wide, shape):
    place = lax.broadcasted_iota(jnp.int32, shape, 0)
    return (place // GRID < high) & (place % GRID < wide)


def normalized(values):
    center = jnp.mean(values, axis=-1, keepdims=True)
    shifted = values - center
    spread = jnp.mean(shifted * shifted, axis=-1, keepdims=True)
    inverse = lax.rsqrt(spread + EPSILON)
    return shifted * inverse, inverse


def norm_pull(grad, gain, unit, inverse):
    scaled = grad * gain
    mean_plain = jnp.mean(scaled, axis=-1, keepdims=True)
    mean_unit = jnp.mean(scaled * unit, axis=-1, keepdims=True)
    return (scaled - mean_plain - unit * mean_unit) * inverse


def fold_rows(values):
    rows, width = values.shape
    return jnp.sum(values.reshape(rows // 8, 8, width), axis=0)


def move_cells(values, step):
    rows, width = values.shape
    parts = values.reshape(rows // GRID, 2, 8, width)
    turned = pltpu.roll(parts, step % 8, axis=2)
    first, last = turned[:, 0:1], turned[:, 1:2]
    line = lax.broadcasted_iota(jnp.int32, first.shape, 2)
    if step == 1:
        edge = line == 0
        moved = jnp.concatenate((jnp.where(edge, 0.0, first), jnp.where(edge, first, last)), axis=1)
    else:
        edge = line == 7
        moved = jnp.concatenate((jnp.where(edge, last, first), jnp.where(edge, 0.0, last)), axis=1)
    return moved.reshape(rows, width)


def conv_forward_kernel(
    grid_ref, tokens_ref, expand_ref, taps_ref, project_ref, norms_ref,
    field_ref, act_ref, pull_ref, projected_ref, first_ref, frame,
):
    image = pl.program_id(0)
    width = tokens_ref.shape[1]
    hidden = expand_ref.shape[1]
    valid = valid_cells(grid_ref[image, 0], grid_ref[image, 1], (ROWS, width))
    tokens = tokens_ref[...]
    kept = jnp.where(valid, tokens, jnp.zeros_like(tokens))
    projected = jnp.zeros((ROWS, width), F32)
    edge = jnp.zeros((GRID, CHUNK), F32)
    for chunk in range(hidden // CHUNK):
        slot = chunk % 2
        columns = slice(chunk * CHUNK, (chunk + 1) * CHUNK)
        expanded = dot_nn(kept, expand_ref[:, columns])
        field_ref[chunk] = expanded.astype(BF16)
        frame[slot, 0:GRID] = edge
        frame[slot, GRID : GRID + ROWS] = expanded
        frame[slot, GRID + ROWS :] = edge
        for half in range(CHUNK // 128):
            lanes = slice(half * 128, (half + 1) * 128)
            whole = slice(chunk * CHUNK + half * 128, chunk * CHUNK + (half + 1) * 128)
            taps = [taps_ref[k : k + 1, whole] for k in range(9)]
            block = 64
            for start in range(0, ROWS, block):
                near = [frame[slot, start + GRID * a : start + GRID * a + block, lanes] for a in range(3)]
                sums = [sum(taps[3 * a + b] * near[a] for a in range(3)) for b in range(3)]
                conv = sums[1] + move_cells(sums[0], 1) + move_cells(sums[2], -1)
                gate = 0.5 * jnp.tanh(0.5 * conv) + 0.5
                act = conv * gate
                act_ref[chunk, start : start + block, lanes] = act.astype(BF16)
                pull_ref[chunk, start : start + block, lanes] = (gate + act * (1.0 - gate)).astype(BF16)
        projected = projected + dot_nn(act_ref[chunk], project_ref[columns, :])
    projected_ref[...] = projected
    unit, _ = normalized(projected)
    shift = unit * norms_ref[0:1, :] + norms_ref[1:2, :]
    first_ref[...] = tokens.astype(F32) + jnp.where(valid, shift, 0.0)


def whole(shape):
    return pl.BlockSpec(shape, lambda *_: (0,) * len(shape), pipeline_mode=pl.Buffered(1))


def conv_forward(grid, tokens, w_expand, taps, w_project, norms):
    rows, width = tokens.shape
    hidden = w_expand.shape[1]
    chunks = hidden // CHUNK
    per_image = pl.BlockSpec((ROWS, width), lambda i: (i, 0))
    per_chunk = pl.BlockSpec((chunks, ROWS, CHUNK), lambda i: (0, i, 0))
    wide = jax.ShapeDtypeStruct((chunks, rows, CHUNK), BF16)
    return pl.pallas_call(
        conv_forward_kernel,
        grid=(rows // ROWS,),
        in_specs=[
            pl.BlockSpec(memory_space=pltpu.SMEM),
            per_image,
            whole(w_expand.shape),
            whole(taps.shape),
            whole(w_project.shape),
            whole(norms.shape),
        ],
        out_specs=[per_chunk, per_chunk, per_chunk, per_image, per_image],
        out_shape=[
            wide,
            wide,
            wide,
            jax.ShapeDtypeStruct((rows, width), F32),
            jax.ShapeDtypeStruct((rows, width), F32),
        ],
        scratch_shapes=[pltpu.VMEM((2, ROWS + 2 * GRID, CHUNK), F32)],
        compiler_params=pltpu.CompilerParams(vmem_limit_bytes=VMEM_BYTES),
        name="conv_forward",
    )(grid, tokens, w_expand, taps, w_project, norms)


def middle_kernel(
    grid_ref, first_ref, cotan_ref, mixed_ref, up_ref, down_ref, norms_ref,
    layer_ref, d_first_ref, g_mixed_ref, g_up_ref, g_down_ref, g_norm_ref,
    a_mixed, a_up, a_down, expo, keys, values, queries, attended_t, d_qkv,
):
    image = pl.program_id(0)
    width = first_ref.shape[1]
    hidden = up_ref.shape[1]
    pairs = width // 128

    @pl.when(image == 0)
    def _():
        for ref in (a_mixed, a_up, a_down, g_norm_ref):
            ref[...] = jnp.zeros_like(ref)

    high, wide = grid_ref[image, 0], grid_ref[image, 1]
    valid = valid_cells(high, wide, (ROWS, width))
    first = first_ref[...]
    unit1, inverse1 = normalized(first)
    normed = (unit1 * norms_ref[2:3, :] + norms_ref[3:4, :]).astype(BF16)
    packed = dot_nn(normed, mixed_ref[:, : 3 * width]).astype(BF16)
    lane = lax.broadcasted_iota(jnp.int32, (ROWS, 128), 1) // HDIM
    line = lax.broadcasted_iota(jnp.int32, (128, ROWS), 0) // HDIM
    zero = jnp.zeros((ROWS, 128), BF16)
    key_bias = jnp.where(valid_cells(high, wide, (ROWS, ROWS)), 0.0, -1e9)
    key_bias = jnp.concatenate((key_bias, key_bias), axis=0)
    inverses = []
    for pair in range(pairs):
        at = pair * 128
        query = packed[:, at : at + 128] * jnp.asarray(HDIM**-0.5, BF16)
        key = packed[:, width + at : width + at + 128]
        value = packed[:, 2 * width + at : 2 * width + at + 128]
        for head in range(2):
            keys[pair, head * ROWS : (head + 1) * ROWS] = jnp.where(lane == head, key, zero)
            values[pair, head * ROWS : (head + 1) * ROWS] = jnp.where(lane == head, value, zero)
            queries[pair, head * ROWS : (head + 1) * ROWS] = jnp.where(lane == head, query, zero)
        scores = dot_nt(keys[pair], query) + key_bias
        totals = []
        for head in range(2):
            part = scores[head * ROWS : (head + 1) * ROWS]
            power = jnp.exp(part - jnp.max(part, axis=0, keepdims=True))
            totals.append(1.0 / jnp.sum(power, axis=0, keepdims=True))
            expo[pair, head * ROWS : (head + 1) * ROWS] = power.astype(BF16)
        inverse = jnp.where(line == 0, totals[0], totals[1])
        inverses.append(inverse)
        attended_t[at : at + 128] = (dot_tn(values[pair], expo[pair]) * inverse).astype(BF16)
    second = first + jnp.where(valid, dot_tn(attended_t[...], mixed_ref[:, 3 * width :]), 0.0)

    cotan = cotan_ref[...]
    unit2, inverse2 = normalized(second)
    normed3 = (unit2 * norms_ref[4:5, :] + norms_ref[5:6, :]).astype(BF16)
    d_down = jnp.where(valid, cotan, jnp.zeros_like(cotan))
    normed3_t = normed3.T
    d_down_t = d_down.T
    result = jnp.zeros((ROWS, width), F32)
    d_normed3 = jnp.zeros((ROWS, width), F32)
    for chunk in range(hidden // CHUNK):
        columns = slice(chunk * CHUNK, (chunk + 1) * CHUNK)
        upper = dot_nn(normed3, up_ref[:, columns])
        d_hidden = dot_nt(d_down, down_ref[columns, :])
        square = upper * upper
        bent = jnp.tanh(upper * (0.7978845608028654 + (0.7978845608028654 * 0.044715) * square))
        gate = 0.5 * bent + 0.5
        hid = (upper * gate).astype(BF16)
        slope = gate + upper * (gate - gate * gate) * (
            2 * 0.7978845608028654 + (6 * 0.7978845608028654 * 0.044715) * square
        )
        d_upper = (d_hidden * slope).astype(BF16)
        result = result + dot_nn(hid, down_ref[columns, :])
        a_down[:, columns] += dot_nn(d_down_t, hid)
        a_up[:, columns] += dot_nn(normed3_t, d_upper)
        d_normed3 = d_normed3 + dot_nt(d_upper, up_ref[:, columns])
    layer_ref[...] = (second + jnp.where(valid, result, 0.0)).astype(BF16)

    g_norm_ref[0:8] += fold_rows(d_normed3 * unit2)
    g_norm_ref[8:16] += fold_rows(d_normed3)
    d_second = cotan.astype(F32) + norm_pull(d_normed3, norms_ref[4:5, :], unit2, inverse2)

    d_out = jnp.where(valid, d_second, 0.0).astype(BF16)
    a_mixed[:, 3 * width :] += dot_nn(attended_t[...], d_out)
    for pair in range(pairs):
        at = pair * 128
        d_attended = dot_nt(mixed_ref[at : at + 128, 3 * width :], d_out)
        inverse = inverses[pair]
        d_low = d_attended.astype(BF16)
        inner = d_low.astype(F32) * attended_t[at : at + 128].astype(F32)
        d_scaled = d_low.astype(F32) * inverse
        d_scaled_low = d_scaled.astype(BF16)
        inner = inner * inverse
        deltas = [jnp.sum(inner[head * HDIM : (head + 1) * HDIM], axis=0, keepdims=True) for head in range(2)]
        d_probs = dot_nn(values[pair], d_scaled_low)
        d_value = jnp.zeros((ROWS, 128), F32)
        d_key = jnp.zeros((ROWS, 128), F32)
        steps = []
        for head in range(2):
            rows = slice(head * ROWS, (head + 1) * ROWS)
            power = expo[pair, rows]
            d_score = (power.astype(F32) * (d_probs[rows] - deltas[head])).astype(BF16)
            steps.append(d_score)
            own = jnp.where(line == head, d_scaled_low, jnp.zeros_like(d_scaled_low))
            d_value = d_value + dot_nt(power, own)
            d_key = d_key + dot_nn(d_score, queries[pair, rows])
        d_query_t = dot_tn(keys[pair], jnp.concatenate(steps, axis=0)) * (HDIM**-0.5)
        d_qkv[:, at : at + 128] = d_query_t.astype(BF16).T
        d_qkv[:, width + at : width + at + 128] = d_key.astype(BF16)
        d_qkv[:, 2 * width + at : 2 * width + at + 128] = d_value.astype(BF16)
    a_mixed[:, : 3 * width] += dot_nn(normed.T, d_qkv[...])
    d_normed = dot_nt(d_qkv[...], mixed_ref[:, : 3 * width])
    g_norm_ref[16:24] += fold_rows(d_normed * unit1)
    g_norm_ref[24:32] += fold_rows(d_normed)
    d_first_ref[...] = d_second + norm_pull(d_normed, norms_ref[2:3, :], unit1, inverse1)

    @pl.when(image == pl.num_programs(0) - 1)
    def _():
        g_mixed_ref[...] = a_mixed[...].astype(BF16)
        g_up_ref[...] = a_up[...].astype(BF16)
        g_down_ref[...] = a_down[...].astype(BF16).T


def middle(grid, first, cotangent, w_mixed, w_up, w_down, norms):
    rows, width = first.shape
    hidden = w_up.shape[1]
    pairs = width // 128
    per_image = pl.BlockSpec((ROWS, width), lambda i: (i, 0))
    weights = (w_mixed, w_up, w_down)
    return pl.pallas_call(
        middle_kernel,
        grid=(rows // ROWS,),
        in_specs=[pl.BlockSpec(memory_space=pltpu.SMEM), per_image, per_image]
        + [whole(weight.shape) for weight in weights]
        + [whole(norms.shape)],
        out_specs=[per_image, per_image] + [whole(weight.shape) for weight in weights] + [whole((32, width))],
        out_shape=[jax.ShapeDtypeStruct((rows, width), BF16), jax.ShapeDtypeStruct((rows, width), F32)]
        + [jax.ShapeDtypeStruct(weight.shape, BF16) for weight in weights]
        + [jax.ShapeDtypeStruct((32, width), F32)],
        scratch_shapes=[
            pltpu.VMEM(w_mixed.shape, F32),
            pltpu.VMEM(w_up.shape, F32),
            pltpu.VMEM((width, hidden), F32),
            pltpu.VMEM((pairs, 2 * ROWS, ROWS), BF16),
            pltpu.VMEM((pairs, 2 * ROWS, 128), BF16),
            pltpu.VMEM((pairs, 2 * ROWS, 128), BF16),
            pltpu.VMEM((pairs, 2 * ROWS, 128), BF16),
            pltpu.VMEM((width, ROWS), BF16),
            pltpu.VMEM((ROWS, 3 * width), BF16),
        ],
        compiler_params=pltpu.CompilerParams(vmem_limit_bytes=VMEM_BYTES),
        name="middle",
    )(grid, first, cotangent, *weights, norms)


def conv_backward_kernel(
    grid_ref, tokens_ref, d_first_ref, projected_ref, field_ref, act_ref, pull_ref,
    expand_ref, taps_ref, project_ref, norms_ref,
    d_tokens_ref, g_expand_ref, g_project_ref, g_taps_ref, g_norm_ref,
    d_proj, d_proj_t, tokens_t, d_image, frames, a_expand, a_project,
):
    chunk = pl.program_id(0)
    last = pl.num_programs(0) - 1
    rows, width = tokens_ref.shape
    images = rows // ROWS

    @pl.when(chunk == 0)
    def _():
        g_norm_ref[...] = jnp.zeros_like(g_norm_ref)
        frames[...] = jnp.zeros_like(frames)

        @pl.loop(0, images)
        def _(image):
            here = pl.ds(pl.multiple_of(image * ROWS, ROWS), ROWS)
            valid = valid_cells(grid_ref[image, 0], grid_ref[image, 1], (ROWS, width))
            unit, inverse = normalized(projected_ref[here, :])
            grad = jnp.where(valid, d_first_ref[here, :], 0.0)
            g_norm_ref[0:8] += fold_rows(grad * unit)
            g_norm_ref[8:16] += fold_rows(grad)
            low = norm_pull(grad, norms_ref[0:1, :], unit, inverse).astype(BF16)
            d_proj[image] = low
            d_proj_t[image] = low.T
            tokens_t[image] = tokens_ref[here, :].T

    a_expand[...] = jnp.zeros_like(a_expand)
    a_project[...] = jnp.zeros_like(a_project)
    g_taps_ref[...] = jnp.zeros_like(g_taps_ref)

    @pl.loop(0, images)
    def _(image):
        here = pl.ds(pl.multiple_of(image * ROWS, ROWS), ROWS)
        d_act = dot_nt(d_proj[image], project_ref[...])
        d_conv = d_act * pull_ref[0, here, :].astype(F32)
        frames[1, GRID : GRID + ROWS] = d_conv
        frames[0, GRID : GRID + ROWS] = move_cells(d_conv, -1)
        frames[2, GRID : GRID + ROWS] = move_cells(d_conv, 1)
        field = field_ref[0, here, :].astype(F32)
        valid = valid_cells(grid_ref[image, 0], grid_ref[image, 1], (ROWS, 128))
        parts = []
        for half in range(CHUNK // 128):
            lanes = slice(half * 128, (half + 1) * 128)
            taps = [taps_ref[k : k + 1, lanes] for k in range(9)]
            totals = [jnp.zeros((8, 128), F32) for _ in range(9)]
            block = 64
            stack = []
            for start in range(0, ROWS, block):
                own = field[start : start + block, lanes]
                grad = jnp.zeros((block, 128), F32)
                for a in range(3):
                    for b in range(3):
                        at = start + GRID * (2 - a)
                        near = frames[b, at : at + block, lanes]
                        grad = grad + taps[3 * a + b] * near
                        totals[3 * a + b] = totals[3 * a + b] + fold_rows(near * own)
                stack.append(jnp.where(valid[start : start + block], grad, 0.0).astype(BF16))
            parts.append(jnp.concatenate(stack, axis=0))
            for k in range(9):
                g_taps_ref[8 * k : 8 * k + 8, lanes] += totals[k]
        d_field = jnp.concatenate(parts, axis=1)
        a_project[...] += dot_nn(d_proj_t[image], act_ref[0, here, :])
        a_expand[...] += dot_nn(tokens_t[image], d_field)
        more = dot_nt(d_field, expand_ref[...])

        @pl.when(chunk == 0)
        def _():
            d_image[image] = d_first_ref[here, :] + more

        @pl.when((chunk > 0) & (chunk < last))
        def _():
            d_image[image] += more

        @pl.when(chunk == last)
        def _():
            d_tokens_ref[here, :] = (d_image[image] + more).astype(BF16)

    g_expand_ref[...] = a_expand[...].astype(BF16)
    g_project_ref[...] = a_project[...].astype(BF16).T


def conv_backward(grid, tokens, d_first, projected, field, act, pull, w_expand, taps, w_project, norms):
    rows, width = tokens.shape
    hidden = w_expand.shape[1]
    images = rows // ROWS
    per_chunk = pl.BlockSpec((1, rows, CHUNK), lambda c: (c, 0, 0))
    columns = pl.BlockSpec((width, CHUNK), lambda c: (0, c))
    lines = pl.BlockSpec((CHUNK, width), lambda c: (c, 0))
    full = whole((rows, width))
    return pl.pallas_call(
        conv_backward_kernel,
        grid=(hidden // CHUNK,),
        in_specs=[
            pl.BlockSpec(memory_space=pltpu.SMEM),
            full,
            full,
            full,
            per_chunk,
            per_chunk,
            per_chunk,
            columns,
            pl.BlockSpec((taps.shape[0], CHUNK), lambda c: (0, c)),
            lines,
            whole(norms.shape),
        ],
        out_specs=[full, columns, lines, pl.BlockSpec((72, CHUNK), lambda c: (0, c)), whole((16, width))],
        out_shape=[
            jax.ShapeDtypeStruct((rows, width), BF16),
            jax.ShapeDtypeStruct(w_expand.shape, BF16),
            jax.ShapeDtypeStruct(w_project.shape, BF16),
            jax.ShapeDtypeStruct((72, hidden), F32),
            jax.ShapeDtypeStruct((16, width), F32),
        ],
        scratch_shapes=[
            pltpu.VMEM((images, ROWS, width), BF16),
            pltpu.VMEM((images, width, ROWS), BF16),
            pltpu.VMEM((images, width, ROWS), BF16),
            pltpu.VMEM((images, ROWS, width), F32),
            pltpu.VMEM((3, ROWS + 2 * GRID, CHUNK), F32),
            pltpu.VMEM((width, CHUNK), F32),
            pltpu.VMEM((width, CHUNK), F32),
        ],
        compiler_params=pltpu.CompilerParams(vmem_limit_bytes=VMEM_BYTES),
        name="conv_backward",
    )(grid, tokens, d_first, projected, field, act, pull, w_expand, taps, w_project, norms)


MESH = pl.DeviceIdType.MESH


def places(sides):
    dp, fsdp = lax.axis_index("dp"), lax.axis_index("fsdp")
    return dp // 2, dp % 2, fsdp // sides, fsdp % sides


def half_of(ref, lead, part):
    rows, columns = ref.shape[-2:]
    if columns > rows * 4:
        size = columns // 2
        return ref.at[lead + (slice(None), pl.ds(pl.multiple_of(part * size, 128), size))]
    size = rows // 2
    return ref.at[lead + (pl.ds(pl.multiple_of(part * size, 8), size), slice(None))]


def half_shape(shape):
    rows, columns = shape
    return (rows, columns // 2) if columns > rows * 4 else (rows // 2, columns)


def remote(source, target, sends, receives, index, device):
    return pltpu.make_async_remote_copy(
        src_ref=source,
        dst_ref=target,
        send_sem=sends.at[index],
        recv_sem=receives.at[index],
        device_id=device,
        device_id_type=MESH,
    )


def greet(devices):
    barrier = pltpu.get_barrier_semaphore()
    for device in devices:
        pl.semaphore_signal(barrier, inc=1, device_id=device, device_id_type=MESH)
    pl.semaphore_wait(barrier, len(devices))


def peers_of(layers):
    x, core, z, y = places(2)
    dp, fsdp = x * 2 + core, z * 2 + y
    along = [(dp, (z ^ step) * 2 + y) for step in range(1, layers)]
    return along, (dp, z * 2 + 1 - y), (x * 2 + 1 - core, fsdp), ((1 - x) * 2 + core, fsdp)


class Gather:
    def __init__(self, shard, full, sems, number):
        self.shard, self.full = shard, full
        self.layers = full.shape[0]
        base = number * (2 * self.layers + 2)
        sends, receives, local = sems
        self.x, self.core, self.z, self.y = places(2)
        along, self.across, self.sibling, _ = peers_of(self.layers)
        own = half_of(shard, (), self.core)
        self.local = pltpu.make_async_copy(own, self.part(self.z, self.y), local.at[number])
        self.along = [
            remote(own, self.part(self.z, self.y), sends, receives, base + step, along[step])
            for step in range(self.layers - 1)
        ]
        base += self.layers - 1
        self.over = []
        for step in range(self.layers):
            target = self.part(self.z ^ step, self.y)
            self.over.append(remote(own if step == 0 else target, target, sends, receives, base + step, self.across))
        base += self.layers
        self.inside = []
        for step, side in enumerate((self.y, 1 - self.y)):
            target = half_of(full, (slice(None), side), self.core)
            self.inside.append(remote(target, target, sends, receives, base + step, self.sibling))

    def part(self, z, y):
        return half_of(self.full, (z, y), self.core)

    def start(self):
        for copy in self.along:
            copy.start()
        self.over[0].start()
        self.local.start()

    def forward(self):
        for step, copy in enumerate(self.along):
            copy.wait_recv()
            self.over[step + 1].start()
        self.local.wait()
        self.inside[0].start()

    def share(self):
        for copy in self.over:
            copy.wait_recv()
        self.inside[1].start()

    def finish(self):
        for copy in self.inside:
            copy.wait_recv()

    def drain(self):
        for copy in self.along + self.over + self.inside:
            copy.wait_send()


def gather_kernel(count, *refs):
    shards, fulls, sems = refs[:count], refs[count : 2 * count], refs[2 * count :]
    along, across, sibling, _ = peers_of(fulls[0].shape[0])
    greet(along + [across, sibling])
    parts = [Gather(shards[i], fulls[i], sems, i) for i in range(count)]
    for part in parts:
        part.start()
    for part in parts:
        part.forward()
    for part in parts:
        part.share()
    for part in parts:
        part.finish()
    for part in parts:
        part.drain()


def gather(shards, layers):
    count = len(shards)
    anywhere = pl.BlockSpec(memory_space=pl.ANY)
    copies = count * (2 * layers + 2)
    return pl.pallas_call(
        functools.partial(gather_kernel, count),
        in_specs=[anywhere] * count,
        out_specs=[anywhere] * count,
        out_shape=[jax.ShapeDtypeStruct((layers, 2) + shard.shape, shard.dtype) for shard in shards],
        scratch_shapes=[
            pltpu.SemaphoreType.DMA((copies,)),
            pltpu.SemaphoreType.DMA((copies,)),
            pltpu.SemaphoreType.DMA((count,)),
        ],
        compiler_params=pltpu.CompilerParams(collective_id=0, has_side_effects=True),
        name="gather_weights",
    )(*shards)


class Reduce:
    def __init__(self, terms, result, buffers, sems, number):
        self.terms, self.result = terms, result
        self.from_core, self.chip, self.from_side, self.line, self.from_along, self.own, self.from_x, self.total = buffers
        self.layers = terms.shape[0]
        base = number * (self.layers + 3)
        sends, receives = sems
        self.x, self.core, self.z, self.y = places(2)
        along, across, sibling, beyond = peers_of(self.layers)
        other = half_of(terms, (slice(None), slice(None)), 1 - self.core)
        self.inside = remote(other, self.from_core, sends, receives, base, sibling)
        self.over = remote(self.chip.at[:, 1 - self.y], self.from_side, sends, receives, base + 1, across)
        self.along = [
            remote(self.line.at[self.z ^ (step + 1)], self.from_along.at[step], sends, receives, base + 2 + step, along[step])
            for step in range(self.layers - 1)
        ]
        base += self.layers + 1
        self.beyond = remote(self.own, self.from_x, sends, receives, base, beyond)
        self.back = remote(self.total, half_of(result, (), self.core), sends, receives, base + 1, sibling)

    def start(self):
        self.inside.start()

    def add_chip(self):
        self.inside.wait_recv()
        for z in range(self.layers):
            for y in range(2):
                mine = half_of(self.terms, (z, y), self.core)[...].astype(F32)
                self.chip[z, y] = (mine + self.from_core[z, y].astype(F32)).astype(self.chip.dtype)
        self.over.start()

    def add_side(self):
        self.over.wait_recv()
        for z in range(self.layers):
            mine = self.chip[z, self.y].astype(F32)
            self.line[z] = (mine + self.from_side[z].astype(F32)).astype(self.line.dtype)
        for copy in self.along:
            copy.start()

    def add_line(self):
        mine = self.line[self.z].astype(F32)
        for step, copy in enumerate(self.along):
            copy.wait_recv()
            mine = mine + self.from_along[step].astype(F32)
        self.own[...] = mine.astype(self.own.dtype)
        self.beyond.start()

    def add_x(self):
        self.beyond.wait_recv()
        self.total[...] = self.own[...].astype(F32) + self.from_x[...].astype(F32)
        self.back.start()
        half_of(self.result, (), self.core)[...] = self.total[...]

    def finish(self):
        self.back.wait_recv()
        for copy in [self.inside, self.over, self.beyond, self.back] + self.along:
            copy.wait_send()


def reduce_kernel(count, *refs):
    terms, results, rest = refs[:count], refs[count : 2 * count], refs[2 * count :]
    sems = rest[8 * count :]
    along, across, sibling, beyond = peers_of(terms[0].shape[0])
    greet(along + [across, sibling, beyond])
    parts = [Reduce(terms[i], results[i], rest[8 * i : 8 * i + 8], sems, i) for i in range(count)]
    for stage in ("start", "add_chip", "add_side", "add_line", "add_x", "finish"):
        for part in parts:
            getattr(part, stage)()


def reduce_buffers(shape, dtype):
    layers, sides = shape[:2]
    half = half_shape(shape[2:])
    return [
        pltpu.VMEM((layers, sides) + half, dtype),
        pltpu.VMEM((layers, sides) + half, dtype),
        pltpu.VMEM((layers,) + half, dtype),
        pltpu.VMEM((layers,) + half, dtype),
        pltpu.VMEM((layers - 1,) + half, dtype),
        pltpu.VMEM(half, dtype),
        pltpu.VMEM(half, dtype),
        pltpu.VMEM(half, F32),
    ]


def reduce(terms):
    count = len(terms)
    layers = terms[0].shape[0]
    copies = count * (layers + 3)
    here = pl.BlockSpec(memory_space=pltpu.VMEM)
    scratch = []
    for term in terms:
        scratch += reduce_buffers(term.shape, term.dtype)
    return pl.pallas_call(
        functools.partial(reduce_kernel, count),
        in_specs=[here] * count,
        out_specs=[here] * count,
        out_shape=[jax.ShapeDtypeStruct(term.shape[2:], F32) for term in terms],
        scratch_shapes=scratch + [pltpu.SemaphoreType.DMA((copies,)), pltpu.SemaphoreType.DMA((copies,))],
        compiler_params=pltpu.CompilerParams(collective_id=1, has_side_effects=True, vmem_limit_bytes=VMEM_BYTES),
        name="reduce_gradients",
    )(*terms)


def gather_plain(shards, fsdp):
    return [lax.all_gather(shard, "fsdp", axis=0).reshape((1, fsdp) + shard.shape) for shard in shards]


def reduce_plain(terms):
    results = []
    for term in terms:
        flat = term.reshape((-1,) + term.shape[2:])
        share = lax.psum_scatter(flat, "fsdp", scatter_dimension=0, tiled=False)
        results.append(lax.psum(share, "dp").astype(F32))
    return results


def local(
    fsdp, quick,
    tokens, grid, w_expand, w_depth, w_project, gain_conv, bias_conv, gain_attend, bias_attend,
    w_qkv, w_out, gain_mlp, bias_mlp, w_up, w_down, cotangent,
):
    slots, rows, width = tokens.shape
    hidden = w_expand.shape[1]
    share, thin = w_depth.shape[1], gain_conv.shape[0]
    span = -(-share // 128) * 128
    lines = [jnp.pad(w_depth, ((0, 0), (0, span - share)))]
    for vector in (gain_conv, bias_conv, gain_attend, bias_attend, gain_mlp, bias_mlp):
        lines.append(jnp.pad(vector, (0, span - thin))[None, :])
    lines.append(jnp.zeros((1, span), w_depth.dtype))
    small = jnp.concatenate(lines, axis=0).astype(F32)
    mixed = jnp.concatenate((w_qkv, w_out), axis=1)
    shards = [small, w_expand, w_project, mixed, w_up, w_down]
    if quick:
        layers = fsdp // 2
        fulls = gather(shards, layers)
    else:
        layers = 1
        fulls = gather_plain(shards, fsdp)
    shapes = [full.shape for full in fulls]
    small = fulls[0].reshape(fsdp, 16, span)
    f_expand, f_project, f_mixed, f_up, f_down = [
        full.reshape(fsdp * full.shape[2], full.shape[3]) for full in fulls[1:]
    ]
    taps = jnp.pad(small[:, :9, :share].transpose(1, 0, 2).reshape(9, hidden), ((0, 7), (0, 0)))
    norms = jnp.pad(small[:, 9:15, :thin].transpose(1, 0, 2).reshape(6, width), ((0, 2), (0, 0)))
    flat, cotan = tokens.reshape(slots * rows, width), cotangent.reshape(slots * rows, width)
    field, act, pull, projected, first = conv_forward(grid, flat, f_expand, taps, f_project, norms)
    layer_out, d_first, g_mixed, g_up, g_down, g_norm = middle(grid, first, cotan, f_mixed, f_up, f_down, norms)
    d_tokens, g_expand, g_project, g_taps, g_norm_conv = conv_backward(
        grid, flat, d_first, projected, field, act, pull, f_expand, taps, f_project, norms
    )
    g_taps = jnp.sum(g_taps.reshape(9, 8, fsdp, share), axis=1)
    g_norm = jnp.concatenate((g_norm_conv, g_norm[16:], g_norm[:16]), axis=0)
    g_norm = jnp.sum(g_norm.reshape(6, 8, fsdp, thin), axis=1)
    g_small = jnp.concatenate(
        (
            jnp.pad(g_taps, ((0, 0), (0, 0), (0, span - share))),
            jnp.pad(g_norm, ((0, 1), (0, 0), (0, span - thin))),
        ),
        axis=0,
    ).transpose(1, 0, 2)
    terms = [
        term.reshape(shape) for term, shape in zip((g_small, g_expand, g_project, g_mixed, g_up, g_down), shapes)
    ]
    small, s_expand, s_project, s_mixed, s_up, s_down = (reduce if quick else reduce_plain)(terms)
    return (
        layer_out.reshape(tokens.shape),
        d_tokens.reshape(tokens.shape),
        s_expand,
        small[:9, :share],
        s_project,
        small[9, :thin],
        small[10, :thin],
        small[11, :thin],
        small[12, :thin],
        s_mixed[:, : 3 * width],
        s_mixed[:, 3 * width :],
        small[13, :thin],
        small[14, :thin],
        s_up,
        s_down,
    )


def solution(mesh):
    fsdp, dp = mesh.shape["fsdp"], mesh.shape["dp"]
    quick = fsdp == 8 and dp == 4
    images, wide, tall, vector = P(("dp", "fsdp"), None, None), P("fsdp", None), P(None, "fsdp"), P("fsdp")
    in_specs = (
        images, P(("dp", "fsdp"), None), wide, tall, wide, vector, vector, vector, vector,
        wide, wide, vector, vector, wide, wide, images,
    )
    out_specs = (
        images, images, wide, tall, wide, vector, vector, vector, vector,
        wide, wide, vector, vector, wide, wide,
    )
    return jax.shard_map(
        functools.partial(local, fsdp, quick), mesh=mesh, in_specs=in_specs, out_specs=out_specs, check_vma=False
    )
```

```python
import functools

import jax
import jax.numpy as jnp
from jax import lax
from jax.experimental import pallas as pl
from jax.experimental.pallas import tpu as pltpu
from jax.sharding import PartitionSpec as P

HDIM = 64
GRID = 16
ROWS = GRID * GRID
CHUNK = 256
EPSILON = 1e-05
VMEM_BYTES = 60 * 1024 * 1024
F32 = jnp.float32
BF16 = jnp.bfloat16


def dot_nn(left, right):
    return jnp.dot(left, right, preferred_element_type=F32)


def dot_nt(left, right):
    return lax.dot_general(left, right, (((1,), (1,)), ((), ())), preferred_element_type=F32)


def dot_tn(left, right):
    return lax.dot_general(left, right, (((0,), (0,)), ((), ())), preferred_element_type=F32)


def valid_cells(high, wide, shape):
    place = lax.broadcasted_iota(jnp.int32, shape, 0)
    return (place // GRID < high) & (place % GRID < wide)


def normalized(values):
    center = jnp.mean(values, axis=-1, keepdims=True)
    shifted = values - center
    spread = jnp.mean(shifted * shifted, axis=-1, keepdims=True)
    inverse = lax.rsqrt(spread + EPSILON)
    return shifted * inverse, inverse


def norm_pull(grad, gain, unit, inverse):
    scaled = grad * gain
    mean_plain = jnp.mean(scaled, axis=-1, keepdims=True)
    mean_unit = jnp.mean(scaled * unit, axis=-1, keepdims=True)
    return (scaled - mean_plain - unit * mean_unit) * inverse


def fold_rows(values):
    rows, width = values.shape
    return jnp.sum(values.reshape(rows // 8, 8, width), axis=0)


def move_cells(values, step):
    rows, width = values.shape
    parts = values.reshape(rows // GRID, 2, 8, width)
    turned = pltpu.roll(parts, step % 8, axis=2)
    first, last = turned[:, 0:1], turned[:, 1:2]
    line = lax.broadcasted_iota(jnp.int32, first.shape, 2)
    if step == 1:
        edge = line == 0
        moved = jnp.concatenate((jnp.where(edge, 0.0, first), jnp.where(edge, first, last)), axis=1)
    else:
        edge = line == 7
        moved = jnp.concatenate((jnp.where(edge, last, first), jnp.where(edge, 0.0, last)), axis=1)
    return moved.reshape(rows, width)


MESH = pl.DeviceIdType.MESH


def places(sides):
    dp, fsdp = lax.axis_index("dp"), lax.axis_index("fsdp")
    return dp // 2, dp % 2, fsdp // sides, fsdp % sides


def half_of(ref, lead, part):
    rows, columns = ref.shape[-2:]
    if columns > rows * 4:
        size = columns // 2
        return ref.at[lead + (slice(None), pl.ds(pl.multiple_of(part * size, 128), size))]
    size = rows // 2
    return ref.at[lead + (pl.ds(pl.multiple_of(part * size, 8), size), slice(None))]


def half_shape(shape):
    rows, columns = shape
    return (rows, columns // 2) if columns > rows * 4 else (rows // 2, columns)


def remote(source, target, sends, receives, index, device):
    return pltpu.make_async_remote_copy(
        src_ref=source,
        dst_ref=target,
        send_sem=sends.at[index],
        recv_sem=receives.at[index],
        device_id=device,
        device_id_type=MESH,
    )


def greet(devices):
    barrier = pltpu.get_barrier_semaphore()
    for device in devices:
        pl.semaphore_signal(barrier, inc=1, device_id=device, device_id_type=MESH)
    pl.semaphore_wait(barrier, len(devices))


def peers_of(layers):
    x, core, z, y = places(2)
    dp, fsdp = x * 2 + core, z * 2 + y
    along = [(dp, (z ^ step) * 2 + y) for step in range(1, layers)]
    return along, (dp, z * 2 + 1 - y), (x * 2 + 1 - core, fsdp), ((1 - x) * 2 + core, fsdp)


class Gather:
    def __init__(self, shard, full, sems, number):
        self.shard, self.full = shard, full
        self.layers = full.shape[0]
        base = number * (2 * self.layers + 2)
        sends, receives, local = sems
        self.x, self.core, self.z, self.y = places(2)
        along, self.across, self.sibling, _ = peers_of(self.layers)
        own = half_of(shard, (), self.core)
        self.local = pltpu.make_async_copy(own, self.part(self.z, self.y), local.at[number])
        self.along = [
            remote(own, self.part(self.z, self.y), sends, receives, base + step, along[step])
            for step in range(self.layers - 1)
        ]
        base += self.layers - 1
        self.over = []
        for step in range(self.layers):
            target = self.part(self.z ^ step, self.y)
            self.over.append(remote(own if step == 0 else target, target, sends, receives, base + step, self.across))
        base += self.layers
        self.inside = []
        for step, side in enumerate((self.y, 1 - self.y)):
            target = half_of(full, (slice(None), side), self.core)
            self.inside.append(remote(target, target, sends, receives, base + step, self.sibling))

    def part(self, z, y):
        return half_of(self.full, (z, y), self.core)

    def start(self):
        for copy in self.along:
            copy.start()
        self.over[0].start()
        self.local.start()

    def forward(self):
        for step, copy in enumerate(self.along):
            copy.wait_recv()
            self.over[step + 1].start()
        self.local.wait()
        self.inside[0].start()

    def share(self):
        for copy in self.over:
            copy.wait_recv()
        self.inside[1].start()

    def finish(self):
        for copy in self.inside:
            copy.wait_recv()

    def drain(self):
        for copy in self.along + self.over + self.inside:
            copy.wait_send()


def conv_forward_body(
    image, grid_ref, tokens_ref, expand_ref, taps_ref, project_ref, norms_ref,
    field_ref, act_ref, pull_ref, projected_ref, first_ref, frame, ready,
):
    width = tokens_ref.shape[1]
    hidden = taps_ref.shape[1]
    valid = valid_cells(grid_ref[image, 0], grid_ref[image, 1], (ROWS, width))
    tokens = tokens_ref[...]
    kept = jnp.where(valid, tokens, jnp.zeros_like(tokens))
    edge = jnp.zeros((GRID, CHUNK), F32)
    for chunk in range(hidden // CHUNK):
        slot = chunk % 2
        columns = slice(chunk * CHUNK, (chunk + 1) * CHUNK)
        expanded = dot_nn(kept, expand_ref[..., columns].reshape(width, CHUNK))
        field_ref[chunk] = expanded.astype(BF16)
        frame[slot, 0:GRID] = edge
        frame[slot, GRID : GRID + ROWS] = expanded
        frame[slot, GRID + ROWS :] = edge
        for half in range(CHUNK // 128):
            lanes = slice(half * 128, (half + 1) * 128)
            whole = slice(chunk * CHUNK + half * 128, chunk * CHUNK + (half + 1) * 128)
            taps = [taps_ref[k : k + 1, whole] for k in range(9)]
            block = 64
            for start in range(0, ROWS, block):
                near = [frame[slot, start + GRID * a : start + GRID * a + block, lanes] for a in range(3)]
                sums = [sum(taps[3 * a + b] * near[a] for a in range(3)) for b in range(3)]
                conv = sums[1] + move_cells(sums[0], 1) + move_cells(sums[2], -1)
                gate = 0.5 * jnp.tanh(0.5 * conv) + 0.5
                act = conv * gate
                act_ref[chunk, start : start + block, lanes] = act.astype(BF16)
                pull_ref[chunk, start : start + block, lanes] = (gate + act * (1.0 - gate)).astype(BF16)
    ready()
    weights = project_ref[...].reshape(hidden, width)
    projected = jnp.zeros((ROWS, width), F32)
    for chunk in range(hidden // CHUNK):
        projected = projected + dot_nn(act_ref[chunk], weights[chunk * CHUNK : (chunk + 1) * CHUNK, :])
    projected_ref[...] = projected
    unit, _ = normalized(projected)
    shift = unit * norms_ref[1:2, :] + norms_ref[2:3, :]
    first_ref[...] = tokens.astype(F32) + jnp.where(valid, shift, 0.0)


def conv_forward_kernel(
    grid_ref, tokens_ref, expand_ref, taps_ref, project_ref, norms_ref,
    field_ref, act_ref, pull_ref, projected_ref, first_ref, frame,
):
    conv_forward_body(
        pl.program_id(0), grid_ref, tokens_ref, expand_ref, taps_ref, project_ref, norms_ref,
        field_ref, act_ref, pull_ref, projected_ref, first_ref, frame, lambda: None,
    )


def gather_forward_kernel(
    grid_ref, tokens_ref, depth_ref, gain1_ref, bias1_ref, gain2_ref, bias2_ref, gain3_ref, bias3_ref,
    s_expand, s_project, s_qkv, s_out, s_up, s_down,
    field_ref, act_ref, pull_ref, projected_ref, first_ref,
    taps_ref, norms_ref, f_expand, f_project, f_mixed, f_up, f_down,
    frame, v_expand, v_project, v_small, own_small, own_mixed, sends, receives, locals_,
):
    image = pl.program_id(0)
    sems = (sends, receives, locals_)
    small = Gather(own_small, v_small, sems, 0)
    expand = Gather(s_expand, v_expand, sems, 1)
    project = Gather(s_project, v_project, sems, 2)
    mixed = Gather(own_mixed, f_mixed, sems, 3)
    up = Gather(s_up, f_up, sems, 4)
    down = Gather(s_down, f_down, sems, 5)
    early, late = (small, expand, project), (mixed, up, down)
    share, thin = depth_ref.shape[1], gain1_ref.shape[0]
    cut = s_qkv.shape[1]
    pieces = [
        pltpu.make_async_copy(s_qkv, own_mixed.at[:, :cut], locals_.at[6]),
        pltpu.make_async_copy(s_out, own_mixed.at[:, cut:], locals_.at[7]),
    ]
    saves = [
        pltpu.make_async_copy(v_expand, f_expand, locals_.at[8]),
        pltpu.make_async_copy(v_project, f_project, locals_.at[9]),
    ]

    @pl.when(image == 0)
    def _():
        for piece in pieces:
            piece.start()
        own_small[...] = jnp.zeros_like(own_small)
        own_small[0:9, 0:share] = depth_ref[...].astype(F32)
        for line, ref in enumerate((gain1_ref, bias1_ref, gain2_ref, bias2_ref, gain3_ref, bias3_ref)):
            own_small[9 + line : 10 + line, 0:thin] = ref[...].astype(F32).reshape(1, thin)
        along, across, sibling, _ = peers_of(v_small.shape[0])
        greet(along + [across, sibling])
        for part in early:
            part.start()
        for part in early:
            part.forward()
        for part in early:
            part.share()
        for piece in pieces:
            piece.wait()
        for part in late:
            part.start()
        small.finish()
        expand.finish()
        layers = v_small.shape[0]
        blocks = [v_small[z, y] for z in range(layers) for y in range(2)]
        taps_ref[...] = jnp.concatenate([block[:, :share] for block in blocks], axis=1)
        norms_ref[...] = jnp.concatenate([block[8:, :thin] for block in blocks], axis=1)

    def ready():
        @pl.when(image == 0)
        def _():
            project.finish()
            for save in saves:
                save.start()

    conv_forward_body(
        image, grid_ref, tokens_ref, v_expand, taps_ref, v_project, norms_ref,
        field_ref, act_ref, pull_ref, projected_ref, first_ref, frame, ready,
    )

    for step, part in zip((2, 3, 4), late):
        pl.when(image == step)(part.forward)
    for step, part in zip((4, 5, 6), late):
        pl.when(image == step)(part.share)

    @pl.when(image == pl.num_programs(0) - 1)
    def _():
        for part in late:
            part.finish()
        for part in early + late:
            part.drain()
        for save in saves:
            save.wait()


def whole(shape):
    return pl.BlockSpec(shape, lambda *_: (0,) * len(shape), pipeline_mode=pl.Buffered(1))


def conv_forward(grid, tokens, w_expand, taps, w_project, norms):
    rows, width = tokens.shape
    hidden = w_expand.shape[1]
    chunks = hidden // CHUNK
    per_image = pl.BlockSpec((ROWS, width), lambda i: (i, 0))
    per_chunk = pl.BlockSpec((chunks, ROWS, CHUNK), lambda i: (0, i, 0))
    wide = jax.ShapeDtypeStruct((chunks, rows, CHUNK), BF16)
    return pl.pallas_call(
        conv_forward_kernel,
        grid=(rows // ROWS,),
        in_specs=[
            pl.BlockSpec(memory_space=pltpu.SMEM),
            per_image,
            whole(w_expand.shape),
            whole(taps.shape),
            whole(w_project.shape),
            whole(norms.shape),
        ],
        out_specs=[per_chunk, per_chunk, per_chunk, per_image, per_image],
        out_shape=[
            wide,
            wide,
            wide,
            jax.ShapeDtypeStruct((rows, width), F32),
            jax.ShapeDtypeStruct((rows, width), F32),
        ],
        scratch_shapes=[pltpu.VMEM((2, ROWS + 2 * GRID, CHUNK), F32)],
        compiler_params=pltpu.CompilerParams(vmem_limit_bytes=VMEM_BYTES),
        name="conv_forward",
    )(grid, tokens, w_expand, taps, w_project, norms)


def gather_forward(grid, tokens, w_depth, vectors, w_expand, w_project, w_qkv, w_out, w_up, w_down, layers):
    rows, width = tokens.shape
    hidden = w_expand.shape[1]
    chunks = hidden // CHUNK
    per_image = pl.BlockSpec((ROWS, width), lambda i: (i, 0))
    per_chunk = pl.BlockSpec((chunks, ROWS, CHUNK), lambda i: (0, i, 0))
    wide = jax.ShapeDtypeStruct((chunks, rows, CHUNK), BF16)
    tall = jax.ShapeDtypeStruct((rows, width), F32)
    anywhere = pl.BlockSpec(memory_space=pl.ANY)
    here = pl.BlockSpec(memory_space=pltpu.VMEM)
    span = -(-w_depth.shape[1] // 128) * 128
    mixed = (w_qkv.shape[0], w_qkv.shape[1] + w_out.shape[1])
    fulls = [(layers, 2) + shape for shape in (w_expand.shape, w_project.shape, mixed, w_up.shape, w_down.shape)]
    copies = 6 * (2 * layers + 2)
    return pl.pallas_call(
        gather_forward_kernel,
        grid=(rows // ROWS,),
        in_specs=[pl.BlockSpec(memory_space=pltpu.SMEM), per_image] + [here] * 7 + [anywhere] * 6,
        out_specs=[per_chunk, per_chunk, per_chunk, per_image, per_image, whole((16, hidden)), whole((8, width))]
        + [anywhere] * 5,
        out_shape=[wide, wide, wide, tall, tall, jax.ShapeDtypeStruct((16, hidden), F32), jax.ShapeDtypeStruct((8, width), F32)]
        + [jax.ShapeDtypeStruct(full, BF16) for full in fulls],
        scratch_shapes=[
            pltpu.VMEM((2, ROWS + 2 * GRID, CHUNK), F32),
            pltpu.VMEM(fulls[0], BF16),
            pltpu.VMEM(fulls[1], BF16),
            pltpu.VMEM((layers, 2, 16, span), F32),
            pltpu.VMEM((16, span), F32),
            pltpu.VMEM(mixed, BF16),
            pltpu.SemaphoreType.DMA((copies,)),
            pltpu.SemaphoreType.DMA((copies,)),
            pltpu.SemaphoreType.DMA((10,)),
        ],
        compiler_params=pltpu.CompilerParams(
            vmem_limit_bytes=VMEM_BYTES, collective_id=0, has_side_effects=True
        ),
        name="gather_forward",
    )(grid, tokens, w_depth, *vectors, w_expand, w_project, w_qkv, w_out, w_up, w_down)


def middle_kernel(
    grid_ref, first_ref, cotan_ref, mixed_ref, up_ref, down_ref, norms_ref,
    layer_ref, d_first_ref, g_mixed_ref, g_up_ref, g_down_ref, g_norm_ref,
    a_mixed, a_up, a_down, expo, keys, values, queries, attended_t, d_qkv,
):
    image = pl.program_id(0)
    width = first_ref.shape[1]
    hidden = up_ref.shape[1]
    pairs = width // 128

    @pl.when(image == 0)
    def _():
        for ref in (a_mixed, a_up, a_down, g_norm_ref):
            ref[...] = jnp.zeros_like(ref)

    high, wide = grid_ref[image, 0], grid_ref[image, 1]
    valid = valid_cells(high, wide, (ROWS, width))
    first = first_ref[...]
    unit1, inverse1 = normalized(first)
    normed = (unit1 * norms_ref[3:4, :] + norms_ref[4:5, :]).astype(BF16)
    packed = dot_nn(normed, mixed_ref[:, : 3 * width]).astype(BF16)
    lane = lax.broadcasted_iota(jnp.int32, (ROWS, 128), 1) // HDIM
    line = lax.broadcasted_iota(jnp.int32, (128, ROWS), 0) // HDIM
    zero = jnp.zeros((ROWS, 128), BF16)
    key_bias = jnp.where(valid_cells(high, wide, (ROWS, ROWS)), 0.0, -1e9)
    key_bias = jnp.concatenate((key_bias, key_bias), axis=0)
    inverses = []
    for pair in range(pairs):
        at = pair * 128
        query = packed[:, at : at + 128] * jnp.asarray(HDIM**-0.5, BF16)
        key = packed[:, width + at : width + at + 128]
        value = packed[:, 2 * width + at : 2 * width + at + 128]
        for head in range(2):
            keys[pair, head * ROWS : (head + 1) * ROWS] = jnp.where(lane == head, key, zero)
            values[pair, head * ROWS : (head + 1) * ROWS] = jnp.where(lane == head, value, zero)
            queries[pair, head * ROWS : (head + 1) * ROWS] = jnp.where(lane == head, query, zero)
        scores = dot_nt(keys[pair], query) + key_bias
        totals = []
        for head in range(2):
            part = scores[head * ROWS : (head + 1) * ROWS]
            power = jnp.exp(part - jnp.max(part, axis=0, keepdims=True))
            totals.append(1.0 / jnp.sum(power, axis=0, keepdims=True))
            expo[pair, head * ROWS : (head + 1) * ROWS] = power.astype(BF16)
        inverse = jnp.where(line == 0, totals[0], totals[1])
        inverses.append(inverse)
        attended_t[at : at + 128] = (dot_tn(values[pair], expo[pair]) * inverse).astype(BF16)
    second = first + jnp.where(valid, dot_tn(attended_t[...], mixed_ref[:, 3 * width :]), 0.0)

    cotan = cotan_ref[...]
    unit2, inverse2 = normalized(second)
    normed3 = (unit2 * norms_ref[5:6, :] + norms_ref[6:7, :]).astype(BF16)
    d_down = jnp.where(valid, cotan, jnp.zeros_like(cotan))
    normed3_t = normed3.T
    d_down_t = d_down.T
    result = jnp.zeros((ROWS, width), F32)
    d_normed3 = jnp.zeros((ROWS, width), F32)
    for chunk in range(hidden // CHUNK):
        columns = slice(chunk * CHUNK, (chunk + 1) * CHUNK)
        upper = dot_nn(normed3, up_ref[:, columns])
        d_hidden = dot_nt(d_down, down_ref[columns, :])
        square = upper * upper
        bent = jnp.tanh(upper * (0.7978845608028654 + (0.7978845608028654 * 0.044715) * square))
        gate = 0.5 * bent + 0.5
        hid = (upper * gate).astype(BF16)
        slope = gate + upper * (gate - gate * gate) * (
            2 * 0.7978845608028654 + (6 * 0.7978845608028654 * 0.044715) * square
        )
        d_upper = (d_hidden * slope).astype(BF16)
        result = result + dot_nn(hid, down_ref[columns, :])
        a_down[:, columns] += dot_nn(d_down_t, hid)
        a_up[:, columns] += dot_nn(normed3_t, d_upper)
        d_normed3 = d_normed3 + dot_nt(d_upper, up_ref[:, columns])
    layer_ref[...] = (second + jnp.where(valid, result, 0.0)).astype(BF16)

    g_norm_ref[0:8] += fold_rows(d_normed3 * unit2)
    g_norm_ref[8:16] += fold_rows(d_normed3)
    d_second = cotan.astype(F32) + norm_pull(d_normed3, norms_ref[5:6, :], unit2, inverse2)

    d_out = jnp.where(valid, d_second, 0.0).astype(BF16)
    a_mixed[:, 3 * width :] += dot_nn(attended_t[...], d_out)
    for pair in range(pairs):
        at = pair * 128
        d_attended = dot_nt(mixed_ref[at : at + 128, 3 * width :], d_out)
        inverse = inverses[pair]
        d_low = d_attended.astype(BF16)
        inner = d_low.astype(F32) * attended_t[at : at + 128].astype(F32)
        d_scaled = d_low.astype(F32) * inverse
        d_scaled_low = d_scaled.astype(BF16)
        inner = inner * inverse
        deltas = [jnp.sum(inner[head * HDIM : (head + 1) * HDIM], axis=0, keepdims=True) for head in range(2)]
        d_probs = dot_nn(values[pair], d_scaled_low)
        d_value = jnp.zeros((ROWS, 128), F32)
        d_key = jnp.zeros((ROWS, 128), F32)
        steps = []
        for head in range(2):
            rows = slice(head * ROWS, (head + 1) * ROWS)
            power = expo[pair, rows]
            d_score = (power.astype(F32) * (d_probs[rows] - deltas[head])).astype(BF16)
            steps.append(d_score)
            own = jnp.where(line == head, d_scaled_low, jnp.zeros_like(d_scaled_low))
            d_value = d_value + dot_nt(power, own)
            d_key = d_key + dot_nn(d_score, queries[pair, rows])
        d_query_t = dot_tn(keys[pair], jnp.concatenate(steps, axis=0)) * (HDIM**-0.5)
        d_qkv[:, at : at + 128] = d_query_t.astype(BF16).T
        d_qkv[:, width + at : width + at + 128] = d_key.astype(BF16)
        d_qkv[:, 2 * width + at : 2 * width + at + 128] = d_value.astype(BF16)
    a_mixed[:, : 3 * width] += dot_nn(normed.T, d_qkv[...])
    d_normed = dot_nt(d_qkv[...], mixed_ref[:, : 3 * width])
    g_norm_ref[16:24] += fold_rows(d_normed * unit1)
    g_norm_ref[24:32] += fold_rows(d_normed)
    d_first_ref[...] = d_second + norm_pull(d_normed, norms_ref[3:4, :], unit1, inverse1)

    @pl.when(image == pl.num_programs(0) - 1)
    def _():
        g_mixed_ref[...] = a_mixed[...].astype(BF16)
        g_up_ref[...] = a_up[...].astype(BF16)
        g_down_ref[...] = a_down[...].astype(BF16).T


def middle(grid, first, cotangent, w_mixed, w_up, w_down, norms):
    rows, width = first.shape
    hidden = w_up.shape[1]
    pairs = width // 128
    per_image = pl.BlockSpec((ROWS, width), lambda i: (i, 0))
    weights = (w_mixed, w_up, w_down)
    return pl.pallas_call(
        middle_kernel,
        grid=(rows // ROWS,),
        in_specs=[pl.BlockSpec(memory_space=pltpu.SMEM), per_image, per_image]
        + [whole(weight.shape) for weight in weights]
        + [whole(norms.shape)],
        out_specs=[per_image, per_image] + [whole(weight.shape) for weight in weights] + [whole((32, width))],
        out_shape=[jax.ShapeDtypeStruct((rows, width), BF16), jax.ShapeDtypeStruct((rows, width), F32)]
        + [jax.ShapeDtypeStruct(weight.shape, BF16) for weight in weights]
        + [jax.ShapeDtypeStruct((32, width), F32)],
        scratch_shapes=[
            pltpu.VMEM(w_mixed.shape, F32),
            pltpu.VMEM(w_up.shape, F32),
            pltpu.VMEM((width, hidden), F32),
            pltpu.VMEM((pairs, 2 * ROWS, ROWS), BF16),
            pltpu.VMEM((pairs, 2 * ROWS, 128), BF16),
            pltpu.VMEM((pairs, 2 * ROWS, 128), BF16),
            pltpu.VMEM((pairs, 2 * ROWS, 128), BF16),
            pltpu.VMEM((width, ROWS), BF16),
            pltpu.VMEM((ROWS, 3 * width), BF16),
        ],
        compiler_params=pltpu.CompilerParams(vmem_limit_bytes=VMEM_BYTES),
        name="middle",
    )(grid, first, cotangent, *weights, norms)


def conv_backward_kernel(
    grid_ref, tokens_ref, d_first_ref, projected_ref, field_ref, act_ref, pull_ref,
    expand_ref, taps_ref, project_ref, norms_ref,
    d_tokens_ref, g_expand_ref, g_project_ref, g_taps_ref, g_norm_ref,
    d_proj, d_proj_t, tokens_t, d_image, frames, a_expand, a_project,
):
    chunk = pl.program_id(0)
    last = pl.num_programs(0) - 1
    rows, width = tokens_ref.shape
    images = rows // ROWS

    @pl.when(chunk == 0)
    def _():
        g_norm_ref[...] = jnp.zeros_like(g_norm_ref)
        frames[...] = jnp.zeros_like(frames)

        @pl.loop(0, images)
        def _(image):
            here = pl.ds(pl.multiple_of(image * ROWS, ROWS), ROWS)
            valid = valid_cells(grid_ref[image, 0], grid_ref[image, 1], (ROWS, width))
            unit, inverse = normalized(projected_ref[here, :])
            grad = jnp.where(valid, d_first_ref[here, :], 0.0)
            g_norm_ref[0:8] += fold_rows(grad * unit)
            g_norm_ref[8:16] += fold_rows(grad)
            low = norm_pull(grad, norms_ref[1:2, :], unit, inverse).astype(BF16)
            d_proj[image] = low
            d_proj_t[image] = low.T
            tokens_t[image] = tokens_ref[here, :].T

    a_expand[...] = jnp.zeros_like(a_expand)
    a_project[...] = jnp.zeros_like(a_project)
    g_taps_ref[...] = jnp.zeros_like(g_taps_ref)

    @pl.loop(0, images)
    def _(image):
        here = pl.ds(pl.multiple_of(image * ROWS, ROWS), ROWS)
        d_act = dot_nt(d_proj[image], project_ref[...])
        d_conv = d_act * pull_ref[0, here, :].astype(F32)
        frames[1, GRID : GRID + ROWS] = d_conv
        frames[0, GRID : GRID + ROWS] = move_cells(d_conv, -1)
        frames[2, GRID : GRID + ROWS] = move_cells(d_conv, 1)
        field = field_ref[0, here, :].astype(F32)
        valid = valid_cells(grid_ref[image, 0], grid_ref[image, 1], (ROWS, 128))
        parts = []
        for half in range(CHUNK // 128):
            lanes = slice(half * 128, (half + 1) * 128)
            taps = [taps_ref[k : k + 1, lanes] for k in range(9)]
            totals = [jnp.zeros((8, 128), F32) for _ in range(9)]
            block = 64
            stack = []
            for start in range(0, ROWS, block):
                own = field[start : start + block, lanes]
                grad = jnp.zeros((block, 128), F32)
                for a in range(3):
                    for b in range(3):
                        at = start + GRID * (2 - a)
                        near = frames[b, at : at + block, lanes]
                        grad = grad + taps[3 * a + b] * near
                        totals[3 * a + b] = totals[3 * a + b] + fold_rows(near * own)
                stack.append(jnp.where(valid[start : start + block], grad, 0.0).astype(BF16))
            parts.append(jnp.concatenate(stack, axis=0))
            for k in range(9):
                g_taps_ref[8 * k : 8 * k + 8, lanes] += totals[k]
        d_field = jnp.concatenate(parts, axis=1)
        a_project[...] += dot_nn(d_proj_t[image], act_ref[0, here, :])
        a_expand[...] += dot_nn(tokens_t[image], d_field)
        more = dot_nt(d_field, expand_ref[...])

        @pl.when(chunk == 0)
        def _():
            d_image[image] = d_first_ref[here, :] + more

        @pl.when((chunk > 0) & (chunk < last))
        def _():
            d_image[image] += more

        @pl.when(chunk == last)
        def _():
            d_tokens_ref[here, :] = (d_image[image] + more).astype(BF16)

    g_expand_ref[...] = a_expand[...].astype(BF16)
    g_project_ref[...] = a_project[...].astype(BF16).T


def conv_backward(grid, tokens, d_first, projected, field, act, pull, w_expand, taps, w_project, norms):
    rows, width = tokens.shape
    hidden = w_expand.shape[1]
    images = rows // ROWS
    per_chunk = pl.BlockSpec((1, rows, CHUNK), lambda c: (c, 0, 0))
    columns = pl.BlockSpec((width, CHUNK), lambda c: (0, c))
    lines = pl.BlockSpec((CHUNK, width), lambda c: (c, 0))
    full = whole((rows, width))
    return pl.pallas_call(
        conv_backward_kernel,
        grid=(hidden // CHUNK,),
        in_specs=[
            pl.BlockSpec(memory_space=pltpu.SMEM),
            full,
            full,
            full,
            per_chunk,
            per_chunk,
            per_chunk,
            columns,
            pl.BlockSpec((taps.shape[0], CHUNK), lambda c: (0, c)),
            lines,
            whole(norms.shape),
        ],
        out_specs=[full, columns, lines, pl.BlockSpec((72, CHUNK), lambda c: (0, c)), whole((16, width))],
        out_shape=[
            jax.ShapeDtypeStruct((rows, width), BF16),
            jax.ShapeDtypeStruct(w_expand.shape, BF16),
            jax.ShapeDtypeStruct(w_project.shape, BF16),
            jax.ShapeDtypeStruct((72, hidden), F32),
            jax.ShapeDtypeStruct((16, width), F32),
        ],
        scratch_shapes=[
            pltpu.VMEM((images, ROWS, width), BF16),
            pltpu.VMEM((images, width, ROWS), BF16),
            pltpu.VMEM((images, width, ROWS), BF16),
            pltpu.VMEM((images, ROWS, width), F32),
            pltpu.VMEM((3, ROWS + 2 * GRID, CHUNK), F32),
            pltpu.VMEM((width, CHUNK), F32),
            pltpu.VMEM((width, CHUNK), F32),
        ],
        compiler_params=pltpu.CompilerParams(vmem_limit_bytes=VMEM_BYTES),
        name="conv_backward",
    )(grid, tokens, d_first, projected, field, act, pull, w_expand, taps, w_project, norms)


class Reduce:
    def __init__(self, terms, result, buffers, sems, number):
        self.terms, self.result = terms, result
        self.from_core, self.chip, self.from_side, self.line, self.from_along, self.own, self.from_x, self.total = buffers
        self.layers = terms.shape[0]
        base = number * (self.layers + 3)
        sends, receives = sems
        self.x, self.core, self.z, self.y = places(2)
        along, across, sibling, beyond = peers_of(self.layers)
        other = half_of(terms, (slice(None), slice(None)), 1 - self.core)
        self.inside = remote(other, self.from_core, sends, receives, base, sibling)
        self.over = remote(self.chip.at[:, 1 - self.y], self.from_side, sends, receives, base + 1, across)
        self.along = [
            remote(self.line.at[self.z ^ (step + 1)], self.from_along.at[step], sends, receives, base + 2 + step, along[step])
            for step in range(self.layers - 1)
        ]
        base += self.layers + 1
        self.beyond = remote(self.own, self.from_x, sends, receives, base, beyond)
        self.back = remote(self.total, half_of(result, (), self.core), sends, receives, base + 1, sibling)

    def start(self):
        self.inside.start()

    def add_chip(self):
        self.inside.wait_recv()
        for z in range(self.layers):
            for y in range(2):
                mine = half_of(self.terms, (z, y), self.core)[...].astype(F32)
                self.chip[z, y] = (mine + self.from_core[z, y].astype(F32)).astype(self.chip.dtype)
        self.over.start()

    def add_side(self):
        self.over.wait_recv()
        for z in range(self.layers):
            mine = self.chip[z, self.y].astype(F32)
            self.line[z] = (mine + self.from_side[z].astype(F32)).astype(self.line.dtype)
        for copy in self.along:
            copy.start()

    def add_line(self):
        mine = self.line[self.z].astype(F32)
        for step, copy in enumerate(self.along):
            copy.wait_recv()
            mine = mine + self.from_along[step].astype(F32)
        self.own[...] = mine.astype(self.own.dtype)
        self.beyond.start()

    def add_x(self):
        self.beyond.wait_recv()
        self.total[...] = self.own[...].astype(F32) + self.from_x[...].astype(F32)
        self.back.start()
        half_of(self.result, (), self.core)[...] = self.total[...]

    def finish(self):
        self.back.wait_recv()
        for copy in [self.inside, self.over, self.beyond, self.back] + self.along:
            copy.wait_send()


def reduce_kernel(count, *refs):
    terms, results, rest = refs[:count], refs[count : 2 * count], refs[2 * count :]
    sems = rest[8 * count :]
    along, across, sibling, beyond = peers_of(terms[0].shape[0])
    greet(along + [across, sibling, beyond])
    parts = [Reduce(terms[i], results[i], rest[8 * i : 8 * i + 8], sems, i) for i in range(count)]
    for stage in ("start", "add_chip", "add_side", "add_line", "add_x", "finish"):
        for part in parts:
            getattr(part, stage)()


def reduce_buffers(shape, dtype):
    layers, sides = shape[:2]
    half = half_shape(shape[2:])
    return [
        pltpu.VMEM((layers, sides) + half, dtype),
        pltpu.VMEM((layers, sides) + half, dtype),
        pltpu.VMEM((layers,) + half, dtype),
        pltpu.VMEM((layers,) + half, dtype),
        pltpu.VMEM((layers - 1,) + half, dtype),
        pltpu.VMEM(half, dtype),
        pltpu.VMEM(half, dtype),
        pltpu.VMEM(half, F32),
    ]


def reduce(terms):
    count = len(terms)
    layers = terms[0].shape[0]
    copies = count * (layers + 3)
    here = pl.BlockSpec(memory_space=pltpu.VMEM)
    scratch = []
    for term in terms:
        scratch += reduce_buffers(term.shape, term.dtype)
    return pl.pallas_call(
        functools.partial(reduce_kernel, count),
        in_specs=[here] * count,
        out_specs=[here] * count,
        out_shape=[jax.ShapeDtypeStruct(term.shape[2:], F32) for term in terms],
        scratch_shapes=scratch + [pltpu.SemaphoreType.DMA((copies,)), pltpu.SemaphoreType.DMA((copies,))],
        compiler_params=pltpu.CompilerParams(collective_id=1, has_side_effects=True, vmem_limit_bytes=VMEM_BYTES),
        name="reduce_gradients",
    )(*terms)


def reduce_plain(terms):
    results = []
    for term in terms:
        flat = term.reshape((-1,) + term.shape[2:])
        share = lax.psum_scatter(flat, "fsdp", scatter_dimension=0, tiled=False)
        results.append(lax.psum(share, "dp").astype(F32))
    return results


def local(
    fsdp, quick,
    tokens, grid, w_expand, w_depth, w_project, gain_conv, bias_conv, gain_attend, bias_attend,
    w_qkv, w_out, gain_mlp, bias_mlp, w_up, w_down, cotangent,
):
    slots, rows, width = tokens.shape
    hidden = w_expand.shape[1]
    share, thin = w_depth.shape[1], gain_conv.shape[0]
    span = -(-share // 128) * 128
    vectors = (gain_conv, bias_conv, gain_attend, bias_attend, gain_mlp, bias_mlp)
    flat, cotan = tokens.reshape(slots * rows, width), cotangent.reshape(slots * rows, width)
    if quick:
        field, act, pull, projected, first, taps, norms, *fulls = gather_forward(
            grid, flat, w_depth, vectors, w_expand, w_project, w_qkv, w_out, w_up, w_down, fsdp // 2
        )
        f_expand, f_project, f_mixed, f_up, f_down = [full.reshape(-1, full.shape[3]) for full in fulls]
    else:
        mixed = jnp.concatenate((w_qkv, w_out), axis=1)
        f_expand, f_project, f_mixed, f_up, f_down = [
            lax.all_gather(shard, "fsdp", axis=0, tiled=True) for shard in (w_expand, w_project, mixed, w_up, w_down)
        ]
        taps = jnp.pad(lax.all_gather(w_depth, "fsdp", axis=1, tiled=True).astype(F32), ((0, 7), (0, 0)))
        lines = lax.all_gather(jnp.stack(vectors), "fsdp", axis=1, tiled=True).astype(F32)
        norms = jnp.pad(lines, ((1, 1), (0, 0)))
        field, act, pull, projected, first = conv_forward(grid, flat, f_expand, taps, f_project, norms)
    layers, sides = (fsdp // 2, 2) if quick else (1, fsdp)
    shapes = [(layers, sides, 16, span)] + [
        (layers, sides, full.shape[0] // fsdp, full.shape[1]) for full in (f_expand, f_project, f_mixed, f_up, f_down)
    ]
    layer_out, d_first, g_mixed, g_up, g_down, g_norm = middle(grid, first, cotan, f_mixed, f_up, f_down, norms)
    d_tokens, g_expand, g_project, g_taps, g_norm_conv = conv_backward(
        grid, flat, d_first, projected, field, act, pull, f_expand, taps, f_project, norms
    )
    g_taps = jnp.sum(g_taps.reshape(9, 8, fsdp, share), axis=1)
    g_norm = jnp.concatenate((g_norm_conv, g_norm[16:], g_norm[:16]), axis=0)
    g_norm = jnp.sum(g_norm.reshape(6, 8, fsdp, thin), axis=1)
    g_small = jnp.concatenate(
        (
            jnp.pad(g_taps, ((0, 0), (0, 0), (0, span - share))),
            jnp.pad(g_norm, ((0, 1), (0, 0), (0, span - thin))),
        ),
        axis=0,
    ).transpose(1, 0, 2)
    terms = [
        term.reshape(shape) for term, shape in zip((g_small, g_expand, g_project, g_mixed, g_up, g_down), shapes)
    ]
    small, s_expand, s_project, s_mixed, s_up, s_down = (reduce if quick else reduce_plain)(terms)
    return (
        layer_out.reshape(tokens.shape),
        d_tokens.reshape(tokens.shape),
        s_expand,
        small[:9, :share],
        s_project,
        small[9, :thin],
        small[10, :thin],
        small[11, :thin],
        small[12, :thin],
        s_mixed[:, : 3 * width],
        s_mixed[:, 3 * width :],
        small[13, :thin],
        small[14, :thin],
        s_up,
        s_down,
    )


def solution(mesh):
    fsdp, dp = mesh.shape["fsdp"], mesh.shape["dp"]
    quick = fsdp == 8 and dp == 4
    images, wide, tall, vector = P(("dp", "fsdp"), None, None), P("fsdp", None), P(None, "fsdp"), P("fsdp")
    in_specs = (
        images, P(("dp", "fsdp"), None), wide, tall, wide, vector, vector, vector, vector,
        wide, wide, vector, vector, wide, wide, images,
    )
    out_specs = (
        images, images, wide, tall, wide, vector, vector, vector, vector,
        wide, wide, vector, vector, wide, wide,
    )
    return jax.shard_map(
        functools.partial(local, fsdp, quick), mesh=mesh, in_specs=in_specs, out_specs=out_specs, check_vma=False
    )
```

```python
import functools

import jax
import jax.numpy as jnp
from jax import lax
from jax.experimental import pallas as pl
from jax.experimental.pallas import tpu as pltpu
from jax.sharding import PartitionSpec as P

HDIM = 64
GRID = 16
ROWS = GRID * GRID
CHUNK = 256
EPSILON = 1e-05
VMEM_BYTES = 62 * 1024 * 1024
F32 = jnp.float32
BF16 = jnp.bfloat16


def dot_nn(left, right):
    return jnp.dot(left, right, preferred_element_type=F32)


def dot_nt(left, right):
    return lax.dot_general(left, right, (((1,), (1,)), ((), ())), preferred_element_type=F32)


def dot_tn(left, right):
    return lax.dot_general(left, right, (((0,), (0,)), ((), ())), preferred_element_type=F32)


def valid_cells(high, wide, shape):
    place = lax.broadcasted_iota(jnp.int32, shape, 0)
    return (place // GRID < high) & (place % GRID < wide)


def normalized(values):
    center = jnp.mean(values, axis=-1, keepdims=True)
    shifted = values - center
    spread = jnp.mean(shifted * shifted, axis=-1, keepdims=True)
    inverse = lax.rsqrt(spread + EPSILON)
    return shifted * inverse, inverse


def norm_pull(grad, gain, unit, inverse):
    scaled = grad * gain
    mean_plain = jnp.mean(scaled, axis=-1, keepdims=True)
    mean_unit = jnp.mean(scaled * unit, axis=-1, keepdims=True)
    return (scaled - mean_plain - unit * mean_unit) * inverse


def fold_rows(values):
    rows, width = values.shape
    return jnp.sum(values.reshape(rows // 8, 8, width), axis=0)


def move_cells(values, step):
    rows, width = values.shape
    parts = values.reshape(rows // GRID, 2, 8, width)
    turned = pltpu.roll(parts, step % 8, axis=2)
    first, last = turned[:, 0:1], turned[:, 1:2]
    line = lax.broadcasted_iota(jnp.int32, first.shape, 2)
    if step == 1:
        edge = line == 0
        moved = jnp.concatenate((jnp.where(edge, 0.0, first), jnp.where(edge, first, last)), axis=1)
    else:
        edge = line == 7
        moved = jnp.concatenate((jnp.where(edge, last, first), jnp.where(edge, 0.0, last)), axis=1)
    return moved.reshape(rows, width)


MESH = pl.DeviceIdType.MESH


def places(sides):
    dp, fsdp = lax.axis_index("dp"), lax.axis_index("fsdp")
    return dp // 2, dp % 2, fsdp // sides, fsdp % sides


def half_of(ref, lead, part):
    rows, columns = ref.shape[-2:]
    if columns > rows * 4:
        size = columns // 2
        return ref.at[lead + (slice(None), pl.ds(pl.multiple_of(part * size, 128), size))]
    size = rows // 2
    return ref.at[lead + (pl.ds(pl.multiple_of(part * size, 8), size), slice(None))]


def half_shape(shape):
    rows, columns = shape
    return (rows, columns // 2) if columns > rows * 4 else (rows // 2, columns)


def remote(source, target, sends, receives, index, device):
    return pltpu.make_async_remote_copy(
        src_ref=source,
        dst_ref=target,
        send_sem=sends.at[index],
        recv_sem=receives.at[index],
        device_id=device,
        device_id_type=MESH,
    )


def greet(devices):
    barrier = pltpu.get_barrier_semaphore()
    for device in devices:
        pl.semaphore_signal(barrier, inc=1, device_id=device, device_id_type=MESH)
    pl.semaphore_wait(barrier, len(devices))


def peers_of(layers):
    x, core, z, y = places(2)
    dp, fsdp = x * 2 + core, z * 2 + y
    along = [(dp, (z ^ step) * 2 + y) for step in range(1, layers)]
    return along, (dp, z * 2 + 1 - y), (x * 2 + 1 - core, fsdp), ((1 - x) * 2 + core, fsdp)


class Gather:
    def __init__(self, shard, full, sems, number):
        self.shard, self.full = shard, full
        self.layers = full.shape[0]
        base = number * (2 * self.layers + 2)
        sends, receives, local = sems
        self.x, self.core, self.z, self.y = places(2)
        along, self.across, self.sibling, _ = peers_of(self.layers)
        own = half_of(shard, (), self.core)
        self.local = pltpu.make_async_copy(own, self.part(self.z, self.y), local.at[number])
        self.along = [
            remote(own, self.part(self.z, self.y), sends, receives, base + step, along[step])
            for step in range(self.layers - 1)
        ]
        base += self.layers - 1
        self.over = []
        for step in range(self.layers):
            target = self.part(self.z ^ step, self.y)
            self.over.append(remote(own if step == 0 else target, target, sends, receives, base + step, self.across))
        base += self.layers
        self.inside = []
        for step, side in enumerate((self.y, 1 - self.y)):
            target = half_of(full, (slice(None), side), self.core)
            self.inside.append(remote(target, target, sends, receives, base + step, self.sibling))

    def part(self, z, y):
        return half_of(self.full, (z, y), self.core)

    def start(self):
        for copy in self.along:
            copy.start()
        self.over[0].start()
        self.local.start()

    def forward(self):
        for step, copy in enumerate(self.along):
            copy.wait_recv()
            self.over[step + 1].start()
        self.local.wait()
        self.inside[0].start()

    def share(self):
        for copy in self.over:
            copy.wait_recv()
        self.inside[1].start()

    def finish(self):
        for copy in self.inside:
            copy.wait_recv()

    def drain(self):
        for copy in self.along + self.over + self.inside:
            copy.wait_send()


def conv_forward_body(
    image, grid_ref, tokens_ref, expand_ref, taps_ref, project_ref, norms_ref,
    field_ref, act_ref, pull_ref, projected_ref, first_ref, frame, ready,
):
    width = tokens_ref.shape[1]
    hidden = taps_ref.shape[1]
    valid = valid_cells(grid_ref[image, 0], grid_ref[image, 1], (ROWS, width))
    tokens = tokens_ref[...]
    kept = jnp.where(valid, tokens, jnp.zeros_like(tokens))
    edge = jnp.zeros((GRID, CHUNK), F32)
    for chunk in range(hidden // CHUNK):
        slot = chunk % 2
        columns = slice(chunk * CHUNK, (chunk + 1) * CHUNK)
        expanded = dot_nn(kept, expand_ref[..., columns].reshape(width, CHUNK))
        field_ref[chunk] = expanded.astype(BF16)
        frame[slot, 0:GRID] = edge
        frame[slot, GRID : GRID + ROWS] = expanded
        frame[slot, GRID + ROWS :] = edge
        for half in range(CHUNK // 128):
            lanes = slice(half * 128, (half + 1) * 128)
            whole = slice(chunk * CHUNK + half * 128, chunk * CHUNK + (half + 1) * 128)
            taps = [taps_ref[k : k + 1, whole] for k in range(9)]
            block = 64
            for start in range(0, ROWS, block):
                near = [frame[slot, start + GRID * a : start + GRID * a + block, lanes] for a in range(3)]
                sums = [sum(taps[3 * a + b] * near[a] for a in range(3)) for b in range(3)]
                conv = sums[1] + move_cells(sums[0], 1) + move_cells(sums[2], -1)
                gate = 0.5 * jnp.tanh(0.5 * conv) + 0.5
                act = conv * gate
                act_ref[chunk, start : start + block, lanes] = act.astype(BF16)
                pull_ref[chunk, start : start + block, lanes] = (gate + act * (1.0 - gate)).astype(BF16)
    ready()
    weights = project_ref[...].reshape(hidden, width)
    projected = jnp.zeros((ROWS, width), F32)
    for chunk in range(hidden // CHUNK):
        projected = projected + dot_nn(act_ref[chunk], weights[chunk * CHUNK : (chunk + 1) * CHUNK, :])
    projected_ref[...] = projected
    unit, _ = normalized(projected)
    shift = unit * norms_ref[1:2, :] + norms_ref[2:3, :]
    first_ref[...] = tokens.astype(F32) + jnp.where(valid, shift, 0.0)


def conv_forward_kernel(
    grid_ref, tokens_ref, expand_ref, taps_ref, project_ref, norms_ref,
    field_ref, act_ref, pull_ref, projected_ref, first_ref, frame,
):
    conv_forward_body(
        pl.program_id(0), grid_ref, tokens_ref, expand_ref, taps_ref, project_ref, norms_ref,
        field_ref, act_ref, pull_ref, projected_ref, first_ref, frame, lambda: None,
    )


def gather_forward_kernel(
    grid_ref, tokens_ref, depth_ref, gain1_ref, bias1_ref, gain2_ref, bias2_ref, gain3_ref, bias3_ref,
    s_expand, s_project, s_qkv, s_out, s_up, s_down,
    field_ref, act_ref, pull_ref, projected_ref, first_ref,
    taps_ref, norms_ref, f_expand, f_project, f_mixed, f_up, f_down,
    frame, v_expand, v_project, v_small, own_small, own_mixed, sends, receives, locals_,
):
    image = pl.program_id(0)
    sems = (sends, receives, locals_)
    small = Gather(own_small, v_small, sems, 0)
    expand = Gather(s_expand, v_expand, sems, 1)
    project = Gather(s_project, v_project, sems, 2)
    mixed = Gather(own_mixed, f_mixed, sems, 3)
    up = Gather(s_up, f_up, sems, 4)
    down = Gather(s_down, f_down, sems, 5)
    early, late = (small, expand, project), (mixed, up, down)
    share, thin = depth_ref.shape[1], gain1_ref.shape[0]
    cut = s_qkv.shape[1]
    pieces = [
        pltpu.make_async_copy(s_qkv, own_mixed.at[:, :cut], locals_.at[6]),
        pltpu.make_async_copy(s_out, own_mixed.at[:, cut:], locals_.at[7]),
    ]
    saves = [
        pltpu.make_async_copy(v_expand, f_expand, locals_.at[8]),
        pltpu.make_async_copy(v_project, f_project, locals_.at[9]),
    ]

    @pl.when(image == 0)
    def _():
        for piece in pieces:
            piece.start()
        own_small[...] = jnp.zeros_like(own_small)
        own_small[0:9, 0:share] = depth_ref[...].astype(F32)
        for line, ref in enumerate((gain1_ref, bias1_ref, gain2_ref, bias2_ref, gain3_ref, bias3_ref)):
            own_small[9 + line : 10 + line, 0:thin] = ref[...].astype(F32).reshape(1, thin)
        along, across, sibling, _ = peers_of(v_small.shape[0])
        greet(along + [across, sibling])
        for part in early:
            part.start()
        for part in early:
            part.forward()
        for part in early:
            part.share()
        for piece in pieces:
            piece.wait()
        for part in late:
            part.start()
        small.finish()
        expand.finish()
        layers = v_small.shape[0]
        blocks = [v_small[z, y] for z in range(layers) for y in range(2)]
        taps_ref[...] = jnp.concatenate([block[:, :share] for block in blocks], axis=1)
        norms_ref[...] = jnp.concatenate([block[8:, :thin] for block in blocks], axis=1)

    def ready():
        @pl.when(image == 0)
        def _():
            project.finish()
            for save in saves:
                save.start()

    conv_forward_body(
        image, grid_ref, tokens_ref, v_expand, taps_ref, v_project, norms_ref,
        field_ref, act_ref, pull_ref, projected_ref, first_ref, frame, ready,
    )

    for step, part in zip((2, 3, 4), late):
        pl.when(image == step)(part.forward)
    for step, part in zip((4, 5, 6), late):
        pl.when(image == step)(part.share)

    @pl.when(image == pl.num_programs(0) - 1)
    def _():
        for part in late:
            part.finish()
        for part in early + late:
            part.drain()
        for save in saves:
            save.wait()


def whole(shape):
    return pl.BlockSpec(shape, lambda *_: (0,) * len(shape), pipeline_mode=pl.Buffered(1))


def conv_forward(grid, tokens, w_expand, taps, w_project, norms):
    rows, width = tokens.shape
    hidden = w_expand.shape[1]
    chunks = hidden // CHUNK
    per_image = pl.BlockSpec((ROWS, width), lambda i: (i, 0))
    per_chunk = pl.BlockSpec((chunks, ROWS, CHUNK), lambda i: (0, i, 0))
    wide = jax.ShapeDtypeStruct((chunks, rows, CHUNK), BF16)
    return pl.pallas_call(
        conv_forward_kernel,
        grid=(rows // ROWS,),
        in_specs=[
            pl.BlockSpec(memory_space=pltpu.SMEM),
            per_image,
            whole(w_expand.shape),
            whole(taps.shape),
            whole(w_project.shape),
            whole(norms.shape),
        ],
        out_specs=[per_chunk, per_chunk, per_chunk, per_image, per_image],
        out_shape=[
            wide,
            wide,
            wide,
            jax.ShapeDtypeStruct((rows, width), F32),
            jax.ShapeDtypeStruct((rows, width), F32),
        ],
        scratch_shapes=[pltpu.VMEM((2, ROWS + 2 * GRID, CHUNK), F32)],
        compiler_params=pltpu.CompilerParams(vmem_limit_bytes=VMEM_BYTES),
        name="conv_forward",
    )(grid, tokens, w_expand, taps, w_project, norms)


def gather_forward(grid, tokens, w_depth, vectors, w_expand, w_project, w_qkv, w_out, w_up, w_down, layers):
    rows, width = tokens.shape
    hidden = w_expand.shape[1]
    chunks = hidden // CHUNK
    per_image = pl.BlockSpec((ROWS, width), lambda i: (i, 0))
    per_chunk = pl.BlockSpec((chunks, ROWS, CHUNK), lambda i: (0, i, 0))
    wide = jax.ShapeDtypeStruct((chunks, rows, CHUNK), BF16)
    tall = jax.ShapeDtypeStruct((rows, width), F32)
    anywhere = pl.BlockSpec(memory_space=pl.ANY)
    here = pl.BlockSpec(memory_space=pltpu.VMEM)
    span = -(-w_depth.shape[1] // 128) * 128
    mixed = (w_qkv.shape[0], w_qkv.shape[1] + w_out.shape[1])
    fulls = [(layers, 2) + shape for shape in (w_expand.shape, w_project.shape, mixed, w_up.shape, w_down.shape)]
    copies = 6 * (2 * layers + 2)
    return pl.pallas_call(
        gather_forward_kernel,
        grid=(rows // ROWS,),
        in_specs=[pl.BlockSpec(memory_space=pltpu.SMEM), per_image] + [here] * 7 + [anywhere] * 6,
        out_specs=[per_chunk, per_chunk, per_chunk, per_image, per_image, whole((16, hidden)), whole((8, width))]
        + [anywhere] * 5,
        out_shape=[wide, wide, wide, tall, tall, jax.ShapeDtypeStruct((16, hidden), F32), jax.ShapeDtypeStruct((8, width), F32)]
        + [jax.ShapeDtypeStruct(full, BF16) for full in fulls],
        scratch_shapes=[
            pltpu.VMEM((2, ROWS + 2 * GRID, CHUNK), F32),
            pltpu.VMEM(fulls[0], BF16),
            pltpu.VMEM(fulls[1], BF16),
            pltpu.VMEM((layers, 2, 16, span), F32),
            pltpu.VMEM((16, span), F32),
            pltpu.VMEM(mixed, BF16),
            pltpu.SemaphoreType.DMA((copies,)),
            pltpu.SemaphoreType.DMA((copies,)),
            pltpu.SemaphoreType.DMA((10,)),
        ],
        compiler_params=pltpu.CompilerParams(
            vmem_limit_bytes=VMEM_BYTES, collective_id=0, has_side_effects=True
        ),
        name="gather_forward",
    )(grid, tokens, w_depth, *vectors, w_expand, w_project, w_qkv, w_out, w_up, w_down)


def middle_kernel(
    grid_ref, first_ref, cotan_ref, mixed_ref, up_ref, down_ref, norms_ref,
    layer_ref, d_first_ref, g_mixed_ref, g_up_ref, g_down_ref, g_norm_ref,
    a_mixed, a_up, a_down, expo, keys, values, queries, attended_t, d_qkv,
):
    image = pl.program_id(0)
    width = first_ref.shape[1]
    hidden = up_ref.shape[1]
    pairs = width // 128

    @pl.when(image == 0)
    def _():
        for ref in (a_mixed, a_up, a_down, g_norm_ref):
            ref[...] = jnp.zeros_like(ref)

    high, wide = grid_ref[image, 0], grid_ref[image, 1]
    valid = valid_cells(high, wide, (ROWS, width))
    first = first_ref[...]
    unit1, inverse1 = normalized(first)
    normed = (unit1 * norms_ref[3:4, :] + norms_ref[4:5, :]).astype(BF16)
    packed = dot_nn(normed, mixed_ref[:, : 3 * width]).astype(BF16)
    lane = lax.broadcasted_iota(jnp.int32, (ROWS, 128), 1) // HDIM
    line = lax.broadcasted_iota(jnp.int32, (128, ROWS), 0) // HDIM
    zero = jnp.zeros((ROWS, 128), BF16)
    key_bias = jnp.where(valid_cells(high, wide, (ROWS, ROWS)), 0.0, -1e9)
    key_bias = jnp.concatenate((key_bias, key_bias), axis=0)
    inverses = []
    for pair in range(pairs):
        at = pair * 128
        query = packed[:, at : at + 128] * jnp.asarray(HDIM**-0.5, BF16)
        key = packed[:, width + at : width + at + 128]
        value = packed[:, 2 * width + at : 2 * width + at + 128]
        for head in range(2):
            keys[pair, head * ROWS : (head + 1) * ROWS] = jnp.where(lane == head, key, zero)
            values[pair, head * ROWS : (head + 1) * ROWS] = jnp.where(lane == head, value, zero)
            queries[pair, head * ROWS : (head + 1) * ROWS] = jnp.where(lane == head, query, zero)
        scores = dot_nt(keys[pair], query) + key_bias
        totals = []
        for head in range(2):
            part = scores[head * ROWS : (head + 1) * ROWS]
            power = jnp.exp(part - jnp.max(part, axis=0, keepdims=True))
            totals.append(1.0 / jnp.sum(power, axis=0, keepdims=True))
            expo[pair, head * ROWS : (head + 1) * ROWS] = power.astype(BF16)
        inverse = jnp.where(line == 0, totals[0], totals[1])
        inverses.append(inverse)
        attended_t[at : at + 128] = (dot_tn(values[pair], expo[pair]) * inverse).astype(BF16)
    second = first + jnp.where(valid, dot_tn(attended_t[...], mixed_ref[:, 3 * width :]), 0.0)

    cotan = cotan_ref[...]
    unit2, inverse2 = normalized(second)
    normed3 = (unit2 * norms_ref[5:6, :] + norms_ref[6:7, :]).astype(BF16)
    d_down = jnp.where(valid, cotan, jnp.zeros_like(cotan))
    normed3_t = normed3.T
    d_down_t = d_down.T
    result = jnp.zeros((ROWS, width), F32)
    d_normed3 = jnp.zeros((ROWS, width), F32)
    for chunk in range(hidden // CHUNK):
        columns = slice(chunk * CHUNK, (chunk + 1) * CHUNK)
        upper = dot_nn(normed3, up_ref[:, columns])
        d_hidden = dot_nt(d_down, down_ref[columns, :])
        square = upper * upper
        bent = jnp.tanh(upper * (0.7978845608028654 + (0.7978845608028654 * 0.044715) * square))
        gate = 0.5 * bent + 0.5
        hid = (upper * gate).astype(BF16)
        slope = gate + upper * (gate - gate * gate) * (
            2 * 0.7978845608028654 + (6 * 0.7978845608028654 * 0.044715) * square
        )
        d_upper = (d_hidden * slope).astype(BF16)
        result = result + dot_nn(hid, down_ref[columns, :])
        a_down[:, columns] += dot_nn(d_down_t, hid)
        a_up[:, columns] += dot_nn(normed3_t, d_upper)
        d_normed3 = d_normed3 + dot_nt(d_upper, up_ref[:, columns])
    layer_ref[...] = (second + jnp.where(valid, result, 0.0)).astype(BF16)

    g_norm_ref[0:8] += fold_rows(d_normed3 * unit2)
    g_norm_ref[8:16] += fold_rows(d_normed3)
    d_second = cotan.astype(F32) + norm_pull(d_normed3, norms_ref[5:6, :], unit2, inverse2)

    d_out = jnp.where(valid, d_second, 0.0).astype(BF16)
    a_mixed[:, 3 * width :] += dot_nn(attended_t[...], d_out)
    for pair in range(pairs):
        at = pair * 128
        d_attended = dot_nt(mixed_ref[at : at + 128, 3 * width :], d_out)
        inverse = inverses[pair]
        d_low = d_attended.astype(BF16)
        inner = d_low.astype(F32) * attended_t[at : at + 128].astype(F32)
        d_scaled = d_low.astype(F32) * inverse
        d_scaled_low = d_scaled.astype(BF16)
        inner = inner * inverse
        deltas = [jnp.sum(inner[head * HDIM : (head + 1) * HDIM], axis=0, keepdims=True) for head in range(2)]
        d_probs = dot_nn(values[pair], d_scaled_low)
        d_value = jnp.zeros((ROWS, 128), F32)
        d_key = jnp.zeros((ROWS, 128), F32)
        steps = []
        for head in range(2):
            rows = slice(head * ROWS, (head + 1) * ROWS)
            power = expo[pair, rows]
            d_score = (power.astype(F32) * (d_probs[rows] - deltas[head])).astype(BF16)
            steps.append(d_score)
            own = jnp.where(line == head, d_scaled_low, jnp.zeros_like(d_scaled_low))
            d_value = d_value + dot_nt(power, own)
            d_key = d_key + dot_nn(d_score, queries[pair, rows])
        d_query_t = dot_tn(keys[pair], jnp.concatenate(steps, axis=0)) * (HDIM**-0.5)
        d_qkv[:, at : at + 128] = d_query_t.astype(BF16).T
        d_qkv[:, width + at : width + at + 128] = d_key.astype(BF16)
        d_qkv[:, 2 * width + at : 2 * width + at + 128] = d_value.astype(BF16)
    a_mixed[:, : 3 * width] += dot_nn(normed.T, d_qkv[...])
    d_normed = dot_nt(d_qkv[...], mixed_ref[:, : 3 * width])
    g_norm_ref[16:24] += fold_rows(d_normed * unit1)
    g_norm_ref[24:32] += fold_rows(d_normed)
    d_first_ref[...] = d_second + norm_pull(d_normed, norms_ref[3:4, :], unit1, inverse1)

    @pl.when(image == pl.num_programs(0) - 1)
    def _():
        g_mixed_ref[...] = a_mixed[...].astype(BF16)
        g_up_ref[...] = a_up[...].astype(BF16)
        g_down_ref[...] = a_down[...].astype(BF16).T


def middle(grid, first, cotangent, w_mixed, w_up, w_down, norms):
    rows, width = first.shape
    hidden = w_up.shape[1]
    pairs = width // 128
    per_image = pl.BlockSpec((ROWS, width), lambda i: (i, 0))
    weights = (w_mixed, w_up, w_down)
    return pl.pallas_call(
        middle_kernel,
        grid=(rows // ROWS,),
        in_specs=[pl.BlockSpec(memory_space=pltpu.SMEM), per_image, per_image]
        + [whole(weight.shape) for weight in weights]
        + [whole(norms.shape)],
        out_specs=[per_image, per_image] + [whole(weight.shape) for weight in weights] + [whole((32, width))],
        out_shape=[jax.ShapeDtypeStruct((rows, width), BF16), jax.ShapeDtypeStruct((rows, width), F32)]
        + [jax.ShapeDtypeStruct(weight.shape, BF16) for weight in weights]
        + [jax.ShapeDtypeStruct((32, width), F32)],
        scratch_shapes=[
            pltpu.VMEM(w_mixed.shape, F32),
            pltpu.VMEM(w_up.shape, F32),
            pltpu.VMEM((width, hidden), F32),
            pltpu.VMEM((pairs, 2 * ROWS, ROWS), BF16),
            pltpu.VMEM((pairs, 2 * ROWS, 128), BF16),
            pltpu.VMEM((pairs, 2 * ROWS, 128), BF16),
            pltpu.VMEM((pairs, 2 * ROWS, 128), BF16),
            pltpu.VMEM((width, ROWS), BF16),
            pltpu.VMEM((ROWS, 3 * width), BF16),
        ],
        compiler_params=pltpu.CompilerParams(vmem_limit_bytes=VMEM_BYTES),
        name="middle",
    )(grid, first, cotangent, *weights, norms)


def part_of(ref, lead, index, count=2):
    rows, columns = ref.shape[-2:]
    if columns > rows * 4:
        size = columns // count
        return ref.at[lead + (slice(None), pl.ds(pl.multiple_of(index * size, size), size))]
    size = rows // count
    return ref.at[lead + (pl.ds(pl.multiple_of(index * size, size), size), slice(None))]


def part_shape(shape, count=2):
    rows, columns = shape
    return (rows, columns // count) if columns > rows * 4 else (rows // count, columns)


class Reduce:
    def __init__(self, terms, mine, result, cross, buffers, sems, base):
        sends, receives, locals_ = sems
        self.terms, self.mine, self.result, self.cross = terms, mine, result, cross
        self.layers = terms.shape[0]
        self.x, self.core, self.z, self.y = places(2)
        self.along_devices, across, sibling, beyond = peers_of(self.layers)
        buffers = list(buffers)
        every = (slice(None), slice(None))
        self.from_core, self.chip = buffers[:2]
        other = part_of(terms, every, 1 - self.core)
        self.inside = remote(other, self.from_core, sends, receives, base, sibling)
        self.fetch = None
        if mine is not None:
            self.fetch = pltpu.make_async_copy(part_of(terms, every, self.core), mine, locals_.at[base])
        rest = buffers[2:]
        if cross:
            self.from_cross, self.wide = rest[:2]
            self.over_x = remote(part_of(self.chip, every, 1 - self.x), self.from_cross, sends, receives, base + 1, beyond)
            rest = rest[2:]
        else:
            self.wide = self.chip
        self.from_side, self.line, self.from_along, self.own, self.from_x, self.total = rest
        self.over = remote(self.wide.at[:, 1 - self.y], self.from_side, sends, receives, base + 2, across)
        self.along = [
            remote(self.line.at[self.z ^ (step + 1)], self.from_along.at[step], sends, receives, base + 3 + step, device)
            for step, device in enumerate(self.along_devices)
        ]
        base += 3 + self.layers - 1
        half = part_of(result, (), self.core)
        if cross:
            self.spot = part_of(half, (), self.x)
            self.beyond = remote(self.total, self.spot, sends, receives, base, beyond)
            self.back = remote(half, half, sends, receives, base + 1, sibling)
        else:
            self.spot = half
            self.beyond = remote(self.own, self.from_x, sends, receives, base, beyond)
            self.back = remote(self.total, half, sends, receives, base + 1, sibling)

    def start(self):
        self.inside.start()
        if self.fetch is not None:
            self.fetch.start()

    def add_core(self):
        if self.fetch is not None:
            self.fetch.wait()
        self.inside.wait_recv()
        for z in range(self.layers):
            for y in range(2):
                if self.mine is not None:
                    own = self.mine[z, y]
                else:
                    own = part_of(self.terms, (z, y), self.core)[...]
                self.chip[z, y] = own + self.from_core[z, y]
        (self.over_x if self.cross else self.over).start()

    def add_cross(self):
        self.over_x.wait_recv()
        for z in range(self.layers):
            for y in range(2):
                self.wide[z, y] = part_of(self.chip, (z, y), self.x)[...] + self.from_cross[z, y]
        self.over.start()

    def add_side(self):
        self.over.wait_recv()
        for z in range(self.layers):
            self.line[z] = self.wide[z, self.y] + self.from_side[z]
        for copy in self.along:
            copy.start()

    def add_line(self):
        mine = self.line[self.z].astype(F32)
        for step, copy in enumerate(self.along):
            copy.wait_recv()
            mine = mine + self.from_along[step].astype(F32)
        if self.cross:
            self.total[...] = mine
            self.spot[...] = mine
        else:
            self.own[...] = mine.astype(self.own.dtype)
        self.beyond.start()

    def add_x(self):
        self.beyond.wait_recv()
        if not self.cross:
            mine = self.own[...].astype(F32) + self.from_x[...].astype(F32)
            self.total[...] = mine
            self.spot[...] = mine
        self.back.start()

    def finish(self):
        self.back.wait_recv()
        copies = [self.inside, self.over, self.beyond, self.back] + self.along
        if self.cross:
            copies.append(self.over_x)
        for copy in copies:
            copy.wait_send()


def reduce_buffers(shape, dtype, cross):
    layers, sides = shape[:2]
    half = part_shape(shape[2:])
    last = part_shape(half) if cross else half
    buffers = [(layers, sides) + half] * 2
    if cross:
        buffers += [(layers, sides) + last] * 2
    buffers += [(layers,) + last] * 2 + [(layers - 1,) + last, last, last]
    return [pltpu.VMEM(buffer, dtype) for buffer in buffers] + [pltpu.VMEM(last, F32)]


def conv_backward_kernel(layers, *refs):
    quick = layers > 0
    take = iter(refs)
    grid_ref = next(take)
    tokens_hbm, d_first_hbm, projected_hbm, field_hbm, act_hbm, pull_hbm = [next(take) for _ in range(6)]
    expand_hbm, taps_ref, project_hbm, norms_ref = [next(take) for _ in range(4)]
    if quick:
        late_norm_ref = next(take)
        late = [next(take) for _ in range(3)]
    d_tokens_ref = next(take)
    if quick:
        results = [next(take) for _ in range(6)]
    else:
        g_expand_ref, g_project_ref, g_taps_ref, g_norm_ref = [next(take) for _ in range(4)]
    (tokens_v, d_image, projected_v, field, act, pull, expand, project, load_sems) = [next(take) for _ in range(9)]
    (d_proj, d_proj_t, tokens_t, keep, taps_b, a_expand, a_project, a_taps, a_norm) = [next(take) for _ in range(9)]
    frames = [next(take), next(take)]
    fields = [next(take), next(take)]
    images, _, width = d_proj.shape
    images -= 1
    chunks = field.shape[0]
    hidden = chunks * CHUNK
    items = images * chunks
    per = images // 2

    loads = []
    for number, (source, target) in enumerate(
        ((projected_hbm, projected_v), (d_first_hbm, d_image), (tokens_hbm, tokens_v), (project_hbm, project))
    ):
        loads.append(pltpu.make_async_copy(source, target, load_sems.at[number]))
    for chunk in range(chunks):
        source = expand_hbm.at[:, chunk * CHUNK : (chunk + 1) * CHUNK]
        loads.append(pltpu.make_async_copy(source, expand.at[chunk], load_sems.at[4 + chunk]))
    base = 4 + chunks

    def stream(kind, chunk):
        source, target = ((act_hbm, act), (pull_hbm, pull), (field_hbm, field))[kind]
        return pltpu.make_async_copy(source.at[chunk], target.at[chunk], load_sems.at[base + kind * chunks + chunk])

    for load in loads:
        load.start()
    for chunk in range(chunks):
        for kind in range(3):
            stream(kind, chunk).start()

    plan = {}
    if quick:
        number = 0
        stage_project, stage_small = next(take), next(take)
        stage_expand = [next(take) for _ in range(chunks)]
        mines = [next(take) for _ in range(3)]
        rest = list(take)
        sems = rest[-3:]
        rest = rest[:-3]
        span = 3 + layers + 1

        def reducer(terms, mine, result, cross):
            nonlocal number, rest
            count = 10 if cross else 8
            made = Reduce(terms, mine, result, cross, rest[:count], sems, number * span)
            rest = rest[count:]
            number += 1
            return made

        mixed = reducer(late[0], mines[0], results[3], True)
        up = reducer(late[1], mines[1], results[4], False)
        down = reducer(late[2], mines[2], results[5], True)
        whole_project = reducer(stage_project, None, results[2], False)
        parts = [
            reducer(stage_expand[c], None, results[1].at[:, c * CHUNK : (c + 1) * CHUNK], False) for c in range(chunks)
        ]
        small = reducer(stage_small, None, results[0], False)
        along, across, sibling, beyond = peers_of(layers)
        greet(along + [across, sibling, beyond])
        for part in (up, down, mixed):
            part.start()

        def send_project():
            for chunk in range(chunks):
                lines = a_project[chunk].astype(BF16).T
                for f in range(2 * layers):
                    lo, hi = max(f * (hidden // (2 * layers)), chunk * CHUNK), min((f + 1) * (hidden // (2 * layers)), (chunk + 1) * CHUNK)
                    if lo < hi:
                        at = lo - f * (hidden // (2 * layers))
                        stage_project[f // 2, f % 2, at : at + hi - lo] = lines[lo - chunk * CHUNK : hi - chunk * CHUNK]
            whole_project.start()

        def send_part(chunk):
            stage_expand[chunk][...] = a_expand[chunk].astype(BF16).reshape(stage_expand[chunk].shape)
            parts[chunk].start()

        def at(segment, *works):
            plan.setdefault(segment, []).extend(works)

        at(2, up.add_core, down.add_core)
        at(3, mixed.add_core, lambda: send_part(0))
        at(5, lambda: send_part(1), parts[0].add_core)
        at(6, send_project)
        at(7, up.add_side, down.add_cross, lambda: send_part(2), parts[1].add_core)
        at(8, whole_project.add_core)
        at(9, parts[0].add_side, lambda: send_part(3), parts[2].add_core)
        at(10, down.add_side, parts[1].add_side)
        at(11, mixed.add_cross, lambda: send_part(4), parts[3].add_core)

    a_norm[...] = jnp.zeros_like(a_norm)
    a_taps[...] = jnp.zeros_like(a_taps)
    a_expand[...] = jnp.zeros_like(a_expand)
    a_project[...] = jnp.zeros_like(a_project)
    d_proj[images] = jnp.zeros((ROWS, width), BF16)
    for ref in frames + fields:
        ref[...] = jnp.zeros_like(ref)
    for chunk in range(chunks):
        for k in range(9):
            line = taps_ref[k : k + 1, chunk * CHUNK : (chunk + 1) * CHUNK]
            taps_b[chunk, k] = jnp.broadcast_to(line, (GRID, CHUNK)).astype(BF16)
    for load in loads[:3]:
        load.wait()

    @pl.loop(0, images)
    def _(image):
        high, wide = grid_ref[image, 0], grid_ref[image, 1]
        valid = valid_cells(high, wide, (ROWS, width))
        keep[image] = jnp.where(valid_cells(high, wide, (ROWS, 128)), 1.0, 0.0).astype(BF16)
        unit, inverse = normalized(projected_v[image])
        grad = jnp.where(valid, d_image[image], 0.0)
        a_norm[0:8] += fold_rows(grad * unit)
        a_norm[8:16] += fold_rows(grad)
        low = norm_pull(grad, norms_ref[1:2, :], unit, inverse).astype(BF16)
        d_proj[image] = low
        d_proj_t[:, pl.ds(pl.multiple_of(image * ROWS, ROWS), ROWS)] = low.T
        tokens_t[image] = tokens_v[image].T

    for load in loads[3:]:
        load.wait()

    def item(t):
        t = jnp.clip(t, 0, items - 1)
        return t // images, t % images

    def step(t, odd, lead):
        c2, i2 = item(t - 2)
        ready = fields[odd][...]
        a_expand[c2] += dot_nn(tokens_t[i2], ready)
        d_image[i2] += dot_nt(ready, expand[c2])
        c0, i0 = item(t)
        d_act = dot_nt(d_proj[jnp.where(t < items, i0, images)], project[c0])
        if lead:
            cp, ip = item(2 * t)
            two = pl.ds(pl.multiple_of(ip * ROWS, 2 * ROWS), 2 * ROWS)
            a_project[cp] += dot_nn(d_proj_t[:, two], act[cp, two, :])
        c1, i1 = item(t - 1)
        old, new = frames[1 - odd], frames[odd]
        block = 64
        rows = block // GRID
        for half in range(CHUNK // 128):
            lanes = slice(half * 128, (half + 1) * 128)
            taps = [taps_b[c1, k, :, lanes] for k in range(9)]
            totals = [jnp.zeros((8, 128), F32) for _ in range(9)]
            for start in range(0, ROWS, block):
                own = field[c1, pl.ds(pl.multiple_of(i1 * ROWS, ROWS) + start, block), lanes].reshape(rows, GRID, 128)
                lines = []
                for a in range(3):
                    line = None
                    for b in range(3):
                        k = 3 * a + b
                        at = start + GRID * (2 - a)
                        near = old[b, at : at + block, lanes].reshape(rows, GRID, 128)
                        term = taps[k] * near
                        line = term if line is None else line + term
                        prod = near * own
                        quad = ((prod[0] + prod[1]) + (prod[2] + prod[3])).astype(F32)
                        totals[k] = totals[k] + (quad[:8] + quad[8:])
                    lines.append(line)
                grad = (lines[0] + lines[1] + lines[2]).reshape(block, 128)
                fields[1 - odd][start : start + block, lanes] = grad * keep[i1, start : start + block, :]
            for k in range(9):
                a_taps[c1, 8 * k : 8 * k + 8, lanes] += totals[k]
        d_conv = d_act * pull[c0, pl.ds(pl.multiple_of(i0 * ROWS, ROWS), ROWS), :].astype(F32)
        new[0, GRID : GRID + ROWS] = move_cells(d_conv, -1).astype(BF16)
        new[1, GRID : GRID + ROWS] = d_conv.astype(BF16)
        new[2, GRID : GRID + ROWS] = move_cells(d_conv, 1).astype(BF16)

    def segment(s, lead):
        for key in plan:
            @pl.when(s == key)
            def _(works=plan[key]):
                for work in works:
                    work()

        if lead:
            stream(0, s).wait()

        @pl.when(s % 2 == 0)
        def _():
            stream(1, s // 2).wait()
            stream(2, s // 2).wait()

        @pl.loop(0, per // 2)
        def _(pair):
            t = s * per + pair * 2
            step(t, 0, lead)
            step(t + 1, 1, lead)

    middle_segment = chunks
    pl.loop(0, middle_segment)(lambda s: segment(s, True))
    pl.loop(middle_segment, 2 * chunks)(lambda s: segment(s, False))
    step(items, 0, False)
    step(items + 1, 1, False)

    if not quick:
        for chunk in range(chunks):
            g_expand_ref[:, chunk * CHUNK : (chunk + 1) * CHUNK] = a_expand[chunk].astype(BF16)
            g_project_ref[chunk * CHUNK : (chunk + 1) * CHUNK, :] = a_project[chunk].astype(BF16).T
            g_taps_ref[:, chunk * CHUNK : (chunk + 1) * CHUNK] = a_taps[chunk]
        g_norm_ref[...] = a_norm[...]
        for image in range(images):
            d_tokens_ref[image * ROWS : (image + 1) * ROWS, :] = d_image[image].astype(BF16)
        return

    send_part(chunks - 1)
    lines = []
    for k in range(9):
        line = jnp.concatenate([a_taps[c, 8 * k : 8 * k + 8, :] for c in range(chunks)], axis=1)
        lines.append(jnp.sum(line, axis=0, keepdims=True))
    depth = jnp.concatenate(lines, axis=0)
    vectors = [a_norm[0:8], a_norm[8:16]] + [late_norm_ref[8 * k : 8 * k + 8] for k in (2, 3, 0, 1)]
    vectors = jnp.concatenate([jnp.sum(vector, axis=0, keepdims=True) for vector in vectors], axis=0)
    share, thin = hidden // (2 * layers), width // (2 * layers)
    stage_small[...] = jnp.zeros_like(stage_small)
    for f in range(2 * layers):
        stage_small[f // 2, f % 2, 0:9, 0:share] = depth[:, f * share : (f + 1) * share]
        stage_small[f // 2, f % 2, 9:15, 0:thin] = vectors[:, f * thin : (f + 1) * thin]
    small.start()
    whole_project.add_side()
    parts[2].add_side()
    up.add_line()
    for image in range(images):
        d_tokens_ref[image * ROWS : (image + 1) * ROWS, :] = d_image[image].astype(BF16)
    parts[4].add_core()
    parts[5].add_core()
    small.add_core()
    down.add_line()
    parts[0].add_line()
    parts[1].add_line()
    parts[3].add_side()
    mixed.add_side()
    parts[4].add_side()
    parts[5].add_side()
    small.add_side()
    up.add_x()
    down.add_x()
    whole_project.add_line()
    parts[0].add_x()
    parts[1].add_x()
    parts[2].add_line()
    parts[3].add_line()
    mixed.add_line()
    parts[4].add_line()
    parts[5].add_line()
    small.add_line()
    whole_project.add_x()
    parts[2].add_x()
    parts[3].add_x()
    mixed.add_x()
    parts[4].add_x()
    parts[5].add_x()
    small.add_x()
    for part in [up, down, mixed, whole_project, small] + parts:
        part.finish()


def conv_backward(grid, tokens, d_first, projected, field, act, pull, w_expand, taps, w_project, norms, late=None):
    rows, width = tokens.shape
    hidden = w_expand.shape[1]
    chunks = hidden // CHUNK
    images = rows // ROWS
    anywhere = pl.BlockSpec(memory_space=pl.ANY)
    here = pl.BlockSpec(memory_space=pltpu.VMEM)
    by_image = (images, ROWS, width)
    wide = (chunks, rows, CHUNK)
    scratch = [
        pltpu.VMEM(by_image, BF16),
        pltpu.VMEM(by_image, F32),
        pltpu.VMEM(by_image, F32),
        pltpu.VMEM(wide, BF16),
        pltpu.VMEM(wide, BF16),
        pltpu.VMEM(wide, BF16),
        pltpu.VMEM((chunks, width, CHUNK), BF16),
        pltpu.VMEM((chunks, CHUNK, width), BF16),
        pltpu.SemaphoreType.DMA((4 + chunks * 4,)),
        pltpu.VMEM((images + 1, ROWS, width), BF16),
        pltpu.VMEM((width, rows), BF16),
        pltpu.VMEM((images, width, ROWS), BF16),
        pltpu.VMEM((images, ROWS, 128), BF16),
        pltpu.VMEM((chunks, 9, GRID, CHUNK), BF16),
        pltpu.VMEM((chunks, width, CHUNK), F32),
        pltpu.VMEM((chunks, width, CHUNK), F32),
        pltpu.VMEM((chunks, 72, CHUNK), F32),
        pltpu.VMEM((16, width), F32),
    ]
    scratch += [pltpu.VMEM((3, ROWS + 2 * GRID, CHUNK), BF16)] * 2 + [pltpu.VMEM((ROWS, CHUNK), BF16)] * 2
    operands = [
        grid, tokens.reshape(by_image), d_first.reshape(by_image), projected.reshape(by_image), field, act, pull,
        w_expand, taps, w_project.reshape(chunks, CHUNK, width), norms,
    ]
    in_specs = [pl.BlockSpec(memory_space=pltpu.SMEM)] + [anywhere] * 7 + [here, anywhere, here]
    d_tokens = jax.ShapeDtypeStruct((rows, width), BF16)
    if late is None:
        layers, params = 0, {}
        out_shape = [
            d_tokens,
            jax.ShapeDtypeStruct(w_expand.shape, BF16),
            jax.ShapeDtypeStruct(w_project.shape, BF16),
            jax.ShapeDtypeStruct((72, hidden), F32),
            jax.ShapeDtypeStruct((16, width), F32),
        ]
    else:
        g_norm, g_mixed, g_up, g_down = late
        layers = g_up.shape[0]
        params = dict(collective_id=1, has_side_effects=True)
        operands += [g_norm, g_mixed, g_up, g_down]
        in_specs += [here] + [anywhere] * 3
        span = -(-hidden // (2 * layers) // 128) * 128
        b_small, b_expand, b_project = (16, span), (width // (2 * layers), hidden), (hidden // (2 * layers), width)
        blocks = (b_small, b_expand, b_project, g_mixed.shape[2:], g_up.shape[2:], g_down.shape[2:])
        out_shape = [d_tokens] + [jax.ShapeDtypeStruct(block, F32) for block in blocks]
        lead = (layers, 2)
        piece = (b_expand[0], CHUNK)
        scratch += [pltpu.VMEM(lead + b_project, BF16), pltpu.VMEM(lead + b_small, F32)]
        scratch += [pltpu.VMEM(lead + piece, BF16)] * chunks
        scratch += [pltpu.VMEM(lead + part_shape(block), BF16) for block in blocks[3:]]
        for shape, dtype, cross in (
            [(blocks[3], BF16, True), (blocks[4], BF16, False), (blocks[5], BF16, True), (blocks[2], BF16, False)]
            + [(piece, BF16, False)] * chunks
            + [(b_small, F32, False)]
        ):
            scratch += reduce_buffers(lead + shape, dtype, cross)
        copies = (5 + chunks) * (4 + layers)
        scratch += [pltpu.SemaphoreType.DMA((copies,))] * 3
    return pl.pallas_call(
        functools.partial(conv_backward_kernel, layers),
        in_specs=in_specs,
        out_specs=[here] * len(out_shape),
        out_shape=out_shape,
        scratch_shapes=scratch,
        compiler_params=pltpu.CompilerParams(vmem_limit_bytes=VMEM_BYTES, **params),
        name="conv_backward",
    )(*operands)


def reduce_plain(terms):
    results = []
    for term in terms:
        share = lax.psum_scatter(term, "fsdp", scatter_dimension=0, tiled=False)
        results.append(lax.psum(share, "dp").astype(F32))
    return results


def local(
    fsdp, quick,
    tokens, grid, w_expand, w_depth, w_project, gain_conv, bias_conv, gain_attend, bias_attend,
    w_qkv, w_out, gain_mlp, bias_mlp, w_up, w_down, cotangent,
):
    slots, rows, width = tokens.shape
    hidden = w_expand.shape[1]
    share, thin = w_depth.shape[1], gain_conv.shape[0]
    span = -(-share // 128) * 128
    vectors = (gain_conv, bias_conv, gain_attend, bias_attend, gain_mlp, bias_mlp)
    flat, cotan = tokens.reshape(slots * rows, width), cotangent.reshape(slots * rows, width)
    if quick:
        field, act, pull, projected, first, taps, norms, *fulls = gather_forward(
            grid, flat, w_depth, vectors, w_expand, w_project, w_qkv, w_out, w_up, w_down, fsdp // 2
        )
        f_expand, f_project, f_mixed, f_up, f_down = [full.reshape(-1, full.shape[3]) for full in fulls]
    else:
        mixed = jnp.concatenate((w_qkv, w_out), axis=1)
        f_expand, f_project, f_mixed, f_up, f_down = [
            lax.all_gather(shard, "fsdp", axis=0, tiled=True) for shard in (w_expand, w_project, mixed, w_up, w_down)
        ]
        taps = jnp.pad(lax.all_gather(w_depth, "fsdp", axis=1, tiled=True).astype(F32), ((0, 7), (0, 0)))
        lines = lax.all_gather(jnp.stack(vectors), "fsdp", axis=1, tiled=True).astype(F32)
        norms = jnp.pad(lines, ((1, 1), (0, 0)))
        field, act, pull, projected, first = conv_forward(grid, flat, f_expand, taps, f_project, norms)
    layer_out, d_first, g_mixed, g_up, g_down, g_norm = middle(grid, first, cotan, f_mixed, f_up, f_down, norms)
    inputs = (grid, flat, d_first, projected, field, act, pull, f_expand, taps, f_project, norms)
    if quick:
        late = [term.reshape((fsdp // 2, 2, -1, term.shape[1])) for term in (g_mixed, g_up, g_down)]
        d_tokens, small, s_expand, s_project, s_mixed, s_up, s_down = conv_backward(*inputs, late=[g_norm] + late)
    else:
        d_tokens, g_expand, g_project, g_taps, g_norm_conv = conv_backward(*inputs)
        g_taps = jnp.sum(g_taps.reshape(9, 8, fsdp, share), axis=1)
        g_norm = jnp.concatenate((g_norm_conv, g_norm[16:], g_norm[:16]), axis=0)
        g_norm = jnp.sum(g_norm.reshape(6, 8, fsdp, thin), axis=1)
        g_small = jnp.concatenate(
            (
                jnp.pad(g_taps, ((0, 0), (0, 0), (0, span - share))),
                jnp.pad(g_norm, ((0, 1), (0, 0), (0, span - thin))),
            ),
            axis=0,
        ).transpose(1, 0, 2)
        terms = [g_small] + [
            term.reshape((fsdp, -1, term.shape[1])) for term in (g_expand, g_project, g_mixed, g_up, g_down)
        ]
        small, s_expand, s_project, s_mixed, s_up, s_down = reduce_plain(terms)
    return (
        layer_out.reshape(tokens.shape),
        d_tokens.reshape(tokens.shape),
        s_expand,
        small[:9, :share],
        s_project,
        small[9, :thin],
        small[10, :thin],
        small[11, :thin],
        small[12, :thin],
        s_mixed[:, : 3 * width],
        s_mixed[:, 3 * width :],
        small[13, :thin],
        small[14, :thin],
        s_up,
        s_down,
    )


def solution(mesh):
    fsdp, dp = mesh.shape["fsdp"], mesh.shape["dp"]
    quick = fsdp == 8 and dp == 4
    images, wide, tall, vector = P(("dp", "fsdp"), None, None), P("fsdp", None), P(None, "fsdp"), P("fsdp")
    in_specs = (
        images, P(("dp", "fsdp"), None), wide, tall, wide, vector, vector, vector, vector,
        wide, wide, vector, vector, wide, wide, images,
    )
    out_specs = (
        images, images, wide, tall, wide, vector, vector, vector, vector,
        wide, wide, vector, vector, wide, wide,
    )
    return jax.shard_map(
        functools.partial(local, fsdp, quick), mesh=mesh, in_specs=in_specs, out_specs=out_specs, check_vma=False
    )
```

```python
import functools

import jax
import jax.numpy as jnp
from jax import lax
from jax.experimental import pallas as pl
from jax.experimental.pallas import tpu as pltpu
from jax.sharding import PartitionSpec as P

HDIM = 64
GRID = 16
ROWS = GRID * GRID
CHUNK = 256
EPSILON = 1e-05
VMEM_BYTES = 62 * 1024 * 1024
F32 = jnp.float32
BF16 = jnp.bfloat16


def dot_nn(left, right):
    return jnp.dot(left, right, preferred_element_type=F32)


def dot_nt(left, right):
    return lax.dot_general(left, right, (((1,), (1,)), ((), ())), preferred_element_type=F32)


def dot_tn(left, right):
    return lax.dot_general(left, right, (((0,), (0,)), ((), ())), preferred_element_type=F32)


def valid_cells(high, wide, shape):
    place = lax.broadcasted_iota(jnp.int32, shape, 0)
    return (place // GRID < high) & (place % GRID < wide)


def normalized(values):
    center = jnp.mean(values, axis=-1, keepdims=True)
    shifted = values - center
    spread = jnp.mean(shifted * shifted, axis=-1, keepdims=True)
    inverse = lax.rsqrt(spread + EPSILON)
    return shifted * inverse, inverse


def norm_pull(grad, gain, unit, inverse):
    scaled = grad * gain
    mean_plain = jnp.mean(scaled, axis=-1, keepdims=True)
    mean_unit = jnp.mean(scaled * unit, axis=-1, keepdims=True)
    return (scaled - mean_plain - unit * mean_unit) * inverse


def both(left, right):
    return jnp.concatenate((left, right), axis=1)


def fold_rows(values):
    rows, width = values.shape
    return jnp.sum(values.reshape(rows // 8, 8, width), axis=0)


def move_cells(values, step):
    rows, width = values.shape
    parts = values.reshape(rows // GRID, 2, 8, width)
    turned = pltpu.roll(parts, step % 8, axis=2)
    first, last = turned[:, 0:1], turned[:, 1:2]
    line = lax.broadcasted_iota(jnp.int32, first.shape, 2)
    if step == 1:
        edge = line == 0
        moved = jnp.concatenate((jnp.where(edge, 0.0, first), jnp.where(edge, first, last)), axis=1)
    else:
        edge = line == 7
        moved = jnp.concatenate((jnp.where(edge, last, first), jnp.where(edge, 0.0, last)), axis=1)
    return moved.reshape(rows, width)


MESH = pl.DeviceIdType.MESH


def places(sides):
    dp, fsdp = lax.axis_index("dp"), lax.axis_index("fsdp")
    return dp // 2, dp % 2, fsdp // sides, fsdp % sides


def part_of(ref, lead, index, count=2):
    rows, columns = ref.shape[-2:]
    if columns > rows * 4:
        size = columns // count
        return ref.at[lead + (slice(None), pl.ds(pl.multiple_of(index * size, size), size))]
    size = rows // count
    return ref.at[lead + (pl.ds(pl.multiple_of(index * size, size), size), slice(None))]


def part_shape(shape, count=2):
    rows, columns = shape
    return (rows, columns // count) if columns > rows * 4 else (rows // count, columns)


def remote(source, target, sends, receives, index, device):
    return pltpu.make_async_remote_copy(
        src_ref=source,
        dst_ref=target,
        send_sem=sends.at[index],
        recv_sem=receives.at[index],
        device_id=device,
        device_id_type=MESH,
    )


def greet(devices):
    barrier = pltpu.get_barrier_semaphore()
    for device in devices:
        pl.semaphore_signal(barrier, inc=1, device_id=device, device_id_type=MESH)
    pl.semaphore_wait(barrier, len(devices))


def peers_of(layers):
    x, core, z, y = places(2)
    dp, fsdp = x * 2 + core, z * 2 + y
    along = [(dp, (z ^ step) * 2 + y) for step in range(1, layers)]
    return along, (dp, z * 2 + 1 - y), (x * 2 + 1 - core, fsdp), ((1 - x) * 2 + core, fsdp)


class Gather:
    def __init__(self, shard, full, cross, sems, number):
        sends, receives, locals_ = sems
        self.full, self.cross, self.layers = full, cross, full.shape[0]
        self.x, self.core, self.z, self.y = places(2)
        along, across, sibling, beyond = peers_of(self.layers)
        base = number * (2 * self.layers + 3)
        own = self.piece(shard, ())
        spot = self.piece(full, (self.z, self.y))
        self.local = pltpu.make_async_copy(own, spot, locals_.at[number])
        self.along = [remote(own, spot, sends, receives, base + step, device) for step, device in enumerate(along)]
        base += self.layers - 1
        self.over = []
        for step in range(self.layers):
            target = self.piece(full, (self.z ^ step, self.y))
            self.over.append(remote(own if step == 0 else target, target, sends, receives, base + step, across))
        base += self.layers
        self.beyond, self.inside = [], []
        for step, side in enumerate((self.y, 1 - self.y)):
            half = part_of(full, (slice(None), side), self.core)
            self.inside.append(remote(half, half, sends, receives, base + step, sibling))
            if cross:
                target = self.piece(full, (slice(None), side))
                self.beyond.append(remote(target, target, sends, receives, base + 2 + step, beyond))

    def piece(self, ref, lead):
        half = part_of(ref, lead, self.core)
        return part_of(half, (slice(None),) * (len(half.shape) - 2), self.x) if self.cross else half

    def start(self):
        for copy in self.along:
            copy.start()
        self.over[0].start()
        self.local.start()

    def forward(self):
        for step, copy in enumerate(self.along):
            copy.wait_recv()
            self.over[step + 1].start()
        self.local.wait()
        (self.beyond if self.cross else self.inside)[0].start()

    def side(self):
        for copy in self.over:
            copy.wait_recv()
        (self.beyond if self.cross else self.inside)[1].start()

    def share(self):
        for copy, after in zip(self.beyond, self.inside):
            copy.wait_recv()
            after.start()

    def finish(self):
        for copy in self.inside:
            copy.wait_recv()

    def drain(self):
        for copy in self.along + self.over + self.beyond + self.inside:
            copy.wait_send()


class Spread:
    def __init__(self, block, full, sems, base):
        sends, receives, local = sems
        layers = full.shape[0]
        x, core, z, y = places(2)
        spot = full.at[z, y]
        self.local = pltpu.make_async_copy(block, spot, local)
        self.copies = [
            remote(block, spot, sends, receives, base + 2 * up + over - 1, (x * 2 + core, (z ^ up) * 2 + (y ^ over)))
            for up in range(layers)
            for over in range(2)
            if up + over > 0
        ]

    def start(self):
        for copy in self.copies:
            copy.start()
        self.local.start()

    def finish(self):
        for copy in self.copies:
            copy.wait_recv()
        self.local.wait()

    def drain(self):
        for copy in self.copies:
            copy.wait_send()


def spread_taps(taps_ref, taps_b):
    for chunk in range(taps_b.shape[0]):
        for k in range(9):
            line = taps_ref[k : k + 1, chunk * CHUNK : (chunk + 1) * CHUNK]
            taps_b[chunk, k] = jnp.broadcast_to(line, (GRID, CHUNK)).astype(BF16)


def conv_chunk(chunk, kept, weights, taps_ref, frames, field_ref, act_ref, pull_ref, acts, slot):
    expanded = dot_nn(kept, weights)
    block = 64
    for half in range(CHUNK // 128):
        lanes = slice(half * 128, (half + 1) * 128)
        field_ref[chunk * 2 + half] = expanded[:, lanes].astype(BF16)
        frames[chunk % 2, half, GRID : GRID + ROWS] = expanded[:, lanes]
        whole = slice(chunk * CHUNK + half * 128, chunk * CHUNK + (half + 1) * 128)
        taps = [taps_ref[k : k + 1, whole] for k in range(9)]
        for start in range(0, ROWS, block):
            near = [frames[chunk % 2, half, start + GRID * a : start + GRID * a + block] for a in range(3)]
            sums = [sum(taps[3 * a + b] * near[a] for a in range(3)) for b in range(3)]
            conv = sums[1] + move_cells(sums[0], 1) + move_cells(sums[2], -1)
            gate = 0.5 * jnp.tanh(0.5 * conv) + 0.5
            act = conv * gate
            low = act.astype(BF16)
            act_ref[chunk * 2 + half, start : start + block] = low
            acts[slot, chunk * 2 + half, start : start + block] = low
            pull_ref[chunk * 2 + half, start : start + block] = (gate + act * (1.0 - gate)).astype(BF16)


def project_chunks(chunk, acts, slot, project):
    left = jnp.concatenate([acts[slot, 2 * chunk + part] for part in range(4)], axis=1)
    return dot_nn(left, project[chunk * CHUNK : (chunk + 2) * CHUNK, :])


def end_forward(projected, tokens, valid, norms_ref, projected_ref, first_ref):
    projected_ref[...] = projected
    unit, _ = normalized(projected)
    shift = unit * norms_ref[1:2, :] + norms_ref[2:3, :]
    first_ref[...] = tokens.astype(F32) + jnp.where(valid, shift, 0.0)


def conv_forward_body(
    step, before, middle_of_first, grid_ref, tokens_ref, late_tokens_ref, weights, project, norms_ref, taps_ref,
    field_ref, act_ref, pull_ref, projected_ref, first_ref, tokens_t_ref, keep_ref, frames, acts,
):
    width = tokens_ref.shape[1]
    chunks = weights.shape[0]
    images = pl.num_programs(0) - 2
    slot = lax.rem(step, 2)

    def start_image():
        valid = valid_cells(grid_ref[step, 0], grid_ref[step, 1], (ROWS, width))
        tokens = tokens_ref[...]
        tokens_t_ref[0] = tokens.T
        keep_ref[...] = jnp.where(valid[:, :128], 1.0, 0.0).astype(BF16)
        return jnp.where(valid, tokens, jnp.zeros_like(tokens))

    def convolve(chunk, kept):
        conv_chunk(chunk, kept, weights[chunk], taps_ref, frames, field_ref, act_ref, pull_ref, acts, slot)

    def end_image(projected):
        high, wide = grid_ref[step - 2, 0], grid_ref[step - 2, 1]
        valid = valid_cells(high, wide, (ROWS, width))
        end_forward(projected, late_tokens_ref[...], valid, norms_ref, projected_ref, first_ref)

    @pl.when(step == 0)
    def _():
        before()
        frames[...] = jnp.zeros_like(frames)
        kept = start_image()
        for chunk in range(chunks):
            middle_of_first(chunk)
            convolve(chunk, kept)

    @pl.when(step == 1)
    def _():
        kept = start_image()
        for chunk in range(chunks):
            convolve(chunk, kept)

    @pl.when((step > 1) & (step < images))
    def _():
        kept = start_image()
        projected = jnp.zeros((ROWS, width), F32)
        for chunk in range(0, chunks, 2):
            projected = projected + project_chunks(chunk, acts, slot, project)
            convolve(chunk, kept)
            convolve(chunk + 1, kept)
        end_image(projected)

    @pl.when(step >= images)
    def _():
        projected = jnp.zeros((ROWS, width), F32)
        for chunk in range(0, chunks, 2):
            projected = projected + project_chunks(chunk, acts, slot, project)
        end_image(projected)


def conv_forward_kernel(
    grid_ref, tokens_ref, late_tokens_ref, weights, taps_ref, project_ref, norms_ref,
    field_ref, act_ref, pull_ref, projected_ref, first_ref, tokens_t_ref, keep_ref, frames, acts,
):
    conv_forward_body(
        pl.program_id(0), lambda: None, lambda chunk: None,
        grid_ref, tokens_ref, late_tokens_ref, weights, project_ref, norms_ref, taps_ref,
        field_ref, act_ref, pull_ref, projected_ref, first_ref, tokens_t_ref, keep_ref, frames, acts,
    )


def gather_forward_kernel(
    grid_ref, tokens_ref, late_tokens_ref, depth_ref, gain1_ref, bias1_ref, gain2_ref, bias2_ref, gain3_ref, bias3_ref,
    s_expand, s_project, s_qkv, s_out, s_up, s_down,
    field_ref, act_ref, pull_ref, projected_ref, first_ref, tokens_t_ref, keep_ref,
    taps_ref, norms_ref, f_expand, f_project, f_mixed, f_up, f_down,
    frames, acts, weights, v_expand, v_project, v_small, own_small, own_mixed, sends, receives, locals_,
):
    step = pl.program_id(0)
    last = pl.num_programs(0) - 1
    sems = (sends, receives, locals_)
    layers = v_small.shape[0]
    hidden, width = taps_ref.shape[1], tokens_ref.shape[1]
    wide = v_expand.shape[-1]
    pieces = v_expand.shape[0]
    expand = [
        Gather(s_expand.at[:, piece * wide : (piece + 1) * wide], v_expand.at[piece], True, sems, piece)
        for piece in range(pieces)
    ]
    project = Gather(s_project, v_project, False, sems, pieces)
    mixed = Gather(own_mixed, f_mixed, True, sems, pieces + 1)
    up = Gather(s_up, f_up, True, sems, pieces + 2)
    down = Gather(s_down, f_down, False, sems, pieces + 3)
    count = pieces + 4
    small = Spread(own_small, v_small, (sends, receives, locals_.at[count]), count * (2 * layers + 3))
    share, thin = depth_ref.shape[1], gain1_ref.shape[0]
    cut = s_qkv.shape[1]
    joins = [
        pltpu.make_async_copy(s_qkv, own_mixed.at[:, :cut], locals_.at[count + 1]),
        pltpu.make_async_copy(s_out, own_mixed.at[:, cut:], locals_.at[count + 2]),
    ]
    save_expand = pltpu.make_async_copy(weights, f_expand, locals_.at[count + 3])
    save_project = pltpu.make_async_copy(v_project, f_project, locals_.at[count + 4])

    @pl.when(step == 0)
    def _():
        for join in joins:
            join.start()
        own_small[...] = jnp.zeros_like(own_small)
        own_small[0:9, 0:share] = depth_ref[...].astype(F32)
        for line, ref in enumerate((gain1_ref, bias1_ref, gain2_ref, bias2_ref, gain3_ref, bias3_ref)):
            own_small[9 + line : 10 + line, 0:thin] = ref[...].astype(F32).reshape(1, thin)
        x, core, z, y = places(2)
        _, _, sibling, beyond = peers_of(layers)
        others = [
            (x * 2 + core, (z ^ more) * 2 + (y ^ over)) for more in range(layers) for over in range(2) if more + over > 0
        ]
        greet(others + [sibling, beyond])
        for part in expand:
            part.start()
        small.start()
        project.start()

    def before():
        for join in joins:
            join.wait()
        for part in expand:
            part.forward()
        small.finish()
        blocks = [v_small[z, y] for z in range(layers) for y in range(2)]
        taps_ref[...] = jnp.concatenate([block[:, :share] for block in blocks], axis=1)
        norms_ref[...] = jnp.concatenate([block[8:, :thin] for block in blocks], axis=1)
        for part in expand:
            part.side()
        mixed.start()
        up.start()
        down.start()

    def middle_of_first(chunk):
        per = wide // CHUNK
        piece, place = chunk // per, chunk % per
        if place == 0:
            expand[piece].share()
            if piece == 1:
                project.forward()
            expand[piece].finish()
        weights[chunk] = v_expand[piece, :, :, :, place * CHUNK : (place + 1) * CHUNK].reshape(width, CHUNK)

    def at(number, *works):
        @pl.when(step == number)
        def _():
            for work in works:
                work()

    at(1, project.side, save_expand.start)
    at(2, project.finish, save_project.start, mixed.forward)
    at(3, mixed.side, up.forward)
    at(4, up.side)
    at(5, mixed.share, down.forward)
    at(6, down.side)
    at(7, up.share)

    conv_forward_body(
        step, before, middle_of_first,
        grid_ref, tokens_ref, late_tokens_ref, weights, v_project.reshape(hidden, width), norms_ref, taps_ref,
        field_ref, act_ref, pull_ref, projected_ref, first_ref, tokens_t_ref, keep_ref, frames, acts,
    )

    @pl.when(step == last)
    def _():
        for part in (mixed, up, down):
            part.finish()
        for part in expand + [small, project, mixed, up, down]:
            part.drain()
        save_expand.wait()
        save_project.wait()


def whole(shape):
    return pl.BlockSpec(shape, lambda *_: (0,) * len(shape), pipeline_mode=pl.Buffered(1))


def forward_specs(rows, width, hidden):
    images, chunks = rows // ROWS, hidden // CHUNK
    here = lambda i: jnp.minimum(i, images - 1)
    late = lambda i: jnp.maximum(i - 2, 0)
    by_image = pl.BlockSpec((ROWS, width), lambda i: (here(i), 0))
    by_late = pl.BlockSpec((ROWS, width), lambda i: (late(i), 0))
    by_chunk = pl.BlockSpec((2 * chunks, ROWS, 128), lambda i: (0, here(i), 0))
    turned = pl.BlockSpec((1, width, ROWS), lambda i: (here(i) // 2, 0, here(i) % 2))
    cells = pl.BlockSpec((ROWS, 128), lambda i: (here(i), 0))
    wide = jax.ShapeDtypeStruct((2 * chunks, rows, 128), BF16)
    tall = jax.ShapeDtypeStruct((rows, width), F32)
    return (
        [pl.BlockSpec(memory_space=pltpu.SMEM), by_image, by_late],
        [by_chunk, by_chunk, by_chunk, by_late, by_late, turned, cells],
        [
            wide, wide, wide, tall, tall,
            jax.ShapeDtypeStruct((images // 2, width, 2 * ROWS), BF16), jax.ShapeDtypeStruct((rows, 128), BF16),
        ],
        [
            pltpu.VMEM((2, 2, ROWS + 2 * GRID, 128), F32),
            pltpu.VMEM((2, 2 * chunks, ROWS, 128), BF16),
        ],
    )


def conv_forward(grid, tokens, w_expand, taps, w_project, norms):
    rows, width = tokens.shape
    in_specs, out_specs, out_shape, scratch = forward_specs(rows, width, taps.shape[1])
    return pl.pallas_call(
        conv_forward_kernel,
        grid=(rows // ROWS + 2,),
        in_specs=in_specs + [whole(w_expand.shape), whole(taps.shape), whole(w_project.shape), whole(norms.shape)],
        out_specs=out_specs,
        out_shape=out_shape,
        scratch_shapes=scratch,
        compiler_params=pltpu.CompilerParams(vmem_limit_bytes=VMEM_BYTES),
        name="conv_forward",
    )(grid, tokens, tokens, w_expand, taps, w_project, norms)


def gather_forward(grid, tokens, w_depth, vectors, w_expand, w_project, w_qkv, w_out, w_up, w_down, layers):
    rows, width = tokens.shape
    hidden = w_expand.shape[1]
    chunks = hidden // CHUNK
    in_specs, out_specs, out_shape, scratch = forward_specs(rows, width, hidden)
    anywhere = pl.BlockSpec(memory_space=pl.ANY)
    here = pl.BlockSpec(memory_space=pltpu.VMEM)
    span = -(-w_depth.shape[1] // 128) * 128
    mixed = (w_qkv.shape[0], w_qkv.shape[1] + w_out.shape[1])
    pieces = 3
    lead = (layers, 2)
    fulls = [(chunks, width, CHUNK)] + [lead + shape for shape in (w_project.shape, mixed, w_up.shape, w_down.shape)]
    copies = (pieces + 4) * (2 * layers + 3) + 2 * layers
    return pl.pallas_call(
        gather_forward_kernel,
        grid=(rows // ROWS + 2,),
        in_specs=in_specs + [here] * 7 + [anywhere] * 6,
        out_specs=out_specs + [whole((16, hidden)), whole((8, width))] + [anywhere] * 5,
        out_shape=out_shape
        + [jax.ShapeDtypeStruct((16, hidden), F32), jax.ShapeDtypeStruct((8, width), F32)]
        + [jax.ShapeDtypeStruct(full, BF16) for full in fulls],
        scratch_shapes=scratch
        + [
            pltpu.VMEM((chunks, width, CHUNK), BF16),
            pltpu.VMEM((pieces,) + lead + (w_expand.shape[0], hidden // pieces), BF16),
            pltpu.VMEM(fulls[1], BF16),
            pltpu.VMEM(lead + (16, span), F32),
            pltpu.VMEM((16, span), F32),
            pltpu.VMEM(mixed, BF16),
            pltpu.SemaphoreType.DMA((copies,)),
            pltpu.SemaphoreType.DMA((copies,)),
            pltpu.SemaphoreType.DMA((pieces + 9,)),
        ],
        compiler_params=pltpu.CompilerParams(
            vmem_limit_bytes=VMEM_BYTES, collective_id=0, has_side_effects=True
        ),
        name="gather_forward",
    )(grid, tokens, tokens, w_depth, *vectors, w_expand, w_project, w_qkv, w_out, w_up, w_down)


def heads_apart(pair):
    lane = lax.broadcasted_iota(jnp.int32, pair.shape, 1) // HDIM
    zero = jnp.zeros_like(pair)
    return jnp.concatenate((jnp.where(lane == 0, pair, zero), jnp.where(lane == 1, pair, zero)), axis=0)


def middle_kernel(*refs):
    take = iter(refs)
    grid_ref, first_ref, cotan_ref, projected_ref, norms_ref = [next(take) for _ in range(5)]
    mixed_hbm, up_hbm, down_hbm = [next(take) for _ in range(3)]
    layer_ref, d_first_ref, d_proj_ref, d_proj_t_ref, g_norm_ref, g_mixed_ref = [next(take) for _ in range(6)]
    g_up_ref, g_down_ref = next(take), next(take)
    w_qkv, w_out, w_up, w_down, load_sems = [next(take) for _ in range(5)]
    a_qkv, a_out, a_up, a_down = [next(take) for _ in range(4)]
    firsts, seconds, normeds, queries, keys, values, expo, inverses, attended, d_qkv = [next(take) for _ in range(10)]
    step = pl.program_id(0)
    pairs = firsts.shape[0]
    width = firsts.shape[2]
    chunks = w_up.shape[0]
    hidden = chunks * CHUNK
    blocks = width // 128
    cut = 3 * width

    loads = [
        pltpu.make_async_copy(mixed_hbm.at[:, :cut], w_qkv, load_sems.at[0]),
        pltpu.make_async_copy(mixed_hbm.at[:, cut:], w_out, load_sems.at[1]),
    ]
    loads.append(pltpu.make_async_copy(down_hbm, w_down, load_sems.at[2]))
    for chunk in range(chunks):
        source = up_hbm.at[:, chunk * CHUNK : (chunk + 1) * CHUNK]
        loads.append(pltpu.make_async_copy(source, w_up.at[chunk], load_sems.at[3 + chunk]))

    @pl.when(step == 0)
    def _():
        for load in loads:
            load.start()
        for ref in (a_qkv, a_out, a_up, a_down, g_norm_ref):
            ref[...] = jnp.zeros_like(ref)
        for load in loads:
            load.wait()

    def sizes(pair, side):
        return grid_ref[2 * pair + side, 0], grid_ref[2 * pair + side, 1]

    def valid_pair(pair):
        return jnp.concatenate([valid_cells(*sizes(pair, side), (ROWS, width)) for side in range(2)], axis=0)

    def forward(pair):
        first = first_ref[...]
        firsts[pair] = first
        unit, _ = normalized(first)
        normed = (unit * norms_ref[3:4, :] + norms_ref[4:5, :]).astype(BF16)
        normeds[pair] = normed
        packed = dot_nn(normed, w_qkv[...]).astype(BF16)
        for side in range(2):
            image = 2 * pair + side
            lines = slice(side * ROWS, (side + 1) * ROWS)
            bias = jnp.where(valid_cells(*sizes(pair, side), (ROWS, ROWS)), 0.0, -1e9)
            for block in range(blocks):
                columns = slice(block * 128, (block + 1) * 128)
                query = packed[lines, block * 128 : (block + 1) * 128] * jnp.asarray(HDIM**-0.5, BF16)
                key = packed[lines, width + block * 128 : width + (block + 1) * 128]
                value = packed[lines, 2 * width + block * 128 : 2 * width + (block + 1) * 128]
                queries[image, block], keys[image, block], values[image, block] = query, key, value
                scores = dot_nt(heads_apart(key), query)
                totals = []
                for head in range(2):
                    rows = slice(head * ROWS, (head + 1) * ROWS)
                    part = scores[rows] + bias
                    power = jnp.exp(part - jnp.max(part, axis=0, keepdims=True))
                    totals.append(1.0 / jnp.sum(power, axis=0, keepdims=True))
                    expo[image, block, rows] = power.astype(BF16)
                line = lax.broadcasted_iota(jnp.int32, (128, ROWS), 0) // HDIM
                inverse = jnp.where(line == 0, totals[0], totals[1])
                inverses[image, block] = inverse
                attended[image, columns] = (dot_tn(heads_apart(value), expo[image, block]) * inverse).astype(BF16)
            valid = valid_cells(*sizes(pair, side), (ROWS, width))
            seconds[pair, lines] = first[lines] + jnp.where(valid, dot_tn(attended[image], w_out[...]), 0.0)

    def feed(pair):
        valid = valid_pair(pair)
        second, cotan = seconds[pair], cotan_ref[...]
        unit, inverse = normalized(second)
        normed = (unit * norms_ref[5:6, :] + norms_ref[6:7, :]).astype(BF16)
        d_down = jnp.where(valid, cotan, jnp.zeros_like(cotan))
        normed_t, d_down_t = normed.T, d_down.T
        result = jnp.zeros((2 * ROWS, width), F32)
        d_normed = jnp.zeros((2 * ROWS, width), F32)
        for chunk in range(chunks):
            lines = w_down[chunk * CHUNK : (chunk + 1) * CHUNK, :]
            upper = dot_nn(normed, w_up[chunk])
            d_hidden = dot_nt(d_down, lines)
            square = upper * upper
            bent = jnp.tanh(upper * (0.7978845608028654 + (0.7978845608028654 * 0.044715) * square))
            gate = 0.5 * bent + 0.5
            hid = (upper * gate).astype(BF16)
            slope = gate + upper * (gate - gate * gate) * (
                2 * 0.7978845608028654 + (6 * 0.7978845608028654 * 0.044715) * square
            )
            d_upper = (d_hidden * slope).astype(BF16)
            result = result + dot_nn(hid, lines)
            a_down[chunk] += dot_nn(d_down_t, hid)
            a_up[chunk] += dot_nn(normed_t, d_upper)
            d_normed = d_normed + dot_nt(d_upper, w_up[chunk])
        layer_ref[...] = (second + jnp.where(valid, result, 0.0)).astype(BF16)
        g_norm_ref[0:8] += fold_rows(d_normed * unit)
        g_norm_ref[8:16] += fold_rows(d_normed)
        seconds[pair] = cotan.astype(F32) + norm_pull(d_normed, norms_ref[5:6, :], unit, inverse)

    def backward(pair):
        valid = valid_pair(pair)
        d_second = seconds[pair]
        d_out = jnp.where(valid, d_second, 0.0).astype(BF16)
        a_out[...] += dot_nn(both(attended[2 * pair], attended[2 * pair + 1]), d_out)
        for side in range(2):
            image = 2 * pair + side
            lines = slice(side * ROWS, (side + 1) * ROWS)
            line = lax.broadcasted_iota(jnp.int32, (128, ROWS), 0) // HDIM
            for block in range(blocks):
                columns = slice(block * 128, (block + 1) * 128)
                d_low = dot_nt(w_out[columns, :], d_out[lines]).astype(BF16).astype(F32)
                inverse = inverses[image, block]
                scaled = d_low * inverse
                low = scaled.astype(BF16)
                inner = scaled * attended[image, columns].astype(F32)
                d_probs = dot_nn(heads_apart(values[image, block]), low)
                query = heads_apart(queries[image, block])
                d_value = jnp.zeros((ROWS, 128), F32)
                d_key = jnp.zeros((ROWS, 128), F32)
                steps = []
                for head in range(2):
                    rows = slice(head * ROWS, (head + 1) * ROWS)
                    delta = jnp.sum(inner[head * HDIM : (head + 1) * HDIM], axis=0, keepdims=True)
                    power = expo[image, block, rows]
                    d_score = (power.astype(F32) * (d_probs[rows] - delta)).astype(BF16)
                    steps.append(d_score)
                    own = jnp.where(line == head, low, jnp.zeros_like(low))
                    d_value = d_value + dot_nt(power, own)
                    d_key = d_key + dot_nn(d_score, query[rows])
                d_query_t = dot_tn(heads_apart(keys[image, block]), jnp.concatenate(steps, axis=0)) * (HDIM**-0.5)
                d_qkv[lines, block * 128 : (block + 1) * 128] = d_query_t.astype(BF16).T
                d_qkv[lines, width + block * 128 : width + (block + 1) * 128] = d_key.astype(BF16)
                d_qkv[lines, 2 * width + block * 128 : 2 * width + (block + 1) * 128] = d_value.astype(BF16)
        a_qkv[...] += dot_nn(normeds[pair].T, d_qkv[...])
        d_normed = dot_nt(d_qkv[...], w_qkv[...])
        unit, inverse = normalized(firsts[pair])
        g_norm_ref[16:24] += fold_rows(d_normed * unit)
        g_norm_ref[24:32] += fold_rows(d_normed)
        d_first = d_second + norm_pull(d_normed, norms_ref[3:4, :], unit, inverse)
        d_first_ref[...] = d_first
        unit, inverse = normalized(projected_ref[...])
        grad = jnp.where(valid, d_first, 0.0)
        g_norm_ref[32:40] += fold_rows(grad * unit)
        g_norm_ref[40:48] += fold_rows(grad)
        low = norm_pull(grad, norms_ref[1:2, :], unit, inverse).astype(BF16)
        d_proj_ref[...] = low
        d_proj_t_ref[0] = low.T

    pl.when(step < pairs)(lambda: forward(step))
    pl.when((step >= pairs) & (step < 2 * pairs))(lambda: feed(step - pairs))
    pl.when(step >= 2 * pairs)(lambda: backward(step - 2 * pairs))

    @pl.when(step == 3 * pairs - 1)
    def _():
        g_mixed_ref[:, :cut] = a_qkv[...].astype(BF16)
        g_mixed_ref[:, cut:] = a_out[...].astype(BF16)
        to_lines(a_down, g_down_ref.reshape(1, 1, hidden, width))
        for chunk in range(chunks):
            g_up_ref[:, chunk * CHUNK : (chunk + 1) * CHUNK] = a_up[chunk].astype(BF16)


def to_lines(blocks, target):
    layers, sides, share = target.shape[:3]
    for chunk in range(blocks.shape[0]):
        lines = blocks[chunk].astype(BF16).T
        for f in range(layers * sides):
            low, high = max(f * share, chunk * CHUNK), min((f + 1) * share, (chunk + 1) * CHUNK)
            if low < high:
                target[f // sides, f % sides, low - f * share : high - f * share] = lines[
                    low - chunk * CHUNK : high - chunk * CHUNK
                ]


def middle(grid, first, cotangent, projected, w_mixed, w_up, w_down, norms):
    rows, width = first.shape
    pairs, blocks = rows // (2 * ROWS), width // 128
    images = 2 * pairs
    hidden = w_up.shape[1]
    chunks = hidden // CHUNK
    cut = 3 * width

    def phase(number):
        return pl.BlockSpec((2 * ROWS, width), lambda i: (jnp.clip(i - number * pairs, 0, pairs - 1), 0))

    turned = pl.BlockSpec((1, width, 2 * ROWS), lambda i: (jnp.clip(i - 2 * pairs, 0, pairs - 1), 0, 0))
    anywhere = pl.BlockSpec(memory_space=pl.ANY)
    full_up, full_down = (width, hidden), (hidden, width)
    scratch = [
        pltpu.VMEM((width, cut), BF16),
        pltpu.VMEM((width, width), BF16),
        pltpu.VMEM((chunks, width, CHUNK), BF16),
        pltpu.VMEM(full_down, BF16),
        pltpu.SemaphoreType.DMA((3 + chunks,)),
        pltpu.VMEM((width, cut), F32),
        pltpu.VMEM((width, width), F32),
        pltpu.VMEM((chunks, width, CHUNK), F32),
        pltpu.VMEM((chunks, width, CHUNK), F32),
        pltpu.VMEM((pairs, 2 * ROWS, width), F32),
        pltpu.VMEM((pairs, 2 * ROWS, width), F32),
        pltpu.VMEM((pairs, 2 * ROWS, width), BF16),
        pltpu.VMEM((images, blocks, ROWS, 128), BF16),
        pltpu.VMEM((images, blocks, ROWS, 128), BF16),
        pltpu.VMEM((images, blocks, ROWS, 128), BF16),
        pltpu.VMEM((images, blocks, 2 * ROWS, ROWS), BF16),
        pltpu.VMEM((images, blocks, 128, ROWS), F32),
        pltpu.VMEM((images, width, ROWS), BF16),
        pltpu.VMEM((2 * ROWS, cut), BF16),
    ]
    grads = [jax.ShapeDtypeStruct(full_up, BF16), jax.ShapeDtypeStruct(full_down, BF16)]
    return pl.pallas_call(
        middle_kernel,
        grid=(3 * pairs,),
        in_specs=[pl.BlockSpec(memory_space=pltpu.SMEM), phase(0), phase(1), phase(2), whole(norms.shape)] + [anywhere] * 3,
        out_specs=[phase(1), phase(2), phase(2), turned, whole((48, width)), whole((width, cut + width))]
        + [whole(grad.shape) for grad in grads],
        out_shape=[
            jax.ShapeDtypeStruct((rows, width), BF16),
            jax.ShapeDtypeStruct((rows, width), F32),
            jax.ShapeDtypeStruct((rows, width), BF16),
            jax.ShapeDtypeStruct((pairs, width, 2 * ROWS), BF16),
            jax.ShapeDtypeStruct((48, width), F32),
            jax.ShapeDtypeStruct((width, cut + width), BF16),
        ]
        + grads,
        scratch_shapes=scratch,
        compiler_params=pltpu.CompilerParams(vmem_limit_bytes=VMEM_BYTES),
        name="middle",
    )(grid, first, cotangent, projected, norms, w_mixed, w_up, w_down)


class Reduce:
    def __init__(self, terms, mine, result, cross, buffers, sems, base, fetch_sem=None):
        sends, receives = sems
        self.terms, self.mine, self.result, self.cross = terms, mine, result, cross
        self.layers = terms.shape[0]
        self.x, self.core, self.z, self.y = places(2)
        self.along_devices, across, sibling, beyond = peers_of(self.layers)
        buffers = list(buffers)
        every = (slice(None), slice(None))
        self.from_core, self.chip = buffers[:2]
        other = part_of(terms, every, 1 - self.core)
        self.inside = remote(other, self.from_core, sends, receives, base, sibling)
        self.fetch = None
        if mine is not None:
            self.fetch = pltpu.make_async_copy(part_of(terms, every, self.core), mine, fetch_sem)
        rest = buffers[2:]
        if cross:
            self.from_cross, self.wide = rest[:2]
            self.over_x = remote(part_of(self.chip, every, 1 - self.x), self.from_cross, sends, receives, base + 1, beyond)
            rest = rest[2:]
        else:
            self.wide = self.chip
        self.from_side, self.line, self.from_along, self.own, self.from_x, self.total = rest
        self.over = remote(self.wide.at[:, 1 - self.y], self.from_side, sends, receives, base + 2, across)
        self.along = [
            remote(self.line.at[self.z ^ (step + 1)], self.from_along.at[step], sends, receives, base + 3 + step, device)
            for step, device in enumerate(self.along_devices)
        ]
        base += 3 + self.layers - 1
        half = part_of(result, (), self.core)
        if cross:
            self.spot = part_of(half, (), self.x)
            self.beyond = remote(self.total, self.spot, sends, receives, base, beyond)
            self.back = remote(half, half, sends, receives, base + 1, sibling)
        else:
            self.spot = half
            self.beyond = remote(self.own, self.from_x, sends, receives, base, beyond)
            self.back = remote(self.total, half, sends, receives, base + 1, sibling)

    def start(self):
        self.inside.start()

    def add_core(self):
        if self.fetch is not None:
            self.fetch.wait()
        self.inside.wait_recv()
        for z in range(self.layers):
            for y in range(2):
                if self.mine is not None:
                    own = self.mine[z, y]
                else:
                    own = part_of(self.terms, (z, y), self.core)[...]
                self.chip[z, y] = own + self.from_core[z, y]
        (self.over_x if self.cross else self.over).start()

    def add_cross(self):
        self.over_x.wait_recv()
        for z in range(self.layers):
            for y in range(2):
                self.wide[z, y] = part_of(self.chip, (z, y), self.x)[...] + self.from_cross[z, y]
        self.over.start()

    def add_side(self):
        self.over.wait_recv()
        for z in range(self.layers):
            self.line[z] = self.wide[z, self.y] + self.from_side[z]
        for copy in self.along:
            copy.start()

    def add_line(self):
        mine = self.line[self.z].astype(F32)
        for step, copy in enumerate(self.along):
            copy.wait_recv()
            mine = mine + self.from_along[step].astype(F32)
        if self.cross:
            self.total[...] = mine
            self.spot[...] = mine
        else:
            self.own[...] = mine.astype(self.own.dtype)
        self.beyond.start()

    def add_x(self):
        self.beyond.wait_recv()
        if not self.cross:
            mine = self.own[...].astype(F32) + self.from_x[...].astype(F32)
            self.total[...] = mine
            self.spot[...] = mine
        self.back.start()

    def finish(self):
        self.back.wait_recv()
        copies = [self.inside, self.over, self.beyond, self.back] + self.along
        if self.cross:
            copies.append(self.over_x)
        for copy in copies:
            copy.wait_send()


def reduce_buffers(shape, dtype, cross):
    layers, sides = shape[:2]
    half = part_shape(shape[2:])
    last = part_shape(half) if cross else half
    buffers = [(layers, sides) + half] * 2
    if cross:
        buffers += [(layers, sides) + last] * 2
    buffers += [(layers,) + last] * 2 + [(layers - 1,) + last, last, last]
    return [pltpu.VMEM(buffer, dtype) for buffer in buffers] + [pltpu.VMEM(last, F32)]


def conv_backward_kernel(layers, *refs):
    quick = layers > 0
    take = iter(refs)
    tokens_t_hbm, keep_hbm, d_first_hbm, d_proj_hbm, d_proj_t_hbm = [next(take) for _ in range(5)]
    field_hbm, act_hbm, pull_hbm, expand_hbm, taps_ref, project_hbm = [next(take) for _ in range(6)]
    if quick:
        late_norm_ref = next(take)
        late = [next(take) for _ in range(3)]
    d_tokens_ref = next(take)
    if quick:
        results = [next(take) for _ in range(6)]
    else:
        g_expand_ref, g_project_ref, g_taps_ref = [next(take) for _ in range(3)]
    (d_image, field, act, pull, expand, project, load_sems) = [next(take) for _ in range(7)]
    (d_proj, d_proj_t, tokens_t, keep, taps_b, a_expand, a_project, a_taps) = [next(take) for _ in range(8)]
    frames = next(take)
    pairs, _, width = d_image.shape
    images = 2 * pairs
    chunks = field.shape[0] // 2
    hidden = chunks * CHUNK
    items = pairs * chunks
    per = pairs // 2

    if quick:
        stage_project, stage_small = next(take), next(take)
        stage_expand = [next(take) for _ in range(chunks)]
        mines = [next(take) for _ in range(3)]
        fetch_sems = next(take)
    loads = []
    for number, (source, target) in enumerate(
        (
            (d_proj_hbm, d_proj), (project_hbm, project), (d_proj_t_hbm, d_proj_t), (keep_hbm, keep),
            (tokens_t_hbm, tokens_t.at[0:pairs]), (d_first_hbm, d_image), (expand_hbm, expand),
        )
    ):
        loads.append(pltpu.make_async_copy(source, target, load_sems.at[number]))
    base = 7

    def stream(kind, chunk):
        source, target = ((act_hbm, act), (pull_hbm, pull), (field_hbm, field))[kind]
        two = pl.ds(2 * chunk, 2)
        return pltpu.make_async_copy(source.at[two], target.at[two], load_sems.at[base + kind * chunks + chunk])

    if quick:
        x, core, z, y = places(2)
        for index, (ref, mine) in enumerate(zip(late, mines)):
            pltpu.make_async_copy(part_of(ref, (slice(None), slice(None)), core), mine, fetch_sems.at[index]).start()
    for load in loads[:3]:
        load.start()
    for kind in range(3):
        stream(kind, 0).start()
    for load in loads[3:]:
        load.start()
    for chunk in range(1, chunks):
        for kind in range(3):
            stream(kind, chunk).start()

    plan = {}
    if quick:
        number = 0
        rest = list(take)
        sems = rest[-2:]
        rest = rest[:-2]
        span = 3 + layers + 1

        def reducer(terms, mine, result, cross, fetch_sem=None):
            nonlocal number, rest
            count = 10 if cross else 8
            made = Reduce(terms, mine, result, cross, rest[:count], sems, number * span, fetch_sem)
            rest = rest[count:]
            number += 1
            return made

        mixed = reducer(late[0], mines[0], results[3], True, fetch_sems.at[0])
        up = reducer(late[1], mines[1], results[4], False, fetch_sems.at[1])
        down = reducer(late[2], mines[2], results[5], True, fetch_sems.at[2])
        whole_project = reducer(stage_project, None, results[2], True)
        parts = [
            reducer(stage_expand[c], None, results[1].at[:, c * CHUNK : (c + 1) * CHUNK], False) for c in range(chunks)
        ]
        small = reducer(stage_small, None, results[0], False)
        along, across, sibling, beyond = peers_of(layers)
        greet(along + [across, sibling, beyond])
        for part in (up, down, mixed):
            part.inside.start()

        def send_project():
            to_lines(a_project, stage_project)
            whole_project.start()

        def send_part(chunk):
            stage_expand[chunk][...] = a_expand[chunk].astype(BF16).reshape(stage_expand[chunk].shape)
            parts[chunk].start()

        def at(segment, *works):
            plan.setdefault(segment, []).extend(works)

        at(1, up.add_core, down.add_core, mixed.add_core)
        at(3, lambda: send_part(0))
        at(4, parts[0].add_core)
        at(5, up.add_side, down.add_cross, lambda: send_part(1))
        at(6, send_project, parts[1].add_core, parts[0].add_side)
        at(7, down.add_side, whole_project.add_core, lambda: send_part(2), parts[1].add_side)
        at(8, mixed.add_cross, up.add_line, parts[2].add_core)
        at(9, parts[0].add_line, parts[1].add_line, lambda: send_part(3), parts[2].add_side)
        at(10, mixed.add_side, down.add_line, up.add_x, parts[3].add_core)
        at(
            11, whole_project.add_cross, lambda: send_part(4), parts[0].add_x, parts[1].add_x, parts[2].add_line,
            parts[3].add_side,
        )

    a_taps[...] = jnp.zeros_like(a_taps)
    a_expand[...] = jnp.zeros_like(a_expand)
    a_project[...] = jnp.zeros_like(a_project)
    frames[...] = jnp.zeros_like(frames)
    tokens_t[pairs] = jnp.zeros((width, 2 * ROWS), BF16)
    spread_taps(taps_ref, taps_b)
    for load in loads:
        load.wait()

    def item(t):
        t = jnp.clip(t, 0, items - 1)
        return t // pairs, t % pairs

    def step(t, lead, new=True, old=True):
        c2, p2 = item(t - 2)
        c1, p1 = item(t - 1)
        c0, p0 = item(t)
        spot = pl.ds(pl.multiple_of(p2 * 2 * ROWS, 2 * ROWS), 2 * ROWS)
        done = both(act[2 * c2, spot, :], act[2 * c2 + 1, spot, :])
        a_expand[c2] += dot_nn(tokens_t[jnp.where(t < 2, pairs, p2)], done)
        if lead:
            cp, pp = t // 2, 2 * (t % 2)
            total = a_project[cp]
            for more in range(2):
                rows = pl.ds(pl.multiple_of((pp + more) * 2 * ROWS, 2 * ROWS), 2 * ROWS)
                total = total + dot_nn(d_proj_t[pp + more], both(act[2 * cp, rows, :], act[2 * cp + 1, rows, :]))
            a_project[cp] = total
        block = 64
        rows = block // GRID
        for half in range(CHUNK // 128 if old else 0):
            lanes = slice(half * 128, (half + 1) * 128)
            taps = [taps_b[c1, k, :, lanes] for k in range(9)]
            totals = [jnp.zeros((8, 128), F32) for _ in range(9)]
            for side in range(2):
                for start in range(0, ROWS, block):
                    spot = pl.ds(pl.multiple_of((2 * p1 + side) * ROWS, ROWS) + start, block)
                    own = field[2 * c1 + half, spot, :].reshape(rows, GRID, 128)
                    lines = []
                    for a in range(3):
                        line = None
                        for b in range(3):
                            k = 3 * a + b
                            at = start + GRID * (2 - a)
                            near = frames[side, b, half, at : at + block].reshape(rows, GRID, 128)
                            term = taps[k] * near
                            line = term if line is None else line + term
                            prod = near * own
                            quad = ((prod[0] + prod[1]) + (prod[2] + prod[3])).astype(F32)
                            totals[k] = totals[k] + (quad[:8] + quad[8:])
                        lines.append(line)
                    grad = (lines[0] + lines[1] + lines[2]).reshape(block, 128)
                    act[2 * c1 + half, spot, :] = grad * keep[2 * p1 + side, start : start + block, :]
            for k in range(9):
                a_taps[c1, 8 * k : 8 * k + 8, lanes] += totals[k]
        if not new:
            return
        d_act = dot_nt(d_proj[p0], project[c0])
        for half in range(CHUNK // 128):
            lanes = slice(half * 128, (half + 1) * 128)
            for side in range(2):
                spot = pl.ds(pl.multiple_of((2 * p0 + side) * ROWS, ROWS), ROWS)
                d_conv = d_act[side * ROWS : (side + 1) * ROWS, lanes] * pull[2 * c0 + half, spot, :].astype(F32)
                frames[side, 0, half, GRID : GRID + ROWS] = move_cells(d_conv, -1).astype(BF16)
                frames[side, 1, half, GRID : GRID + ROWS] = d_conv.astype(BF16)
                frames[side, 2, half, GRID : GRID + ROWS] = move_cells(d_conv, 1).astype(BF16)

    def segment(s, lead):
        for key in plan:
            @pl.when(s == key)
            def _(works=plan[key]):
                for work in works:
                    work()

        if lead:
            stream(0, s).wait()

        @pl.when(s % 2 == 0)
        def _():
            stream(1, s // 2).wait()
            stream(2, s // 2).wait()

        @pl.loop(0, per)
        def _(turn):
            step(s * per + turn, lead)

    middle_segment = chunks
    pl.loop(0, middle_segment)(lambda s: segment(s, True))
    pl.loop(middle_segment, 2 * chunks)(lambda s: segment(s, False))
    step(items, False, new=False)
    step(items + 1, False, new=False, old=False)

    def finish_pair(pair):
        spot = slice(2 * pair * ROWS, 2 * (pair + 1) * ROWS)
        left = jnp.concatenate([act[line, spot, :] for line in range(2 * chunks)], axis=1)
        right = jnp.concatenate([expand[chunk] for chunk in range(chunks)], axis=1)
        d_tokens_ref[spot, :] = (d_image[pair] + dot_nt(left, right)).astype(BF16)


    if not quick:
        for chunk in range(chunks):
            g_expand_ref[:, chunk * CHUNK : (chunk + 1) * CHUNK] = a_expand[chunk].astype(BF16)
            g_project_ref[chunk * CHUNK : (chunk + 1) * CHUNK, :] = a_project[chunk].astype(BF16).T
            g_taps_ref[:, chunk * CHUNK : (chunk + 1) * CHUNK] = a_taps[chunk]
        for pair in range(pairs):
            finish_pair(pair)
        return

    send_part(chunks - 1)
    lines = []
    for k in range(9):
        line = jnp.concatenate([a_taps[c, 8 * k : 8 * k + 8, :] for c in range(chunks)], axis=1)
        lines.append(jnp.sum(line, axis=0, keepdims=True))
    depth = jnp.concatenate(lines, axis=0)
    vectors = [late_norm_ref[8 * k : 8 * k + 8] for k in (4, 5, 2, 3, 0, 1)]
    vectors = jnp.concatenate([jnp.sum(vector, axis=0, keepdims=True) for vector in vectors], axis=0)
    share, thin = hidden // (2 * layers), width // (2 * layers)
    stage_small[...] = jnp.zeros_like(stage_small)
    for f in range(2 * layers):
        stage_small[f // 2, f % 2, 0:9, 0:share] = depth[:, f * share : (f + 1) * share]
        stage_small[f // 2, f % 2, 9:15, 0:thin] = vectors[:, f * thin : (f + 1) * thin]
    small.start()
    finish_pair(0)
    parts[4].add_core()
    parts[5].add_core()
    small.add_core()
    whole_project.add_side()
    down.add_x()
    parts[2].add_x()
    parts[3].add_line()
    finish_pair(1)
    parts[4].add_side()
    parts[5].add_side()
    small.add_side()
    mixed.add_line()
    finish_pair(2)
    parts[3].add_x()
    parts[4].add_line()
    parts[5].add_line()
    small.add_line()
    whole_project.add_line()
    finish_pair(3)
    mixed.add_x()
    parts[4].add_x()
    parts[5].add_x()
    small.add_x()
    whole_project.add_x()
    for part in [up, down, mixed, whole_project, small] + parts:
        part.finish()


def conv_backward(tokens_t, keep, d_first, d_proj, d_proj_t, field, act, pull, w_expand, taps, w_project, late=None):
    rows, width = d_first.shape
    chunks = w_expand.shape[0]
    hidden = chunks * CHUNK
    images = rows // ROWS
    anywhere = pl.BlockSpec(memory_space=pl.ANY)
    here = pl.BlockSpec(memory_space=pltpu.VMEM)
    pairs = images // 2
    by_pair = (pairs, 2 * ROWS, width)
    wide = (2 * chunks, rows, 128)
    scratch = [
        pltpu.VMEM(by_pair, F32),
        pltpu.VMEM(wide, BF16),
        pltpu.VMEM(wide, BF16),
        pltpu.VMEM(wide, BF16),
        pltpu.VMEM((chunks, width, CHUNK), BF16),
        pltpu.VMEM((chunks, CHUNK, width), BF16),
        pltpu.SemaphoreType.DMA((7 + chunks * 3,)),
        pltpu.VMEM((pairs, 2 * ROWS, width), BF16),
        pltpu.VMEM((pairs, width, 2 * ROWS), BF16),
        pltpu.VMEM((pairs + 1, width, 2 * ROWS), BF16),
        pltpu.VMEM((images, ROWS, 128), BF16),
        pltpu.VMEM((chunks, 9, GRID, CHUNK), BF16),
        pltpu.VMEM((chunks, width, CHUNK), F32),
        pltpu.VMEM((chunks, width, CHUNK), F32),
        pltpu.VMEM((chunks, 72, CHUNK), F32),
    ]
    scratch += [pltpu.VMEM((2, 3, 2, ROWS + 2 * GRID, 128), BF16)]
    operands = [
        tokens_t, keep.reshape(images, ROWS, 128), d_first.reshape(by_pair), d_proj.reshape(by_pair), d_proj_t,
        field, act, pull, w_expand, taps, w_project.reshape(chunks, CHUNK, width),
    ]
    in_specs = [anywhere] * 9 + [here, anywhere]
    d_tokens = jax.ShapeDtypeStruct((rows, width), BF16)
    if late is None:
        layers, params = 0, {}
        out_shape = [
            d_tokens,
            jax.ShapeDtypeStruct((width, hidden), BF16),
            jax.ShapeDtypeStruct(w_project.shape, BF16),
            jax.ShapeDtypeStruct((72, hidden), F32),
        ]
    else:
        g_norm, g_mixed, g_up, g_down = late
        layers = g_up.shape[0]
        params = dict(collective_id=1, has_side_effects=True)
        operands += [g_norm, g_mixed, g_up, g_down]
        in_specs += [here] + [anywhere] * 3
        span = -(-hidden // (2 * layers) // 128) * 128
        b_small, b_expand, b_project = (16, span), (width // (2 * layers), hidden), (hidden // (2 * layers), width)
        blocks = (b_small, b_expand, b_project, g_mixed.shape[2:], g_up.shape[2:], g_down.shape[2:])
        out_shape = [d_tokens] + [jax.ShapeDtypeStruct(block, F32) for block in blocks]
        lead = (layers, 2)
        piece = (b_expand[0], CHUNK)
        scratch += [pltpu.VMEM(lead + b_project, BF16), pltpu.VMEM(lead + b_small, F32)]
        scratch += [pltpu.VMEM(lead + piece, BF16)] * chunks
        scratch += [pltpu.VMEM(lead + part_shape(block), BF16) for block in blocks[3:]]
        scratch += [pltpu.SemaphoreType.DMA((3,))]
        for shape, dtype, cross in (
            [(blocks[3], BF16, True), (blocks[4], BF16, False), (blocks[5], BF16, True), (blocks[2], BF16, True)]
            + [(piece, BF16, False)] * chunks
            + [(b_small, F32, False)]
        ):
            scratch += reduce_buffers(lead + shape, dtype, cross)
        copies = (5 + chunks) * (4 + layers)
        scratch += [pltpu.SemaphoreType.DMA((copies,))] * 2
    return pl.pallas_call(
        functools.partial(conv_backward_kernel, layers),
        in_specs=in_specs,
        out_specs=[here] * len(out_shape),
        out_shape=out_shape,
        scratch_shapes=scratch,
        compiler_params=pltpu.CompilerParams(vmem_limit_bytes=VMEM_BYTES, **params),
        name="conv_backward",
    )(*operands)


def deliver_kernel(*refs):
    tokens_in, small_ref, *blocks = refs[:7]
    tokens_out, depth_ref, *rest = refs[7:]
    vectors, outs = rest[:6], rest[6:]
    expand, project, mixed, up, down = blocks
    cut = outs[2].shape[1]
    pairs = [(tokens_in, tokens_out), (expand, outs[0]), (project, outs[1])]
    pairs += [(mixed.at[:, :cut], outs[2]), (mixed.at[:, cut:], outs[3]), (up, outs[4]), (down, outs[5])]
    for source, target in pairs:
        target[...] = source[...]
    depth_ref[...] = small_ref[0 : depth_ref.shape[0], 0 : depth_ref.shape[1]]
    for line, ref in enumerate(vectors):
        ref[...] = small_ref[9 + line, 0 : ref.shape[0]]


def deliver(d_tokens, small, s_expand, s_project, s_mixed, s_up, s_down, share, thin):
    rows, width = s_mixed.shape[0], s_project.shape[1]
    here = pl.BlockSpec(memory_space=pltpu.VMEM)
    blocks = [s_expand.shape, s_project.shape, (rows, 3 * width), (rows, width), s_up.shape, s_down.shape]
    return pl.pallas_call(
        deliver_kernel,
        in_specs=[here] * 7,
        out_specs=[here] * 14,
        out_shape=[jax.ShapeDtypeStruct(d_tokens.shape, BF16), jax.ShapeDtypeStruct((9, share), F32)]
        + [jax.ShapeDtypeStruct((thin,), F32)] * 6
        + [jax.ShapeDtypeStruct(block, F32) for block in blocks],
        compiler_params=pltpu.CompilerParams(vmem_limit_bytes=VMEM_BYTES),
        name="deliver",
    )(d_tokens, small, s_expand, s_project, s_mixed, s_up, s_down)


def reduce_plain(terms):
    results = []
    for term in terms:
        share = lax.psum_scatter(term, "fsdp", scatter_dimension=0, tiled=False)
        results.append(lax.psum(share, "dp").astype(F32))
    return results


def local(
    fsdp, quick,
    tokens, grid, w_expand, w_depth, w_project, gain_conv, bias_conv, gain_attend, bias_attend,
    w_qkv, w_out, gain_mlp, bias_mlp, w_up, w_down, cotangent,
):
    slots, rows, width = tokens.shape
    hidden = w_expand.shape[1]
    share, thin = w_depth.shape[1], gain_conv.shape[0]
    span = -(-share // 128) * 128
    vectors = (gain_conv, bias_conv, gain_attend, bias_attend, gain_mlp, bias_mlp)
    flat, cotan = tokens.reshape(slots * rows, width), cotangent.reshape(slots * rows, width)
    if quick:
        field, act, pull, projected, first, tokens_t, keep, taps, norms, *fulls = gather_forward(
            grid, flat, w_depth, vectors, w_expand, w_project, w_qkv, w_out, w_up, w_down, fsdp // 2
        )
        f_expand = fulls[0]
        f_project, f_mixed, f_up, f_down = [full.reshape(-1, full.shape[3]) for full in fulls[1:]]
    else:
        mixed = jnp.concatenate((w_qkv, w_out), axis=1)
        f_expand, f_project, f_mixed, f_up, f_down = [
            lax.all_gather(shard, "fsdp", axis=0, tiled=True) for shard in (w_expand, w_project, mixed, w_up, w_down)
        ]
        f_expand = f_expand.reshape(width, hidden // CHUNK, CHUNK).transpose(1, 0, 2)
        taps = jnp.pad(lax.all_gather(w_depth, "fsdp", axis=1, tiled=True).astype(F32), ((0, 7), (0, 0)))
        lines = lax.all_gather(jnp.stack(vectors), "fsdp", axis=1, tiled=True).astype(F32)
        norms = jnp.pad(lines, ((1, 1), (0, 0)))
        field, act, pull, projected, first, tokens_t, keep = conv_forward(
            grid, flat, f_expand, taps, f_project, norms
        )
    layer_out, d_first, d_proj, d_proj_t, g_norm, g_mixed, g_up, g_down = middle(
        grid, first, cotan, projected, f_mixed, f_up, f_down, norms
    )
    inputs = (tokens_t, keep, d_first, d_proj, d_proj_t, field, act, pull, f_expand, taps, f_project)
    if quick:
        late = [term.reshape((fsdp // 2, 2, -1, term.shape[1])) for term in (g_mixed, g_up, g_down)]
        d_tokens, small, s_expand, s_project, s_mixed, s_up, s_down = conv_backward(*inputs, late=[g_norm] + late)
    else:
        d_tokens, g_expand, g_project, g_taps = conv_backward(*inputs)
        g_taps = jnp.sum(g_taps.reshape(9, 8, fsdp, share), axis=1)
        g_norm = jnp.concatenate((g_norm[32:], g_norm[16:32], g_norm[:16]), axis=0)
        g_norm = jnp.sum(g_norm.reshape(6, 8, fsdp, thin), axis=1)
        g_small = jnp.concatenate(
            (
                jnp.pad(g_taps, ((0, 0), (0, 0), (0, span - share))),
                jnp.pad(g_norm, ((0, 1), (0, 0), (0, span - thin))),
            ),
            axis=0,
        ).transpose(1, 0, 2)
        terms = [g_small] + [
            term.reshape((fsdp, -1, term.shape[1])) for term in (g_expand, g_project, g_mixed, g_up, g_down)
        ]
        small, s_expand, s_project, s_mixed, s_up, s_down = reduce_plain(terms)
    d_tokens, depth, *rest = deliver(d_tokens, small, s_expand, s_project, s_mixed, s_up, s_down, share, thin)
    vectors, (s_expand, s_project, s_qkv, s_out, s_up, s_down) = rest[:6], rest[6:]
    return (
        layer_out.reshape(tokens.shape),
        d_tokens.reshape(tokens.shape),
        s_expand,
        depth,
        s_project,
        *vectors[:4],
        s_qkv,
        s_out,
        *vectors[4:],
        s_up,
        s_down,
    )


def solution(mesh):
    fsdp, dp = mesh.shape["fsdp"], mesh.shape["dp"]
    quick = fsdp == 8 and dp == 4
    images, wide, tall, vector = P(("dp", "fsdp"), None, None), P("fsdp", None), P(None, "fsdp"), P("fsdp")
    in_specs = (
        images, P(("dp", "fsdp"), None), wide, tall, wide, vector, vector, vector, vector,
        wide, wide, vector, vector, wide, wide, images,
    )
    out_specs = (
        images, images, wide, tall, wide, vector, vector, vector, vector,
        wide, wide, vector, vector, wide, wide,
    )
    return jax.shard_map(
        functools.partial(local, fsdp, quick), mesh=mesh, in_specs=in_specs, out_specs=out_specs, check_vma=False
    )
```

```python
import functools

import jax
import jax.numpy as jnp
from jax import lax
from jax.experimental import pallas as pl
from jax.experimental.pallas import tpu as pltpu
from jax.sharding import PartitionSpec as P

HDIM = 64
GRID = 16
ROWS = GRID * GRID
CHUNK = 256
EPSILON = 1e-05
VMEM_BYTES = 62 * 1024 * 1024
F32 = jnp.float32
BF16 = jnp.bfloat16


def dot_nn(left, right):
    return jnp.dot(left, right, preferred_element_type=F32)


def dot_nt(left, right):
    return lax.dot_general(left, right, (((1,), (1,)), ((), ())), preferred_element_type=F32)


def dot_tn(left, right):
    return lax.dot_general(left, right, (((0,), (0,)), ((), ())), preferred_element_type=F32)


def valid_cells(high, wide, shape):
    place = lax.broadcasted_iota(jnp.int32, shape, 0)
    return (place // GRID < high) & (place % GRID < wide)


def normalized(values):
    center = jnp.mean(values, axis=-1, keepdims=True)
    shifted = values - center
    spread = jnp.mean(shifted * shifted, axis=-1, keepdims=True)
    inverse = lax.rsqrt(spread + EPSILON)
    return shifted * inverse, inverse


def norm_pull(grad, gain, unit, inverse):
    scaled = grad * gain
    mean_plain = jnp.mean(scaled, axis=-1, keepdims=True)
    mean_unit = jnp.mean(scaled * unit, axis=-1, keepdims=True)
    return (scaled - mean_plain - unit * mean_unit) * inverse


def both(left, right):
    return jnp.concatenate((left, right), axis=1)


def fold_rows(values):
    rows, width = values.shape
    return jnp.sum(values.reshape(rows // 8, 8, width), axis=0)


def move_cells(values, step):
    rows, width = values.shape
    parts = values.reshape(rows // GRID, 2, 8, width)
    turned = pltpu.roll(parts, step % 8, axis=2)
    first, last = turned[:, 0:1], turned[:, 1:2]
    line = lax.broadcasted_iota(jnp.int32, first.shape, 2)
    if step == 1:
        edge = line == 0
        moved = jnp.concatenate((jnp.where(edge, 0.0, first), jnp.where(edge, first, last)), axis=1)
    else:
        edge = line == 7
        moved = jnp.concatenate((jnp.where(edge, last, first), jnp.where(edge, 0.0, last)), axis=1)
    return moved.reshape(rows, width)


MESH = pl.DeviceIdType.MESH


def places(sides):
    dp, fsdp = lax.axis_index("dp"), lax.axis_index("fsdp")
    return dp // 2, dp % 2, fsdp // sides, fsdp % sides


def part_of(ref, lead, index, count=2):
    rows, columns = ref.shape[-2:]
    if columns > rows * 4:
        size = columns // count
        return ref.at[lead + (slice(None), pl.ds(pl.multiple_of(index * size, size), size))]
    size = rows // count
    return ref.at[lead + (pl.ds(pl.multiple_of(index * size, size), size), slice(None))]


def part_shape(shape, count=2):
    rows, columns = shape
    return (rows, columns // count) if columns > rows * 4 else (rows // count, columns)


def remote(source, target, sends, receives, index, device):
    return pltpu.make_async_remote_copy(
        src_ref=source,
        dst_ref=target,
        send_sem=sends.at[index],
        recv_sem=receives.at[index],
        device_id=device,
        device_id_type=MESH,
    )


def greet(devices):
    barrier = pltpu.get_barrier_semaphore()
    for device in devices:
        pl.semaphore_signal(barrier, inc=1, device_id=device, device_id_type=MESH)
    pl.semaphore_wait(barrier, len(devices))


def peers_of(layers):
    x, core, z, y = places(2)
    dp, fsdp = x * 2 + core, z * 2 + y
    along = [(dp, (z ^ step) * 2 + y) for step in range(1, layers)]
    return along, (dp, z * 2 + 1 - y), (x * 2 + 1 - core, fsdp), ((1 - x) * 2 + core, fsdp)


class Gather:
    def __init__(self, shard, full, cross, sems, number):
        sends, receives, locals_ = sems
        self.full, self.cross, self.layers = full, cross, full.shape[0]
        self.x, self.core, self.z, self.y = places(2)
        along, across, sibling, beyond = peers_of(self.layers)
        base = number * (2 * self.layers + 3)
        own = self.piece(shard, ())
        spot = self.piece(full, (self.z, self.y))
        self.local = pltpu.make_async_copy(own, spot, locals_.at[number])
        self.along = [remote(own, spot, sends, receives, base + step, device) for step, device in enumerate(along)]
        base += self.layers - 1
        self.over = []
        for step in range(self.layers):
            target = self.piece(full, (self.z ^ step, self.y))
            self.over.append(remote(own if step == 0 else target, target, sends, receives, base + step, across))
        base += self.layers
        self.beyond, self.inside = [], []
        for step, side in enumerate((self.y, 1 - self.y)):
            half = part_of(full, (slice(None), side), self.core)
            self.inside.append(remote(half, half, sends, receives, base + step, sibling))
            if cross:
                target = self.piece(full, (slice(None), side))
                self.beyond.append(remote(target, target, sends, receives, base + 2 + step, beyond))

    def piece(self, ref, lead):
        half = part_of(ref, lead, self.core)
        return part_of(half, (slice(None),) * (len(half.shape) - 2), self.x) if self.cross else half

    def start(self):
        for copy in self.along:
            copy.start()
        self.over[0].start()
        self.local.start()

    def forward(self):
        for step, copy in enumerate(self.along):
            copy.wait_recv()
            self.over[step + 1].start()
        self.local.wait()
        (self.beyond if self.cross else self.inside)[0].start()

    def side(self):
        for copy in self.over:
            copy.wait_recv()
        (self.beyond if self.cross else self.inside)[1].start()

    def share(self):
        for copy, after in zip(self.beyond, self.inside):
            copy.wait_recv()
            after.start()

    def finish(self):
        for copy in self.inside:
            copy.wait_recv()

    def drain(self):
        for copy in self.along + self.over + self.beyond + self.inside:
            copy.wait_send()


class Spread:
    def __init__(self, block, full, sems, base):
        sends, receives, local = sems
        layers = full.shape[0]
        x, core, z, y = places(2)
        spot = full.at[z, y]
        self.local = pltpu.make_async_copy(block, spot, local)
        self.copies = [
            remote(block, spot, sends, receives, base + 2 * up + over - 1, (x * 2 + core, (z ^ up) * 2 + (y ^ over)))
            for up in range(layers)
            for over in range(2)
            if up + over > 0
        ]

    def start(self):
        for copy in self.copies:
            copy.start()
        self.local.start()

    def finish(self):
        for copy in self.copies:
            copy.wait_recv()
        self.local.wait()

    def drain(self):
        for copy in self.copies:
            copy.wait_send()


def spread_taps(taps_ref, taps_b):
    for chunk in range(taps_b.shape[0]):
        for k in range(9):
            line = taps_ref[k : k + 1, chunk * CHUNK : (chunk + 1) * CHUNK]
            taps_b[chunk, k] = jnp.broadcast_to(line, (GRID, CHUNK)).astype(BF16)


def conv_chunk(chunk, kept, weights, taps_ref, frames, field_ref, act_ref, pull_ref, acts, slot):
    expanded = dot_nn(kept, weights)
    block = 64
    for half in range(CHUNK // 128):
        lanes = slice(half * 128, (half + 1) * 128)
        field_ref[chunk * 2 + half] = expanded[:, lanes].astype(BF16)
        frames[chunk % 2, half, GRID : GRID + ROWS] = expanded[:, lanes]
        whole = slice(chunk * CHUNK + half * 128, chunk * CHUNK + (half + 1) * 128)
        taps = [taps_ref[k : k + 1, whole] for k in range(9)]
        for start in range(0, ROWS, block):
            near = [frames[chunk % 2, half, start + GRID * a : start + GRID * a + block] for a in range(3)]
            sums = [sum(taps[3 * a + b] * near[a] for a in range(3)) for b in range(3)]
            conv = sums[1] + move_cells(sums[0], 1) + move_cells(sums[2], -1)
            gate = 0.5 * jnp.tanh(0.5 * conv) + 0.5
            act = conv * gate
            low = act.astype(BF16)
            act_ref[chunk * 2 + half, start : start + block] = low
            acts[slot, chunk * 2 + half, start : start + block] = low
            pull_ref[chunk * 2 + half, start : start + block] = (gate + act * (1.0 - gate)).astype(BF16)


def project_chunks(chunk, acts, slot, project):
    left = jnp.concatenate([acts[slot, 2 * chunk + part] for part in range(4)], axis=1)
    return dot_nn(left, project[chunk * CHUNK : (chunk + 2) * CHUNK, :])


def end_forward(projected, tokens, valid, norms_ref, projected_ref, first_ref):
    projected_ref[...] = projected
    unit, _ = normalized(projected)
    shift = unit * norms_ref[1:2, :] + norms_ref[2:3, :]
    first_ref[...] = tokens.astype(F32) + jnp.where(valid, shift, 0.0)


def conv_forward_body(
    step, before, middle_of_first, grid_ref, tokens_ref, late_tokens_ref, weights, project, norms_ref, taps_ref,
    field_ref, act_ref, pull_ref, projected_ref, first_ref, tokens_t_ref, keep_ref, frames, acts,
):
    width = tokens_ref.shape[1]
    chunks = weights.shape[0]
    images = pl.num_programs(0) - 2
    slot = lax.rem(step, 2)

    def start_image():
        valid = valid_cells(grid_ref[0, step], grid_ref[1, step], (ROWS, width))
        tokens = tokens_ref[...]
        tokens_t_ref[0] = tokens.T
        keep_ref[...] = jnp.where(valid[:, :128], 1.0, 0.0).astype(BF16)
        return jnp.where(valid, tokens, jnp.zeros_like(tokens))

    def convolve(chunk, kept):
        conv_chunk(chunk, kept, weights[chunk], taps_ref, frames, field_ref, act_ref, pull_ref, acts, slot)

    def end_image(projected):
        high, wide = grid_ref[0, step - 2], grid_ref[1, step - 2]
        valid = valid_cells(high, wide, (ROWS, width))
        end_forward(projected, late_tokens_ref[...], valid, norms_ref, projected_ref, first_ref)

    @pl.when(step == 0)
    def _():
        before()
        frames[...] = jnp.zeros_like(frames)
        kept = start_image()
        for chunk in range(chunks):
            middle_of_first(chunk)
            convolve(chunk, kept)

    @pl.when(step == 1)
    def _():
        kept = start_image()
        for chunk in range(chunks):
            convolve(chunk, kept)

    @pl.when((step > 1) & (step < images))
    def _():
        kept = start_image()
        projected = jnp.zeros((ROWS, width), F32)
        for chunk in range(0, chunks, 2):
            projected = projected + project_chunks(chunk, acts, slot, project)
            convolve(chunk, kept)
            convolve(chunk + 1, kept)
        end_image(projected)

    @pl.when(step >= images)
    def _():
        projected = jnp.zeros((ROWS, width), F32)
        for chunk in range(0, chunks, 2):
            projected = projected + project_chunks(chunk, acts, slot, project)
        end_image(projected)


def conv_forward_kernel(
    grid_ref, tokens_ref, late_tokens_ref, weights, taps_ref, project_ref, norms_ref,
    field_ref, act_ref, pull_ref, projected_ref, first_ref, tokens_t_ref, keep_ref, frames, acts,
):
    conv_forward_body(
        pl.program_id(0), lambda: None, lambda chunk: None,
        grid_ref, tokens_ref, late_tokens_ref, weights, project_ref, norms_ref, taps_ref,
        field_ref, act_ref, pull_ref, projected_ref, first_ref, tokens_t_ref, keep_ref, frames, acts,
    )


def gather_forward_kernel(
    grid_ref, tokens_ref, late_tokens_ref, depth_ref, gain1_ref, bias1_ref, gain2_ref, bias2_ref, gain3_ref, bias3_ref,
    s_expand, s_project, s_qkv, s_out, s_up, s_down,
    field_ref, act_ref, pull_ref, projected_ref, first_ref, tokens_t_ref, keep_ref,
    taps_ref, norms_ref, f_expand, f_project, f_mixed, f_up, f_down,
    frames, acts, weights, v_expand, v_project, v_small, own_small, own_mixed, sends, receives, locals_,
):
    step = pl.program_id(0)
    last = pl.num_programs(0) - 1
    sems = (sends, receives, locals_)
    layers = v_small.shape[0]
    hidden, width = taps_ref.shape[1], tokens_ref.shape[1]
    wide = v_expand.shape[-1]
    pieces = v_expand.shape[0]
    expand = [
        Gather(s_expand.at[:, piece * wide : (piece + 1) * wide], v_expand.at[piece], True, sems, piece)
        for piece in range(pieces)
    ]
    project = Gather(s_project, v_project, False, sems, pieces)
    mixed = Gather(own_mixed, f_mixed, True, sems, pieces + 1)
    up = Gather(s_up, f_up, True, sems, pieces + 2)
    down = Gather(s_down, f_down, False, sems, pieces + 3)
    count = pieces + 4
    small = Spread(own_small, v_small, (sends, receives, locals_.at[count]), count * (2 * layers + 3))
    share, thin = depth_ref.shape[1], gain1_ref.shape[0]
    cut = s_qkv.shape[1]
    joins = [
        pltpu.make_async_copy(s_qkv, own_mixed.at[:, :cut], locals_.at[count + 1]),
        pltpu.make_async_copy(s_out, own_mixed.at[:, cut:], locals_.at[count + 2]),
    ]
    save_expand = pltpu.make_async_copy(weights, f_expand, locals_.at[count + 3])
    save_project = pltpu.make_async_copy(v_project, f_project, locals_.at[count + 4])

    @pl.when(step == 0)
    def _():
        for join in joins:
            join.start()
        own_small[...] = jnp.zeros_like(own_small)
        own_small[0:9, 0:share] = depth_ref[...].astype(F32)
        for line, ref in enumerate((gain1_ref, bias1_ref, gain2_ref, bias2_ref, gain3_ref, bias3_ref)):
            own_small[9 + line : 10 + line, 0:thin] = ref[...].astype(F32).reshape(1, thin)
        x, core, z, y = places(2)
        _, _, sibling, beyond = peers_of(layers)
        others = [
            (x * 2 + core, (z ^ more) * 2 + (y ^ over)) for more in range(layers) for over in range(2) if more + over > 0
        ]
        greet(others + [sibling, beyond])
        for part in expand:
            part.start()
        small.start()
        project.start()

    def before():
        for join in joins:
            join.wait()
        for part in expand:
            part.forward()
        small.finish()
        blocks = [v_small[z, y] for z in range(layers) for y in range(2)]
        taps_ref[...] = jnp.concatenate([block[:, :share] for block in blocks], axis=1)
        norms_ref[...] = jnp.concatenate([block[8:, :thin] for block in blocks], axis=1)
        for part in expand:
            part.side()
        mixed.start()
        up.start()
        down.start()

    def middle_of_first(chunk):
        per = wide // CHUNK
        piece, place = chunk // per, chunk % per
        if place == 0:
            expand[piece].share()
            if piece == 1:
                project.forward()
            expand[piece].finish()
        weights[chunk] = v_expand[piece, :, :, :, place * CHUNK : (place + 1) * CHUNK].reshape(width, CHUNK)

    def at(number, *works):
        @pl.when(step == number)
        def _():
            for work in works:
                work()

    at(1, project.side, save_expand.start)
    at(2, project.finish, save_project.start, mixed.forward)
    at(3, mixed.side, up.forward)
    at(4, up.side)
    at(5, mixed.share, down.forward)
    at(6, down.side)
    at(7, up.share)

    conv_forward_body(
        step, before, middle_of_first,
        grid_ref, tokens_ref, late_tokens_ref, weights, v_project.reshape(hidden, width), norms_ref, taps_ref,
        field_ref, act_ref, pull_ref, projected_ref, first_ref, tokens_t_ref, keep_ref, frames, acts,
    )

    @pl.when(step == last)
    def _():
        for part in (mixed, up, down):
            part.finish()
        for part in expand + [small, project, mixed, up, down]:
            part.drain()
        save_expand.wait()
        save_project.wait()


def whole(shape):
    return pl.BlockSpec(shape, lambda *_: (0,) * len(shape), pipeline_mode=pl.Buffered(1))


def forward_specs(rows, width, hidden):
    images, chunks = rows // ROWS, hidden // CHUNK
    here = lambda i: jnp.minimum(i, images - 1)
    late = lambda i: jnp.maximum(i - 2, 0)
    by_image = pl.BlockSpec((ROWS, width), lambda i: (here(i), 0))
    by_late = pl.BlockSpec((ROWS, width), lambda i: (late(i), 0))
    by_chunk = pl.BlockSpec((2 * chunks, ROWS, 128), lambda i: (0, here(i), 0))
    turned = pl.BlockSpec((1, width, ROWS), lambda i: (here(i) // 2, 0, here(i) % 2))
    cells = pl.BlockSpec((ROWS, 128), lambda i: (here(i), 0))
    wide = jax.ShapeDtypeStruct((2 * chunks, rows, 128), BF16)
    tall = jax.ShapeDtypeStruct((rows, width), F32)
    return (
        [pl.BlockSpec(memory_space=pltpu.SMEM), by_image, by_late],
        [by_chunk, by_chunk, by_chunk, by_late, by_late, turned, cells],
        [
            wide, wide, wide, tall, tall,
            jax.ShapeDtypeStruct((images // 2, width, 2 * ROWS), BF16), jax.ShapeDtypeStruct((rows, 128), BF16),
        ],
        [
            pltpu.VMEM((2, 2, ROWS + 2 * GRID, 128), F32),
            pltpu.VMEM((2, 2 * chunks, ROWS, 128), BF16),
        ],
    )


def conv_forward(grid, tokens, w_expand, taps, w_project, norms):
    rows, width = tokens.shape
    in_specs, out_specs, out_shape, scratch = forward_specs(rows, width, taps.shape[1])
    return pl.pallas_call(
        conv_forward_kernel,
        grid=(rows // ROWS + 2,),
        in_specs=in_specs + [whole(w_expand.shape), whole(taps.shape), whole(w_project.shape), whole(norms.shape)],
        out_specs=out_specs,
        out_shape=out_shape,
        scratch_shapes=scratch,
        compiler_params=pltpu.CompilerParams(vmem_limit_bytes=VMEM_BYTES),
        name="conv_forward",
    )(grid, tokens, tokens, w_expand, taps, w_project, norms)


def gather_forward(grid, tokens, w_depth, vectors, w_expand, w_project, w_qkv, w_out, w_up, w_down, layers):
    rows, width = tokens.shape
    hidden = w_expand.shape[1]
    chunks = hidden // CHUNK
    in_specs, out_specs, out_shape, scratch = forward_specs(rows, width, hidden)
    anywhere = pl.BlockSpec(memory_space=pl.ANY)
    here = pl.BlockSpec(memory_space=pltpu.VMEM)
    span = -(-w_depth.shape[1] // 128) * 128
    mixed = (w_qkv.shape[0], w_qkv.shape[1] + w_out.shape[1])
    pieces = 3
    lead = (layers, 2)
    fulls = [(chunks, width, CHUNK)] + [lead + shape for shape in (w_project.shape, mixed, w_up.shape, w_down.shape)]
    copies = (pieces + 4) * (2 * layers + 3) + 2 * layers
    return pl.pallas_call(
        gather_forward_kernel,
        grid=(rows // ROWS + 2,),
        in_specs=in_specs + [here] * 7 + [anywhere] * 6,
        out_specs=out_specs + [whole((16, hidden)), whole((8, width))] + [anywhere] * 5,
        out_shape=out_shape
        + [jax.ShapeDtypeStruct((16, hidden), F32), jax.ShapeDtypeStruct((8, width), F32)]
        + [jax.ShapeDtypeStruct(full, BF16) for full in fulls],
        scratch_shapes=scratch
        + [
            pltpu.VMEM((chunks, width, CHUNK), BF16),
            pltpu.VMEM((pieces,) + lead + (w_expand.shape[0], hidden // pieces), BF16),
            pltpu.VMEM(fulls[1], BF16),
            pltpu.VMEM(lead + (16, span), F32),
            pltpu.VMEM((16, span), F32),
            pltpu.VMEM(mixed, BF16),
            pltpu.SemaphoreType.DMA((copies,)),
            pltpu.SemaphoreType.DMA((copies,)),
            pltpu.SemaphoreType.DMA((pieces + 9,)),
        ],
        compiler_params=pltpu.CompilerParams(
            vmem_limit_bytes=VMEM_BYTES, collective_id=0, has_side_effects=True
        ),
        name="gather_forward",
    )(grid, tokens, tokens, w_depth, *vectors, w_expand, w_project, w_qkv, w_out, w_up, w_down)


def heads_apart(pair):
    lane = lax.broadcasted_iota(jnp.int32, pair.shape, 1) // HDIM
    zero = jnp.zeros_like(pair)
    return jnp.concatenate((jnp.where(lane == 0, pair, zero), jnp.where(lane == 1, pair, zero)), axis=0)


def middle_kernel(*refs):
    take = iter(refs)
    grid_ref, first_ref, cotan_ref, projected_ref, norms_ref = [next(take) for _ in range(5)]
    mixed_hbm, up_hbm, down_hbm = [next(take) for _ in range(3)]
    layer_ref, d_first_ref, d_proj_ref, d_proj_t_ref, g_norm_ref, g_mixed_ref = [next(take) for _ in range(6)]
    g_up_ref, g_down_ref = next(take), next(take)
    w_qkv, w_out, w_up, w_down, load_sems = [next(take) for _ in range(5)]
    a_qkv, a_out, a_up, a_down = [next(take) for _ in range(4)]
    firsts, seconds, normeds, queries, keys, values, expo, inverses, attended, d_qkv = [next(take) for _ in range(10)]
    step = pl.program_id(0)
    pairs = firsts.shape[0]
    width = firsts.shape[2]
    chunks = w_up.shape[0]
    hidden = chunks * CHUNK
    blocks = width // 128
    cut = 3 * width

    loads = [
        pltpu.make_async_copy(mixed_hbm.at[:, :cut], w_qkv, load_sems.at[0]),
        pltpu.make_async_copy(mixed_hbm.at[:, cut:], w_out, load_sems.at[1]),
    ]
    loads.append(pltpu.make_async_copy(down_hbm, w_down, load_sems.at[2]))
    for chunk in range(chunks):
        source = up_hbm.at[:, chunk * CHUNK : (chunk + 1) * CHUNK]
        loads.append(pltpu.make_async_copy(source, w_up.at[chunk], load_sems.at[3 + chunk]))

    @pl.when(step == 0)
    def _():
        for load in loads:
            load.start()
        for ref in (a_qkv, a_out, a_up, a_down, g_norm_ref):
            ref[...] = jnp.zeros_like(ref)
        for load in loads:
            load.wait()

    def sizes(pair, side):
        return grid_ref[0, 2 * pair + side], grid_ref[1, 2 * pair + side]

    def valid_pair(pair):
        return jnp.concatenate([valid_cells(*sizes(pair, side), (ROWS, width)) for side in range(2)], axis=0)

    def forward(pair):
        first = first_ref[...]
        firsts[pair] = first
        unit, _ = normalized(first)
        normed = (unit * norms_ref[3:4, :] + norms_ref[4:5, :]).astype(BF16)
        normeds[pair] = normed
        packed = dot_nn(normed, w_qkv[...]).astype(BF16)
        line = lax.broadcasted_iota(jnp.int32, (128, ROWS), 0) // HDIM
        biases = [jnp.where(valid_cells(*sizes(pair, side), (ROWS, ROWS)), 0.0, -1e9) for side in range(2)]
        units = [(side, block) for side in range(2) for block in range(blocks)]

        def score(side, block):
            image, lines = 2 * pair + side, slice(side * ROWS, (side + 1) * ROWS)
            query = packed[lines, block * 128 : (block + 1) * 128] * jnp.asarray(HDIM**-0.5, BF16)
            key = packed[lines, width + block * 128 : width + (block + 1) * 128]
            value = packed[lines, 2 * width + block * 128 : 2 * width + (block + 1) * 128]
            queries[image, block], keys[image, block], values[image, block] = query, key, value
            return dot_nt(heads_apart(key), query), heads_apart(value)

        ahead = score(*units[0])
        for number, (side, block) in enumerate(units):
            scores, value = ahead
            if number + 1 < len(units):
                ahead = score(*units[number + 1])
            image = 2 * pair + side
            columns = slice(block * 128, (block + 1) * 128)
            totals, powers = [], []
            for head in range(2):
                rows = slice(head * ROWS, (head + 1) * ROWS)
                part = scores[rows] + biases[side]
                power = jnp.exp(part - jnp.max(part, axis=0, keepdims=True))
                totals.append(1.0 / jnp.sum(power, axis=0, keepdims=True))
                powers.append(power.astype(BF16))
                expo[image, block, rows] = powers[-1]
            inverse = jnp.where(line == 0, totals[0], totals[1])
            inverses[image, block] = inverse
            attended[image, columns] = (dot_tn(value, jnp.concatenate(powers, axis=0)) * inverse).astype(BF16)
            if block == blocks - 1:
                lines = slice(side * ROWS, (side + 1) * ROWS)
                valid = valid_cells(*sizes(pair, side), (ROWS, width))
                seconds[pair, lines] = first[lines] + jnp.where(valid, dot_tn(attended[image], w_out[...]), 0.0)

    def feed(pair):
        valid = valid_pair(pair)
        second, cotan = seconds[pair], cotan_ref[...]
        unit, inverse = normalized(second)
        normed = (unit * norms_ref[5:6, :] + norms_ref[6:7, :]).astype(BF16)
        d_down = jnp.where(valid, cotan, jnp.zeros_like(cotan))
        normed_t, d_down_t = normed.T, d_down.T
        result = jnp.zeros((2 * ROWS, width), F32)
        d_normed = jnp.zeros((2 * ROWS, width), F32)

        def begin(chunk):
            lines = w_down[chunk * CHUNK : (chunk + 1) * CHUNK, :]
            return dot_nn(normed, w_up[chunk]), dot_nt(d_down, lines), lines

        ahead = begin(0)
        for chunk in range(chunks):
            upper, d_hidden, lines = ahead
            if chunk + 1 < chunks:
                ahead = begin(chunk + 1)
            square = upper * upper
            bent = jnp.tanh(upper * (0.7978845608028654 + (0.7978845608028654 * 0.044715) * square))
            gate = 0.5 * bent + 0.5
            hid = (upper * gate).astype(BF16)
            slope = gate + upper * (gate - gate * gate) * (
                2 * 0.7978845608028654 + (6 * 0.7978845608028654 * 0.044715) * square
            )
            d_upper = (d_hidden * slope).astype(BF16)
            result = result + dot_nn(hid, lines)
            a_down[chunk] += dot_nn(d_down_t, hid)
            a_up[chunk] += dot_nn(normed_t, d_upper)
            d_normed = d_normed + dot_nt(d_upper, w_up[chunk])
        layer_ref[...] = (second + jnp.where(valid, result, 0.0)).astype(BF16)
        g_norm_ref[0:8] += fold_rows(d_normed * unit)
        g_norm_ref[8:16] += fold_rows(d_normed)
        seconds[pair] = cotan.astype(F32) + norm_pull(d_normed, norms_ref[5:6, :], unit, inverse)

    def backward(pair):
        valid = valid_pair(pair)
        d_second = seconds[pair]
        d_out = jnp.where(valid, d_second, 0.0).astype(BF16)
        a_out[...] += dot_nn(both(attended[2 * pair], attended[2 * pair + 1]), d_out)
        line = lax.broadcasted_iota(jnp.int32, (128, ROWS), 0) // HDIM
        units = [(side, block) for side in range(2) for block in range(blocks)]

        def probe(side, block):
            image, lines = 2 * pair + side, slice(side * ROWS, (side + 1) * ROWS)
            columns = slice(block * 128, (block + 1) * 128)
            d_low = dot_nt(w_out[columns, :], d_out[lines]).astype(BF16).astype(F32)
            scaled = d_low * inverses[image, block]
            low = scaled.astype(BF16)
            inner = scaled * attended[image, columns].astype(F32)
            return low, inner, dot_nn(heads_apart(values[image, block]), low)

        ahead = probe(*units[0])
        for number, (side, block) in enumerate(units):
            low, inner, d_probs = ahead
            if number + 1 < len(units):
                ahead = probe(*units[number + 1])
            image, lines = 2 * pair + side, slice(side * ROWS, (side + 1) * ROWS)
            query = heads_apart(queries[image, block])
            d_value = jnp.zeros((ROWS, 128), F32)
            d_key = jnp.zeros((ROWS, 128), F32)
            steps = []
            for head in range(2):
                rows = slice(head * ROWS, (head + 1) * ROWS)
                delta = jnp.sum(inner[head * HDIM : (head + 1) * HDIM], axis=0, keepdims=True)
                power = expo[image, block, rows]
                d_score = (power.astype(F32) * (d_probs[rows] - delta)).astype(BF16)
                steps.append(d_score)
                own = jnp.where(line == head, low, jnp.zeros_like(low))
                d_value = d_value + dot_nt(power, own)
                d_key = d_key + dot_nn(d_score, query[rows])
            d_query_t = dot_tn(heads_apart(keys[image, block]), jnp.concatenate(steps, axis=0)) * (HDIM**-0.5)
            d_qkv[lines, block * 128 : (block + 1) * 128] = d_query_t.astype(BF16).T
            d_qkv[lines, width + block * 128 : width + (block + 1) * 128] = d_key.astype(BF16)
            d_qkv[lines, 2 * width + block * 128 : 2 * width + (block + 1) * 128] = d_value.astype(BF16)
        a_qkv[...] += dot_nn(normeds[pair].T, d_qkv[...])
        d_normed = dot_nt(d_qkv[...], w_qkv[...])
        unit, inverse = normalized(firsts[pair])
        g_norm_ref[16:24] += fold_rows(d_normed * unit)
        g_norm_ref[24:32] += fold_rows(d_normed)
        d_first = d_second + norm_pull(d_normed, norms_ref[3:4, :], unit, inverse)
        d_first_ref[...] = d_first
        unit, inverse = normalized(projected_ref[...])
        grad = jnp.where(valid, d_first, 0.0)
        g_norm_ref[32:40] += fold_rows(grad * unit)
        g_norm_ref[40:48] += fold_rows(grad)
        low = norm_pull(grad, norms_ref[1:2, :], unit, inverse).astype(BF16)
        d_proj_ref[...] = low
        d_proj_t_ref[0] = low.T

    pl.when(step < pairs)(lambda: forward(step))
    pl.when((step >= pairs) & (step < 2 * pairs))(lambda: feed(step - pairs))
    pl.when(step >= 2 * pairs)(lambda: backward(step - 2 * pairs))

    @pl.when(step == 3 * pairs - 1)
    def _():
        g_mixed_ref[:, :cut] = a_qkv[...].astype(BF16)
        g_mixed_ref[:, cut:] = a_out[...].astype(BF16)
        to_lines(a_down, g_down_ref.reshape(1, 1, hidden, width))
        for chunk in range(chunks):
            g_up_ref[:, chunk * CHUNK : (chunk + 1) * CHUNK] = a_up[chunk].astype(BF16)


def to_lines(blocks, target):
    layers, sides, share = target.shape[:3]
    for chunk in range(blocks.shape[0]):
        lines = blocks[chunk].astype(BF16).T
        for f in range(layers * sides):
            low, high = max(f * share, chunk * CHUNK), min((f + 1) * share, (chunk + 1) * CHUNK)
            if low < high:
                target[f // sides, f % sides, low - f * share : high - f * share] = lines[
                    low - chunk * CHUNK : high - chunk * CHUNK
                ]


def middle(grid, first, cotangent, projected, w_mixed, w_up, w_down, norms):
    rows, width = first.shape
    pairs, blocks = rows // (2 * ROWS), width // 128
    images = 2 * pairs
    hidden = w_up.shape[1]
    chunks = hidden // CHUNK
    cut = 3 * width

    def phase(number):
        return pl.BlockSpec((2 * ROWS, width), lambda i: (jnp.clip(i - number * pairs, 0, pairs - 1), 0))

    turned = pl.BlockSpec((1, width, 2 * ROWS), lambda i: (jnp.clip(i - 2 * pairs, 0, pairs - 1), 0, 0))
    anywhere = pl.BlockSpec(memory_space=pl.ANY)
    full_up, full_down = (width, hidden), (hidden, width)
    scratch = [
        pltpu.VMEM((width, cut), BF16),
        pltpu.VMEM((width, width), BF16),
        pltpu.VMEM((chunks, width, CHUNK), BF16),
        pltpu.VMEM(full_down, BF16),
        pltpu.SemaphoreType.DMA((3 + chunks,)),
        pltpu.VMEM((width, cut), F32),
        pltpu.VMEM((width, width), F32),
        pltpu.VMEM((chunks, width, CHUNK), F32),
        pltpu.VMEM((chunks, width, CHUNK), F32),
        pltpu.VMEM((pairs, 2 * ROWS, width), F32),
        pltpu.VMEM((pairs, 2 * ROWS, width), F32),
        pltpu.VMEM((pairs, 2 * ROWS, width), BF16),
        pltpu.VMEM((images, blocks, ROWS, 128), BF16),
        pltpu.VMEM((images, blocks, ROWS, 128), BF16),
        pltpu.VMEM((images, blocks, ROWS, 128), BF16),
        pltpu.VMEM((images, blocks, 2 * ROWS, ROWS), BF16),
        pltpu.VMEM((images, blocks, 128, ROWS), F32),
        pltpu.VMEM((images, width, ROWS), BF16),
        pltpu.VMEM((2 * ROWS, cut), BF16),
    ]
    grads = [jax.ShapeDtypeStruct(full_up, BF16), jax.ShapeDtypeStruct(full_down, BF16)]
    return pl.pallas_call(
        middle_kernel,
        grid=(3 * pairs,),
        in_specs=[pl.BlockSpec(memory_space=pltpu.SMEM), phase(0), phase(1), phase(2), whole(norms.shape)] + [anywhere] * 3,
        out_specs=[phase(1), phase(2), phase(2), turned, whole((48, width)), whole((width, cut + width))]
        + [whole(grad.shape) for grad in grads],
        out_shape=[
            jax.ShapeDtypeStruct((rows, width), BF16),
            jax.ShapeDtypeStruct((rows, width), F32),
            jax.ShapeDtypeStruct((rows, width), BF16),
            jax.ShapeDtypeStruct((pairs, width, 2 * ROWS), BF16),
            jax.ShapeDtypeStruct((48, width), F32),
            jax.ShapeDtypeStruct((width, cut + width), BF16),
        ]
        + grads,
        scratch_shapes=scratch,
        compiler_params=pltpu.CompilerParams(vmem_limit_bytes=VMEM_BYTES),
        name="middle",
    )(grid, first, cotangent, projected, norms, w_mixed, w_up, w_down)


class Reduce:
    def __init__(self, terms, mine, result, cross, buffers, sems, base, fetch_sem=None):
        sends, receives = sems
        self.terms, self.mine, self.result, self.cross = terms, mine, result, cross
        self.layers = terms.shape[0]
        self.x, self.core, self.z, self.y = places(2)
        self.along_devices, across, sibling, beyond = peers_of(self.layers)
        buffers = list(buffers)
        every = (slice(None), slice(None))
        self.from_core, self.chip = buffers[:2]
        other = part_of(terms, every, 1 - self.core)
        self.inside = remote(other, self.from_core, sends, receives, base, sibling)
        self.fetch = None
        if mine is not None:
            self.fetch = pltpu.make_async_copy(part_of(terms, every, self.core), mine, fetch_sem)
        rest = buffers[2:]
        if cross:
            self.from_cross, self.wide = rest[:2]
            self.over_x = remote(part_of(self.chip, every, 1 - self.x), self.from_cross, sends, receives, base + 1, beyond)
            rest = rest[2:]
        else:
            self.wide = self.chip
        self.from_side, self.line, self.from_along, self.own, self.from_x, self.total = rest
        self.over = remote(self.wide.at[:, 1 - self.y], self.from_side, sends, receives, base + 2, across)
        self.along = [
            remote(self.line.at[self.z ^ (step + 1)], self.from_along.at[step], sends, receives, base + 3 + step, device)
            for step, device in enumerate(self.along_devices)
        ]
        base += 3 + self.layers - 1
        half = part_of(result, (), self.core)
        if cross:
            self.spot = part_of(half, (), self.x)
            self.beyond = remote(self.total, self.spot, sends, receives, base, beyond)
            self.back = remote(half, half, sends, receives, base + 1, sibling)
        else:
            self.spot = half
            self.beyond = remote(self.own, self.from_x, sends, receives, base, beyond)
            self.back = remote(self.total, half, sends, receives, base + 1, sibling)

    def start(self):
        self.inside.start()

    def add_core(self):
        if self.fetch is not None:
            self.fetch.wait()
        self.inside.wait_recv()
        for z in range(self.layers):
            for y in range(2):
                if self.mine is not None:
                    own = self.mine[z, y]
                else:
                    own = part_of(self.terms, (z, y), self.core)[...]
                self.chip[z, y] = own + self.from_core[z, y]
        (self.over_x if self.cross else self.over).start()

    def add_cross(self):
        self.over_x.wait_recv()
        for z in range(self.layers):
            for y in range(2):
                self.wide[z, y] = part_of(self.chip, (z, y), self.x)[...] + self.from_cross[z, y]
        self.over.start()

    def add_side(self):
        self.over.wait_recv()
        for z in range(self.layers):
            self.line[z] = self.wide[z, self.y] + self.from_side[z]
        for copy in self.along:
            copy.start()

    def add_line(self):
        mine = self.line[self.z].astype(F32)
        for step, copy in enumerate(self.along):
            copy.wait_recv()
            mine = mine + self.from_along[step].astype(F32)
        if self.cross:
            self.total[...] = mine
            self.spot[...] = mine
        else:
            self.own[...] = mine.astype(self.own.dtype)
        self.beyond.start()

    def add_x(self):
        self.beyond.wait_recv()
        if not self.cross:
            mine = self.own[...].astype(F32) + self.from_x[...].astype(F32)
            self.total[...] = mine
            self.spot[...] = mine
        self.back.start()

    def finish(self):
        self.back.wait_recv()
        copies = [self.inside, self.over, self.beyond, self.back] + self.along
        if self.cross:
            copies.append(self.over_x)
        for copy in copies:
            copy.wait_send()


def reduce_buffers(shape, dtype, cross):
    layers, sides = shape[:2]
    half = part_shape(shape[2:])
    last = part_shape(half) if cross else half
    buffers = [(layers, sides) + half] * 2
    if cross:
        buffers += [(layers, sides) + last] * 2
    buffers += [(layers,) + last] * 2 + [(layers - 1,) + last, last, last]
    return [pltpu.VMEM(buffer, dtype) for buffer in buffers] + [pltpu.VMEM(last, F32)]


def conv_backward_kernel(layers, *refs):
    quick = layers > 0
    take = iter(refs)
    tokens_t_hbm, keep_hbm, d_first_hbm, d_proj_hbm, d_proj_t_hbm = [next(take) for _ in range(5)]
    field_hbm, act_hbm, pull_hbm, expand_hbm, taps_ref, project_hbm = [next(take) for _ in range(6)]
    if quick:
        late_norm_ref = next(take)
        late = [next(take) for _ in range(3)]
    d_tokens_ref = next(take)
    if quick:
        results = [next(take) for _ in range(6)]
    else:
        g_expand_ref, g_project_ref, g_taps_ref = [next(take) for _ in range(3)]
    (d_image, field, act, pull, expand, project, load_sems) = [next(take) for _ in range(7)]
    (d_proj, d_proj_t, tokens_t, keep, taps_b, a_expand, a_project, a_taps) = [next(take) for _ in range(8)]
    frames = next(take)
    pairs, _, width = d_image.shape
    images = 2 * pairs
    chunks = field.shape[0] // 2
    hidden = chunks * CHUNK
    items = pairs * chunks
    per = pairs // 2

    if quick:
        stage_project, stage_small = next(take), next(take)
        stage_expand = [next(take) for _ in range(chunks)]
        mines = [next(take) for _ in range(3)]
        fetch_sems = next(take)
    loads = []
    for number, (source, target) in enumerate(
        (
            (d_proj_hbm, d_proj), (project_hbm, project), (d_proj_t_hbm, d_proj_t), (keep_hbm, keep),
            (tokens_t_hbm, tokens_t.at[0:pairs]), (d_first_hbm, d_image), (expand_hbm, expand),
        )
    ):
        loads.append(pltpu.make_async_copy(source, target, load_sems.at[number]))
    base = 7

    def stream(kind, chunk):
        source, target = ((act_hbm, act), (pull_hbm, pull), (field_hbm, field))[kind]
        two = pl.ds(2 * chunk, 2)
        return pltpu.make_async_copy(source.at[two], target.at[two], load_sems.at[base + kind * chunks + chunk])

    if quick:
        x, core, z, y = places(2)
        for index, (ref, mine) in enumerate(zip(late, mines)):
            pltpu.make_async_copy(part_of(ref, (slice(None), slice(None)), core), mine, fetch_sems.at[index]).start()
    for load in loads[:3]:
        load.start()
    for kind in range(3):
        stream(kind, 0).start()
    stream(0, 1).start()
    for load in loads[3:]:
        load.start()

    plan = {}
    if quick:
        number = 0
        rest = list(take)
        sems = rest[-2:]
        rest = rest[:-2]
        span = 3 + layers + 1

        def reducer(terms, mine, result, cross, fetch_sem=None):
            nonlocal number, rest
            count = 10 if cross else 8
            made = Reduce(terms, mine, result, cross, rest[:count], sems, number * span, fetch_sem)
            rest = rest[count:]
            number += 1
            return made

        mixed = reducer(late[0], mines[0], results[3], True, fetch_sems.at[0])
        up = reducer(late[1], mines[1], results[4], False, fetch_sems.at[1])
        down = reducer(late[2], mines[2], results[5], True, fetch_sems.at[2])
        whole_project = reducer(stage_project, None, results[2], True)
        parts = [
            reducer(stage_expand[c], None, results[1].at[:, c * CHUNK : (c + 1) * CHUNK], False) for c in range(chunks)
        ]
        small = reducer(stage_small, None, results[0], False)
        along, across, sibling, beyond = peers_of(layers)
        greet(along + [across, sibling, beyond])
        for part in (up, down, mixed):
            part.inside.start()

        def send_project():
            to_lines(a_project, stage_project)
            whole_project.start()

        def send_part(chunk):
            stage_expand[chunk][...] = a_expand[chunk].astype(BF16).reshape(stage_expand[chunk].shape)
            parts[chunk].start()

        def at(segment, *works):
            plan.setdefault(segment, []).extend(works)

        at(1, up.add_core, down.add_core, mixed.add_core)
        at(3, lambda: send_part(0))
        at(4, parts[0].add_core)
        at(5, up.add_side, down.add_cross, lambda: send_part(1))
        at(6, send_project, parts[1].add_core, parts[0].add_side)
        at(7, down.add_side, whole_project.add_core, lambda: send_part(2), parts[1].add_side)
        at(8, mixed.add_cross, up.add_line, parts[2].add_core)
        at(9, parts[0].add_line, parts[1].add_line, lambda: send_part(3), parts[2].add_side)
        at(10, mixed.add_side, down.add_line, up.add_x, parts[3].add_core)
        at(
            11, whole_project.add_cross, lambda: send_part(4), parts[0].add_x, parts[1].add_x, parts[2].add_line,
            parts[3].add_side,
        )

    a_taps[...] = jnp.zeros_like(a_taps)
    a_expand[...] = jnp.zeros_like(a_expand)
    a_project[...] = jnp.zeros_like(a_project)
    frames[...] = jnp.zeros_like(frames)
    tokens_t[pairs] = jnp.zeros((width, 2 * ROWS), BF16)
    spread_taps(taps_ref, taps_b)
    for load in loads:
        load.wait()

    def item(t):
        t = jnp.clip(t, 0, items - 1)
        return t // pairs, t % pairs

    def step(t, lead, new=True, old=True):
        c2, p2 = item(t - 2)
        c1, p1 = item(t - 1)
        c0, p0 = item(t)
        spot = pl.ds(pl.multiple_of(p2 * 2 * ROWS, 2 * ROWS), 2 * ROWS)
        done = both(act[2 * c2, spot, :], act[2 * c2 + 1, spot, :])
        a_expand[c2] += dot_nn(tokens_t[jnp.where(t < 2, pairs, p2)], done)
        if lead:
            cp, pp = t // 2, 2 * (t % 2)
            total = a_project[cp]
            for more in range(2):
                rows = pl.ds(pl.multiple_of((pp + more) * 2 * ROWS, 2 * ROWS), 2 * ROWS)
                total = total + dot_nn(d_proj_t[pp + more], both(act[2 * cp, rows, :], act[2 * cp + 1, rows, :]))
            a_project[cp] = total
        block = 64
        rows = block // GRID
        for half in range(CHUNK // 128 if old else 0):
            lanes = slice(half * 128, (half + 1) * 128)
            taps = [taps_b[c1, k, :, lanes] for k in range(9)]
            totals = [jnp.zeros((8, 128), F32) for _ in range(9)]
            for side in range(2):
                for start in range(0, ROWS, block):
                    spot = pl.ds(pl.multiple_of((2 * p1 + side) * ROWS, ROWS) + start, block)
                    own = field[2 * c1 + half, spot, :].reshape(rows, GRID, 128)
                    lines = []
                    for a in range(3):
                        line = None
                        for b in range(3):
                            k = 3 * a + b
                            at = start + GRID * (2 - a)
                            near = frames[side, b, half, at : at + block].reshape(rows, GRID, 128)
                            term = taps[k] * near
                            line = term if line is None else line + term
                            prod = near * own
                            quad = ((prod[0] + prod[1]) + (prod[2] + prod[3])).astype(F32)
                            totals[k] = totals[k] + (quad[:8] + quad[8:])
                        lines.append(line)
                    grad = (lines[0] + lines[1] + lines[2]).reshape(block, 128)
                    act[2 * c1 + half, spot, :] = grad * keep[2 * p1 + side, start : start + block, :]
            for k in range(9):
                a_taps[c1, 8 * k : 8 * k + 8, lanes] += totals[k]
        if not new:
            return
        d_act = dot_nt(d_proj[p0], project[c0])
        for half in range(CHUNK // 128):
            lanes = slice(half * 128, (half + 1) * 128)
            for side in range(2):
                spot = pl.ds(pl.multiple_of((2 * p0 + side) * ROWS, ROWS), ROWS)
                d_conv = d_act[side * ROWS : (side + 1) * ROWS, lanes] * pull[2 * c0 + half, spot, :].astype(F32)
                frames[side, 0, half, GRID : GRID + ROWS] = move_cells(d_conv, -1).astype(BF16)
                frames[side, 1, half, GRID : GRID + ROWS] = d_conv.astype(BF16)
                frames[side, 2, half, GRID : GRID + ROWS] = move_cells(d_conv, 1).astype(BF16)

    def segment(s, lead):
        for key in plan:
            @pl.when(s == key)
            def _(works=plan[key]):
                for work in works:
                    work()

        if lead:
            stream(0, s).wait()

            @pl.when(s < chunks - 2)
            def _():
                stream(0, s + 2).start()

        @pl.when(s % 2 == 0)
        def _():
            stream(1, s // 2).wait()
            stream(2, s // 2).wait()

            @pl.when(s // 2 < chunks - 1)
            def _():
                stream(1, s // 2 + 1).start()
                stream(2, s // 2 + 1).start()

        @pl.loop(0, per)
        def _(turn):
            step(s * per + turn, lead)

    middle_segment = chunks
    pl.loop(0, middle_segment)(lambda s: segment(s, True))
    pl.loop(middle_segment, 2 * chunks)(lambda s: segment(s, False))
    step(items, False, new=False)
    step(items + 1, False, new=False, old=False)

    def finish_pair(pair):
        spot = slice(2 * pair * ROWS, 2 * (pair + 1) * ROWS)
        left = jnp.concatenate([act[line, spot, :] for line in range(2 * chunks)], axis=1)
        right = jnp.concatenate([expand[chunk] for chunk in range(chunks)], axis=1)
        d_tokens_ref[spot, :] = (d_image[pair] + dot_nt(left, right)).astype(BF16)


    if not quick:
        for chunk in range(chunks):
            g_expand_ref[:, chunk * CHUNK : (chunk + 1) * CHUNK] = a_expand[chunk].astype(BF16)
            g_project_ref[chunk * CHUNK : (chunk + 1) * CHUNK, :] = a_project[chunk].astype(BF16).T
            g_taps_ref[:, chunk * CHUNK : (chunk + 1) * CHUNK] = a_taps[chunk]
        for pair in range(pairs):
            finish_pair(pair)
        return

    send_part(chunks - 1)
    lines = []
    for k in range(9):
        line = jnp.concatenate([a_taps[c, 8 * k : 8 * k + 8, :] for c in range(chunks)], axis=1)
        lines.append(jnp.sum(line, axis=0, keepdims=True))
    depth = jnp.concatenate(lines, axis=0)
    vectors = [late_norm_ref[8 * k : 8 * k + 8] for k in (4, 5, 2, 3, 0, 1)]
    vectors = jnp.concatenate([jnp.sum(vector, axis=0, keepdims=True) for vector in vectors], axis=0)
    share, thin = hidden // (2 * layers), width // (2 * layers)
    stage_small[...] = jnp.zeros_like(stage_small)
    for f in range(2 * layers):
        stage_small[f // 2, f % 2, 0:9, 0:share] = depth[:, f * share : (f + 1) * share]
        stage_small[f // 2, f % 2, 9:15, 0:thin] = vectors[:, f * thin : (f + 1) * thin]
    small.start()
    finish_pair(0)
    parts[4].add_core()
    parts[5].add_core()
    small.add_core()
    whole_project.add_side()
    down.add_x()
    parts[2].add_x()
    parts[3].add_line()
    finish_pair(1)
    parts[4].add_side()
    parts[5].add_side()
    small.add_side()
    mixed.add_line()
    finish_pair(2)
    parts[3].add_x()
    parts[4].add_line()
    parts[5].add_line()
    small.add_line()
    whole_project.add_line()
    finish_pair(3)
    mixed.add_x()
    parts[4].add_x()
    parts[5].add_x()
    small.add_x()
    whole_project.add_x()
    for part in [up, down, mixed, whole_project, small] + parts:
        part.finish()


def conv_backward(tokens_t, keep, d_first, d_proj, d_proj_t, field, act, pull, w_expand, taps, w_project, late=None):
    rows, width = d_first.shape
    chunks = w_expand.shape[0]
    hidden = chunks * CHUNK
    images = rows // ROWS
    anywhere = pl.BlockSpec(memory_space=pl.ANY)
    here = pl.BlockSpec(memory_space=pltpu.VMEM)
    pairs = images // 2
    by_pair = (pairs, 2 * ROWS, width)
    wide = (2 * chunks, rows, 128)
    scratch = [
        pltpu.VMEM(by_pair, F32),
        pltpu.VMEM(wide, BF16),
        pltpu.VMEM(wide, BF16),
        pltpu.VMEM(wide, BF16),
        pltpu.VMEM((chunks, width, CHUNK), BF16),
        pltpu.VMEM((chunks, CHUNK, width), BF16),
        pltpu.SemaphoreType.DMA((7 + chunks * 3,)),
        pltpu.VMEM((pairs, 2 * ROWS, width), BF16),
        pltpu.VMEM((pairs, width, 2 * ROWS), BF16),
        pltpu.VMEM((pairs + 1, width, 2 * ROWS), BF16),
        pltpu.VMEM((images, ROWS, 128), BF16),
        pltpu.VMEM((chunks, 9, GRID, CHUNK), BF16),
        pltpu.VMEM((chunks, width, CHUNK), F32),
        pltpu.VMEM((chunks, width, CHUNK), F32),
        pltpu.VMEM((chunks, 72, CHUNK), F32),
    ]
    scratch += [pltpu.VMEM((2, 3, 2, ROWS + 2 * GRID, 128), BF16)]
    operands = [
        tokens_t, keep.reshape(images, ROWS, 128), d_first.reshape(by_pair), d_proj.reshape(by_pair), d_proj_t,
        field, act, pull, w_expand, taps, w_project.reshape(chunks, CHUNK, width),
    ]
    in_specs = [anywhere] * 9 + [here, anywhere]
    d_tokens = jax.ShapeDtypeStruct((rows, width), BF16)
    if late is None:
        layers, params = 0, {}
        out_shape = [
            d_tokens,
            jax.ShapeDtypeStruct((width, hidden), BF16),
            jax.ShapeDtypeStruct(w_project.shape, BF16),
            jax.ShapeDtypeStruct((72, hidden), F32),
        ]
    else:
        g_norm, g_mixed, g_up, g_down = late
        layers = g_up.shape[0]
        params = dict(collective_id=1, has_side_effects=True)
        operands += [g_norm, g_mixed, g_up, g_down]
        in_specs += [here] + [anywhere] * 3
        span = -(-hidden // (2 * layers) // 128) * 128
        b_small, b_expand, b_project = (16, span), (width // (2 * layers), hidden), (hidden // (2 * layers), width)
        blocks = (b_small, b_expand, b_project, g_mixed.shape[2:], g_up.shape[2:], g_down.shape[2:])
        out_shape = [d_tokens] + [jax.ShapeDtypeStruct(block, F32) for block in blocks]
        lead = (layers, 2)
        piece = (b_expand[0], CHUNK)
        scratch += [pltpu.VMEM(lead + b_project, BF16), pltpu.VMEM(lead + b_small, F32)]
        scratch += [pltpu.VMEM(lead + piece, BF16)] * chunks
        scratch += [pltpu.VMEM(lead + part_shape(block), BF16) for block in blocks[3:]]
        scratch += [pltpu.SemaphoreType.DMA((3,))]
        for shape, dtype, cross in (
            [(blocks[3], BF16, True), (blocks[4], BF16, False), (blocks[5], BF16, True), (blocks[2], BF16, True)]
            + [(piece, BF16, False)] * chunks
            + [(b_small, F32, False)]
        ):
            scratch += reduce_buffers(lead + shape, dtype, cross)
        copies = (5 + chunks) * (4 + layers)
        scratch += [pltpu.SemaphoreType.DMA((copies,))] * 2
    return pl.pallas_call(
        functools.partial(conv_backward_kernel, layers),
        in_specs=in_specs,
        out_specs=[here] * len(out_shape),
        out_shape=out_shape,
        scratch_shapes=scratch,
        compiler_params=pltpu.CompilerParams(vmem_limit_bytes=VMEM_BYTES, **params),
        name="conv_backward",
    )(*operands)


def deliver_kernel(*refs):
    tokens_in, small_ref, *blocks = refs[:7]
    tokens_out, depth_ref, *rest = refs[7:]
    vectors, outs = rest[:6], rest[6:]
    expand, project, mixed, up, down = blocks
    cut = outs[2].shape[1]
    pairs = [(tokens_in, tokens_out), (expand, outs[0]), (project, outs[1])]
    pairs += [(mixed.at[:, :cut], outs[2]), (mixed.at[:, cut:], outs[3]), (up, outs[4]), (down, outs[5])]
    for source, target in pairs:
        target[...] = source[...]
    depth_ref[...] = small_ref[0 : depth_ref.shape[0], 0 : depth_ref.shape[1]]
    for line, ref in enumerate(vectors):
        ref[...] = small_ref[9 + line, 0 : ref.shape[0]]


def deliver(d_tokens, small, s_expand, s_project, s_mixed, s_up, s_down, share, thin):
    rows, width = s_mixed.shape[0], s_project.shape[1]
    here = pl.BlockSpec(memory_space=pltpu.VMEM)
    blocks = [s_expand.shape, s_project.shape, (rows, 3 * width), (rows, width), s_up.shape, s_down.shape]
    return pl.pallas_call(
        deliver_kernel,
        in_specs=[here] * 7,
        out_specs=[here] * 14,
        out_shape=[jax.ShapeDtypeStruct(d_tokens.shape, BF16), jax.ShapeDtypeStruct((9, share), F32)]
        + [jax.ShapeDtypeStruct((thin,), F32)] * 6
        + [jax.ShapeDtypeStruct(block, F32) for block in blocks],
        compiler_params=pltpu.CompilerParams(vmem_limit_bytes=VMEM_BYTES),
        name="deliver",
    )(d_tokens, small, s_expand, s_project, s_mixed, s_up, s_down)


def reduce_plain(terms):
    results = []
    for term in terms:
        share = lax.psum_scatter(term, "fsdp", scatter_dimension=0, tiled=False)
        results.append(lax.psum(share, "dp").astype(F32))
    return results


def local(
    fsdp, quick,
    tokens, grid, w_expand, w_depth, w_project, gain_conv, bias_conv, gain_attend, bias_attend,
    w_qkv, w_out, gain_mlp, bias_mlp, w_up, w_down, cotangent,
):
    slots, rows, width = tokens.shape
    hidden = w_expand.shape[1]
    share, thin = w_depth.shape[1], gain_conv.shape[0]
    span = -(-share // 128) * 128
    vectors = (gain_conv, bias_conv, gain_attend, bias_attend, gain_mlp, bias_mlp)
    grid = grid.T
    flat, cotan = tokens.reshape(slots * rows, width), cotangent.reshape(slots * rows, width)
    if quick:
        field, act, pull, projected, first, tokens_t, keep, taps, norms, *fulls = gather_forward(
            grid, flat, w_depth, vectors, w_expand, w_project, w_qkv, w_out, w_up, w_down, fsdp // 2
        )
        f_expand = fulls[0]
        f_project, f_mixed, f_up, f_down = [full.reshape(-1, full.shape[3]) for full in fulls[1:]]
    else:
        mixed = jnp.concatenate((w_qkv, w_out), axis=1)
        f_expand, f_project, f_mixed, f_up, f_down = [
            lax.all_gather(shard, "fsdp", axis=0, tiled=True) for shard in (w_expand, w_project, mixed, w_up, w_down)
        ]
        f_expand = f_expand.reshape(width, hidden // CHUNK, CHUNK).transpose(1, 0, 2)
        taps = jnp.pad(lax.all_gather(w_depth, "fsdp", axis=1, tiled=True).astype(F32), ((0, 7), (0, 0)))
        lines = lax.all_gather(jnp.stack(vectors), "fsdp", axis=1, tiled=True).astype(F32)
        norms = jnp.pad(lines, ((1, 1), (0, 0)))
        field, act, pull, projected, first, tokens_t, keep = conv_forward(
            grid, flat, f_expand, taps, f_project, norms
        )
    layer_out, d_first, d_proj, d_proj_t, g_norm, g_mixed, g_up, g_down = middle(
        grid, first, cotan, projected, f_mixed, f_up, f_down, norms
    )
    inputs = (tokens_t, keep, d_first, d_proj, d_proj_t, field, act, pull, f_expand, taps, f_project)
    if quick:
        late = [term.reshape((fsdp // 2, 2, -1, term.shape[1])) for term in (g_mixed, g_up, g_down)]
        d_tokens, small, s_expand, s_project, s_mixed, s_up, s_down = conv_backward(*inputs, late=[g_norm] + late)
    else:
        d_tokens, g_expand, g_project, g_taps = conv_backward(*inputs)
        g_taps = jnp.sum(g_taps.reshape(9, 8, fsdp, share), axis=1)
        g_norm = jnp.concatenate((g_norm[32:], g_norm[16:32], g_norm[:16]), axis=0)
        g_norm = jnp.sum(g_norm.reshape(6, 8, fsdp, thin), axis=1)
        g_small = jnp.concatenate(
            (
                jnp.pad(g_taps, ((0, 0), (0, 0), (0, span - share))),
                jnp.pad(g_norm, ((0, 1), (0, 0), (0, span - thin))),
            ),
            axis=0,
        ).transpose(1, 0, 2)
        terms = [g_small] + [
            term.reshape((fsdp, -1, term.shape[1])) for term in (g_expand, g_project, g_mixed, g_up, g_down)
        ]
        small, s_expand, s_project, s_mixed, s_up, s_down = reduce_plain(terms)
    d_tokens, depth, *rest = deliver(d_tokens, small, s_expand, s_project, s_mixed, s_up, s_down, share, thin)
    vectors, (s_expand, s_project, s_qkv, s_out, s_up, s_down) = rest[:6], rest[6:]
    return (
        layer_out.reshape(tokens.shape),
        d_tokens.reshape(tokens.shape),
        s_expand,
        depth,
        s_project,
        *vectors[:4],
        s_qkv,
        s_out,
        *vectors[4:],
        s_up,
        s_down,
    )


def solution(mesh):
    fsdp, dp = mesh.shape["fsdp"], mesh.shape["dp"]
    quick = fsdp == 8 and dp == 4
    images, wide, tall, vector = P(("dp", "fsdp"), None, None), P("fsdp", None), P(None, "fsdp"), P("fsdp")
    in_specs = (
        images, P(("dp", "fsdp"), None), wide, tall, wide, vector, vector, vector, vector,
        wide, wide, vector, vector, wide, wide, images,
    )
    out_specs = (
        images, images, wide, tall, wide, vector, vector, vector, vector,
        wide, wide, vector, vector, wide, wide,
    )
    return jax.shard_map(
        functools.partial(local, fsdp, quick), mesh=mesh, in_specs=in_specs, out_specs=out_specs, check_vma=False
    )
```

```python
import functools

import jax
import jax.numpy as jnp
from jax import lax
from jax.experimental import pallas as pl
from jax.experimental.pallas import tpu as pltpu
from jax.sharding import PartitionSpec as P

HDIM = 64
GRID = 16
ROWS = GRID * GRID
CHUNK = 256
EPSILON = 1e-05
VMEM_BYTES = 62 * 1024 * 1024
F32 = jnp.float32
BF16 = jnp.bfloat16


def dot_nn(left, right):
    return jnp.dot(left, right, preferred_element_type=F32)


def dot_nt(left, right):
    return lax.dot_general(left, right, (((1,), (1,)), ((), ())), preferred_element_type=F32)


def dot_tn(left, right):
    return lax.dot_general(left, right, (((0,), (0,)), ((), ())), preferred_element_type=F32)


def valid_cells(high, wide, shape):
    place = lax.broadcasted_iota(jnp.int32, shape, 0)
    return (place // GRID < high) & (place % GRID < wide)


def normalized(values):
    center = jnp.mean(values, axis=-1, keepdims=True)
    shifted = values - center
    spread = jnp.mean(shifted * shifted, axis=-1, keepdims=True)
    inverse = lax.rsqrt(spread + EPSILON)
    return shifted * inverse, inverse


def norm_pull(grad, gain, unit, inverse):
    scaled = grad * gain
    mean_plain = jnp.mean(scaled, axis=-1, keepdims=True)
    mean_unit = jnp.mean(scaled * unit, axis=-1, keepdims=True)
    return (scaled - mean_plain - unit * mean_unit) * inverse


def both(left, right):
    return jnp.concatenate((left, right), axis=1)


def fold_rows(values):
    rows, width = values.shape
    return jnp.sum(values.reshape(rows // 8, 8, width), axis=0)


def move_cells(values, step):
    rows, width = values.shape
    parts = values.reshape(rows // GRID, 2, 8, width)
    turned = pltpu.roll(parts, step % 8, axis=2)
    first, last = turned[:, 0:1], turned[:, 1:2]
    line = lax.broadcasted_iota(jnp.int32, first.shape, 2)
    if step == 1:
        edge = line == 0
        moved = jnp.concatenate((jnp.where(edge, 0.0, first), jnp.where(edge, first, last)), axis=1)
    else:
        edge = line == 7
        moved = jnp.concatenate((jnp.where(edge, last, first), jnp.where(edge, 0.0, last)), axis=1)
    return moved.reshape(rows, width)


MESH = pl.DeviceIdType.MESH


def places(sides):
    dp, fsdp = lax.axis_index("dp"), lax.axis_index("fsdp")
    return dp // 2, dp % 2, fsdp // sides, fsdp % sides


def part_of(ref, lead, index, count=2):
    rows, columns = ref.shape[-2:]
    if columns > rows * 4:
        size = columns // count
        return ref.at[lead + (slice(None), pl.ds(pl.multiple_of(index * size, size), size))]
    size = rows // count
    return ref.at[lead + (pl.ds(pl.multiple_of(index * size, size), size), slice(None))]


def part_shape(shape, count=2):
    rows, columns = shape
    return (rows, columns // count) if columns > rows * 4 else (rows // count, columns)


def remote(source, target, sends, receives, index, device):
    return pltpu.make_async_remote_copy(
        src_ref=source,
        dst_ref=target,
        send_sem=sends.at[index],
        recv_sem=receives.at[index],
        device_id=device,
        device_id_type=MESH,
    )


def greet(devices):
    barrier = pltpu.get_barrier_semaphore()
    for device in devices:
        pl.semaphore_signal(barrier, inc=1, device_id=device, device_id_type=MESH)
    pl.semaphore_wait(barrier, len(devices))


def peers_of(layers):
    x, core, z, y = places(2)
    dp, fsdp = x * 2 + core, z * 2 + y
    along = [(dp, (z ^ step) * 2 + y) for step in range(1, layers)]
    return along, (dp, z * 2 + 1 - y), (x * 2 + 1 - core, fsdp), ((1 - x) * 2 + core, fsdp)


class Gather:
    def __init__(self, shard, full, cross, sems, number):
        sends, receives, locals_ = sems
        self.full, self.cross, self.layers = full, cross, full.shape[0]
        self.x, self.core, self.z, self.y = places(2)
        along, across, sibling, beyond = peers_of(self.layers)
        base = number * (2 * self.layers + 3)
        own = self.piece(shard, ())
        spot = self.piece(full, (self.z, self.y))
        self.local = pltpu.make_async_copy(own, spot, locals_.at[number])
        self.along = [remote(own, spot, sends, receives, base + step, device) for step, device in enumerate(along)]
        base += self.layers - 1
        self.over = []
        for step in range(self.layers):
            target = self.piece(full, (self.z ^ step, self.y))
            self.over.append(remote(own if step == 0 else target, target, sends, receives, base + step, across))
        base += self.layers
        self.beyond, self.inside = [], []
        for step, side in enumerate((self.y, 1 - self.y)):
            half = part_of(full, (slice(None), side), self.core)
            self.inside.append(remote(half, half, sends, receives, base + step, sibling))
            if cross:
                target = self.piece(full, (slice(None), side))
                self.beyond.append(remote(target, target, sends, receives, base + 2 + step, beyond))

    def piece(self, ref, lead):
        half = part_of(ref, lead, self.core)
        return part_of(half, (slice(None),) * (len(half.shape) - 2), self.x) if self.cross else half

    def start(self):
        for copy in self.along:
            copy.start()
        self.over[0].start()
        self.local.start()

    def forward(self):
        for step, copy in enumerate(self.along):
            copy.wait_recv()
            self.over[step + 1].start()
        self.local.wait()
        (self.beyond if self.cross else self.inside)[0].start()

    def side(self):
        for copy in self.over:
            copy.wait_recv()
        (self.beyond if self.cross else self.inside)[1].start()

    def share(self):
        for copy, after in zip(self.beyond, self.inside):
            copy.wait_recv()
            after.start()

    def finish(self):
        for copy in self.inside:
            copy.wait_recv()

    def drain(self):
        for copy in self.along + self.over + self.beyond + self.inside:
            copy.wait_send()


class Spread:
    def __init__(self, block, full, sems, base):
        sends, receives, local = sems
        layers = full.shape[0]
        x, core, z, y = places(2)
        spot = full.at[z, y]
        self.local = pltpu.make_async_copy(block, spot, local)
        self.copies = [
            remote(block, spot, sends, receives, base + 2 * up + over - 1, (x * 2 + core, (z ^ up) * 2 + (y ^ over)))
            for up in range(layers)
            for over in range(2)
            if up + over > 0
        ]

    def start(self):
        for copy in self.copies:
            copy.start()
        self.local.start()

    def finish(self):
        for copy in self.copies:
            copy.wait_recv()
        self.local.wait()

    def drain(self):
        for copy in self.copies:
            copy.wait_send()


def spread_taps(taps_ref, taps_b):
    for chunk in range(taps_b.shape[0]):
        for k in range(9):
            line = taps_ref[k : k + 1, chunk * CHUNK : (chunk + 1) * CHUNK]
            taps_b[chunk, k] = jnp.broadcast_to(line, (GRID, CHUNK)).astype(BF16)


def conv_chunk(chunk, kept, weights, taps_ref, frames, field_ref, act_ref, pull_ref, acts, slot):
    expanded = dot_nn(kept, weights)
    block = 64
    for half in range(CHUNK // 128):
        lanes = slice(half * 128, (half + 1) * 128)
        field_ref[chunk * 2 + half] = expanded[:, lanes].astype(BF16)
        frames[chunk % 2, half, GRID : GRID + ROWS] = expanded[:, lanes]
        whole = slice(chunk * CHUNK + half * 128, chunk * CHUNK + (half + 1) * 128)
        taps = [taps_ref[k : k + 1, whole] for k in range(9)]
        for start in range(0, ROWS, block):
            near = [frames[chunk % 2, half, start + GRID * a : start + GRID * a + block] for a in range(3)]
            sums = [sum(taps[3 * a + b] * near[a] for a in range(3)) for b in range(3)]
            conv = sums[1] + move_cells(sums[0], 1) + move_cells(sums[2], -1)
            gate = 0.5 * jnp.tanh(0.5 * conv) + 0.5
            act = conv * gate
            low = act.astype(BF16)
            act_ref[chunk * 2 + half, start : start + block] = low
            acts[slot, chunk * 2 + half, start : start + block] = low
            pull_ref[chunk * 2 + half, start : start + block] = (gate + act * (1.0 - gate)).astype(BF16)


def project_chunks(chunk, acts, slot, project):
    left = jnp.concatenate([acts[slot, 2 * chunk + part] for part in range(4)], axis=1)
    return dot_nn(left, project[chunk * CHUNK : (chunk + 2) * CHUNK, :])


def end_forward(projected, tokens, valid, norms_ref, projected_ref, first_ref):
    projected_ref[...] = projected
    unit, _ = normalized(projected)
    shift = unit * norms_ref[1:2, :] + norms_ref[2:3, :]
    first_ref[...] = tokens.astype(F32) + jnp.where(valid, shift, 0.0)


def conv_forward_body(
    step, before, middle_of_first, grid_ref, tokens_ref, late_tokens_ref, weights, project, norms_ref, taps_ref,
    field_ref, act_ref, pull_ref, projected_ref, first_ref, tokens_t_ref, keep_ref, frames, acts,
):
    width = tokens_ref.shape[1]
    chunks = weights.shape[0]
    images = pl.num_programs(0) - 2
    slot = lax.rem(step, 2)

    def start_image():
        valid = valid_cells(grid_ref[0, step], grid_ref[1, step], (ROWS, width))
        tokens = tokens_ref[...]
        tokens_t_ref[0] = tokens.T
        keep_ref[...] = jnp.where(valid[:, :128], 1.0, 0.0).astype(BF16)
        return jnp.where(valid, tokens, jnp.zeros_like(tokens))

    def convolve(chunk, kept):
        conv_chunk(chunk, kept, weights[chunk], taps_ref, frames, field_ref, act_ref, pull_ref, acts, slot)

    def end_image(projected):
        high, wide = grid_ref[0, step - 2], grid_ref[1, step - 2]
        valid = valid_cells(high, wide, (ROWS, width))
        end_forward(projected, late_tokens_ref[...], valid, norms_ref, projected_ref, first_ref)

    @pl.when(step == 0)
    def _():
        before()
        frames[...] = jnp.zeros_like(frames)
        kept = start_image()
        for chunk in range(chunks):
            middle_of_first(chunk)
            convolve(chunk, kept)

    @pl.when(step == 1)
    def _():
        kept = start_image()
        for chunk in range(chunks):
            convolve(chunk, kept)

    @pl.when((step > 1) & (step < images))
    def _():
        kept = start_image()
        projected = jnp.zeros((ROWS, width), F32)
        for chunk in range(0, chunks, 2):
            projected = projected + project_chunks(chunk, acts, slot, project)
            convolve(chunk, kept)
            convolve(chunk + 1, kept)
        end_image(projected)

    @pl.when(step >= images)
    def _():
        projected = jnp.zeros((ROWS, width), F32)
        for chunk in range(0, chunks, 2):
            projected = projected + project_chunks(chunk, acts, slot, project)
        end_image(projected)


def conv_forward_kernel(
    grid_ref, tokens_ref, late_tokens_ref, weights, taps_ref, project_ref, norms_ref,
    field_ref, act_ref, pull_ref, projected_ref, first_ref, tokens_t_ref, keep_ref, frames, acts,
):
    conv_forward_body(
        pl.program_id(0), lambda: None, lambda chunk: None,
        grid_ref, tokens_ref, late_tokens_ref, weights, project_ref, norms_ref, taps_ref,
        field_ref, act_ref, pull_ref, projected_ref, first_ref, tokens_t_ref, keep_ref, frames, acts,
    )


def gather_forward_kernel(
    grid_ref, tokens_ref, late_tokens_ref, depth_ref, gain1_ref, bias1_ref, gain2_ref, bias2_ref, gain3_ref, bias3_ref,
    s_expand, s_project, s_qkv, s_out, s_up, s_down,
    field_ref, act_ref, pull_ref, projected_ref, first_ref, tokens_t_ref, keep_ref,
    taps_ref, norms_ref, f_expand, f_project, f_mixed, f_up, f_down,
    frames, acts, weights, v_expand, v_project, v_small, own_small, own_mixed, sends, receives, locals_,
):
    step = pl.program_id(0)
    last = pl.num_programs(0) - 1
    sems = (sends, receives, locals_)
    layers = v_small.shape[0]
    hidden, width = taps_ref.shape[1], tokens_ref.shape[1]
    wide = v_expand.shape[-1]
    pieces = v_expand.shape[0]
    expand = [
        Gather(s_expand.at[:, piece * wide : (piece + 1) * wide], v_expand.at[piece], True, sems, piece)
        for piece in range(pieces)
    ]
    project = Gather(s_project, v_project, False, sems, pieces)
    mixed = Gather(own_mixed, f_mixed, True, sems, pieces + 1)
    up = Gather(s_up, f_up, True, sems, pieces + 2)
    down = Gather(s_down, f_down, False, sems, pieces + 3)
    count = pieces + 4
    small = Spread(own_small, v_small, (sends, receives, locals_.at[count]), count * (2 * layers + 3))
    share, thin = depth_ref.shape[1], gain1_ref.shape[0]
    cut = s_qkv.shape[1]
    joins = [
        pltpu.make_async_copy(s_qkv, own_mixed.at[:, :cut], locals_.at[count + 1]),
        pltpu.make_async_copy(s_out, own_mixed.at[:, cut:], locals_.at[count + 2]),
    ]
    save_expand = pltpu.make_async_copy(weights, f_expand, locals_.at[count + 3])
    save_project = pltpu.make_async_copy(v_project, f_project, locals_.at[count + 4])

    @pl.when(step == 0)
    def _():
        for join in joins:
            join.start()
        own_small[...] = jnp.zeros_like(own_small)
        own_small[0:9, 0:share] = depth_ref[...].astype(F32)
        for line, ref in enumerate((gain1_ref, bias1_ref, gain2_ref, bias2_ref, gain3_ref, bias3_ref)):
            own_small[9 + line : 10 + line, 0:thin] = ref[...].astype(F32).reshape(1, thin)
        x, core, z, y = places(2)
        _, _, sibling, beyond = peers_of(layers)
        others = [
            (x * 2 + core, (z ^ more) * 2 + (y ^ over)) for more in range(layers) for over in range(2) if more + over > 0
        ]
        greet(others + [sibling, beyond])
        for part in expand:
            part.start()
        small.start()

    def before():
        for join in joins:
            join.wait()
        for part in expand:
            part.forward()
        project.start()
        small.finish()
        blocks = [v_small[z, y] for z in range(layers) for y in range(2)]
        taps_ref[...] = jnp.concatenate([block[:, :share] for block in blocks], axis=1)
        norms_ref[...] = jnp.concatenate([block[8:, :thin] for block in blocks], axis=1)
        for part in expand:
            part.side()
        mixed.start()

    def middle_of_first(chunk):
        per = wide // CHUNK
        piece, place = chunk // per, chunk % per
        if place == 0:
            expand[piece].share()
            expand[piece].finish()
        weights[chunk] = v_expand[piece, :, :, :, place * CHUNK : (place + 1) * CHUNK].reshape(width, CHUNK)

    def at(number, *works):
        @pl.when(step == number)
        def _():
            for work in works:
                work()

    at(1, project.forward, save_expand.start, up.start)
    at(2, project.side, project.finish, save_project.start, mixed.forward, down.start)
    at(3, mixed.side, up.forward)
    at(4, up.side)
    at(5, mixed.share, down.forward)
    at(6, down.side)
    at(7, up.share)

    conv_forward_body(
        step, before, middle_of_first,
        grid_ref, tokens_ref, late_tokens_ref, weights, v_project.reshape(hidden, width), norms_ref, taps_ref,
        field_ref, act_ref, pull_ref, projected_ref, first_ref, tokens_t_ref, keep_ref, frames, acts,
    )

    @pl.when(step == last)
    def _():
        for part in (mixed, up, down):
            part.finish()
        for part in expand + [small, project, mixed, up, down]:
            part.drain()
        save_expand.wait()
        save_project.wait()


def whole(shape):
    return pl.BlockSpec(shape, lambda *_: (0,) * len(shape), pipeline_mode=pl.Buffered(1))


def forward_specs(rows, width, hidden):
    images, chunks = rows // ROWS, hidden // CHUNK
    here = lambda i: jnp.minimum(i, images - 1)
    late = lambda i: jnp.maximum(i - 2, 0)
    by_image = pl.BlockSpec((ROWS, width), lambda i: (here(i), 0))
    by_late = pl.BlockSpec((ROWS, width), lambda i: (late(i), 0))
    by_chunk = pl.BlockSpec((2 * chunks, ROWS, 128), lambda i: (0, here(i), 0))
    turned = pl.BlockSpec((1, width, ROWS), lambda i: (here(i) // 2, 0, here(i) % 2))
    cells = pl.BlockSpec((ROWS, 128), lambda i: (here(i), 0))
    wide = jax.ShapeDtypeStruct((2 * chunks, rows, 128), BF16)
    tall = jax.ShapeDtypeStruct((rows, width), F32)
    return (
        [pl.BlockSpec(memory_space=pltpu.SMEM), by_image, by_late],
        [by_chunk, by_chunk, by_chunk, by_late, by_late, turned, cells],
        [
            wide, wide, wide, tall, tall,
            jax.ShapeDtypeStruct((images // 2, width, 2 * ROWS), BF16), jax.ShapeDtypeStruct((rows, 128), BF16),
        ],
        [
            pltpu.VMEM((2, 2, ROWS + 2 * GRID, 128), F32),
            pltpu.VMEM((2, 2 * chunks, ROWS, 128), BF16),
        ],
    )


def conv_forward(grid, tokens, w_expand, taps, w_project, norms):
    rows, width = tokens.shape
    in_specs, out_specs, out_shape, scratch = forward_specs(rows, width, taps.shape[1])
    return pl.pallas_call(
        conv_forward_kernel,
        grid=(rows // ROWS + 2,),
        in_specs=in_specs + [whole(w_expand.shape), whole(taps.shape), whole(w_project.shape), whole(norms.shape)],
        out_specs=out_specs,
        out_shape=out_shape,
        scratch_shapes=scratch,
        compiler_params=pltpu.CompilerParams(vmem_limit_bytes=VMEM_BYTES),
        name="conv_forward",
    )(grid, tokens, tokens, w_expand, taps, w_project, norms)


def gather_forward(grid, tokens, w_depth, vectors, w_expand, w_project, w_qkv, w_out, w_up, w_down, layers):
    rows, width = tokens.shape
    hidden = w_expand.shape[1]
    chunks = hidden // CHUNK
    in_specs, out_specs, out_shape, scratch = forward_specs(rows, width, hidden)
    anywhere = pl.BlockSpec(memory_space=pl.ANY)
    here = pl.BlockSpec(memory_space=pltpu.VMEM)
    span = -(-w_depth.shape[1] // 128) * 128
    mixed = (w_qkv.shape[0], w_qkv.shape[1] + w_out.shape[1])
    pieces = 3
    lead = (layers, 2)
    fulls = [(chunks, width, CHUNK)] + [lead + shape for shape in (w_project.shape, mixed, w_up.shape, w_down.shape)]
    copies = (pieces + 4) * (2 * layers + 3) + 2 * layers
    return pl.pallas_call(
        gather_forward_kernel,
        grid=(rows // ROWS + 2,),
        in_specs=in_specs + [here] * 7 + [anywhere] * 6,
        out_specs=out_specs + [whole((16, hidden)), whole((8, width))] + [anywhere] * 5,
        out_shape=out_shape
        + [jax.ShapeDtypeStruct((16, hidden), F32), jax.ShapeDtypeStruct((8, width), F32)]
        + [jax.ShapeDtypeStruct(full, BF16) for full in fulls],
        scratch_shapes=scratch
        + [
            pltpu.VMEM((chunks, width, CHUNK), BF16),
            pltpu.VMEM((pieces,) + lead + (w_expand.shape[0], hidden // pieces), BF16),
            pltpu.VMEM(fulls[1], BF16),
            pltpu.VMEM(lead + (16, span), F32),
            pltpu.VMEM((16, span), F32),
            pltpu.VMEM(mixed, BF16),
            pltpu.SemaphoreType.DMA((copies,)),
            pltpu.SemaphoreType.DMA((copies,)),
            pltpu.SemaphoreType.DMA((pieces + 9,)),
        ],
        compiler_params=pltpu.CompilerParams(
            vmem_limit_bytes=VMEM_BYTES, collective_id=0, has_side_effects=True
        ),
        name="gather_forward",
    )(grid, tokens, tokens, w_depth, *vectors, w_expand, w_project, w_qkv, w_out, w_up, w_down)


def heads_apart(pair):
    lane = lax.broadcasted_iota(jnp.int32, pair.shape, 1) // HDIM
    zero = jnp.zeros_like(pair)
    return jnp.concatenate((jnp.where(lane == 0, pair, zero), jnp.where(lane == 1, pair, zero)), axis=0)


def middle_kernel(*refs):
    take = iter(refs)
    grid_ref, first_ref, cotan_ref, projected_ref, norms_ref = [next(take) for _ in range(5)]
    mixed_hbm, up_hbm, down_hbm = [next(take) for _ in range(3)]
    layer_ref, d_first_ref, d_proj_ref, d_proj_t_ref, g_norm_ref, g_mixed_ref = [next(take) for _ in range(6)]
    g_up_ref, g_down_ref = next(take), next(take)
    w_qkv, w_out, w_up, w_down, load_sems = [next(take) for _ in range(5)]
    a_qkv, a_out, a_up, a_down = [next(take) for _ in range(4)]
    firsts, seconds, normeds, queries, keys, values, expo, inverses, attended, d_qkv = [next(take) for _ in range(10)]
    step = pl.program_id(0)
    pairs = firsts.shape[0]
    width = firsts.shape[2]
    chunks = w_up.shape[0]
    hidden = chunks * CHUNK
    blocks = width // 128
    cut = 3 * width

    loads = [
        pltpu.make_async_copy(mixed_hbm.at[:, :cut], w_qkv, load_sems.at[0]),
        pltpu.make_async_copy(mixed_hbm.at[:, cut:], w_out, load_sems.at[1]),
    ]
    loads.append(pltpu.make_async_copy(down_hbm, w_down, load_sems.at[2]))
    for chunk in range(chunks):
        source = up_hbm.at[:, chunk * CHUNK : (chunk + 1) * CHUNK]
        loads.append(pltpu.make_async_copy(source, w_up.at[chunk], load_sems.at[3 + chunk]))

    @pl.when(step == 0)
    def _():
        for load in loads:
            load.start()
        for ref in (a_qkv, a_out, a_up, a_down, g_norm_ref):
            ref[...] = jnp.zeros_like(ref)
        for load in loads[:2]:
            load.wait()

    @pl.when(step == pairs)
    def _():
        for load in loads[2:]:
            load.wait()

    def sizes(pair, side):
        return grid_ref[0, 2 * pair + side], grid_ref[1, 2 * pair + side]

    def valid_pair(pair):
        return jnp.concatenate([valid_cells(*sizes(pair, side), (ROWS, width)) for side in range(2)], axis=0)

    def forward(pair):
        first = first_ref[...]
        firsts[pair] = first
        unit, _ = normalized(first)
        normed = (unit * norms_ref[3:4, :] + norms_ref[4:5, :]).astype(BF16)
        normeds[pair] = normed
        packed = dot_nn(normed, w_qkv[...]).astype(BF16)
        line = lax.broadcasted_iota(jnp.int32, (128, ROWS), 0) // HDIM
        biases = [jnp.where(valid_cells(*sizes(pair, side), (ROWS, ROWS)), 0.0, -1e9) for side in range(2)]
        units = [(side, block) for side in range(2) for block in range(blocks)]

        def score(side, block):
            image, lines = 2 * pair + side, slice(side * ROWS, (side + 1) * ROWS)
            query = packed[lines, block * 128 : (block + 1) * 128] * jnp.asarray(HDIM**-0.5, BF16)
            key = packed[lines, width + block * 128 : width + (block + 1) * 128]
            value = packed[lines, 2 * width + block * 128 : 2 * width + (block + 1) * 128]
            queries[image, block], keys[image, block], values[image, block] = query, key, value
            return dot_nt(heads_apart(key), query), heads_apart(value)

        ahead = score(*units[0])
        for number, (side, block) in enumerate(units):
            scores, value = ahead
            if number + 1 < len(units):
                ahead = score(*units[number + 1])
            image = 2 * pair + side
            columns = slice(block * 128, (block + 1) * 128)
            totals, powers = [], []
            for head in range(2):
                rows = slice(head * ROWS, (head + 1) * ROWS)
                part = scores[rows] + biases[side]
                power = jnp.exp(part - jnp.max(part, axis=0, keepdims=True))
                totals.append(1.0 / jnp.sum(power, axis=0, keepdims=True))
                powers.append(power.astype(BF16))
                expo[image, block, rows] = powers[-1]
            inverse = jnp.where(line == 0, totals[0], totals[1])
            inverses[image, block] = inverse
            attended[image, columns] = (dot_tn(value, jnp.concatenate(powers, axis=0)) * inverse).astype(BF16)
            if block == blocks - 1:
                lines = slice(side * ROWS, (side + 1) * ROWS)
                valid = valid_cells(*sizes(pair, side), (ROWS, width))
                seconds[pair, lines] = first[lines] + jnp.where(valid, dot_tn(attended[image], w_out[...]), 0.0)

    def feed(pair):
        valid = valid_pair(pair)
        second, cotan = seconds[pair], cotan_ref[...]
        unit, inverse = normalized(second)
        normed = (unit * norms_ref[5:6, :] + norms_ref[6:7, :]).astype(BF16)
        d_down = jnp.where(valid, cotan, jnp.zeros_like(cotan))
        normed_t, d_down_t = normed.T, d_down.T
        result = jnp.zeros((2 * ROWS, width), F32)
        d_normed = jnp.zeros((2 * ROWS, width), F32)

        def begin(chunk):
            lines = w_down[chunk * CHUNK : (chunk + 1) * CHUNK, :]
            return dot_nn(normed, w_up[chunk]), dot_nt(d_down, lines), lines

        ahead = begin(0)
        for chunk in range(chunks):
            upper, d_hidden, lines = ahead
            if chunk + 1 < chunks:
                ahead = begin(chunk + 1)
            square = upper * upper
            bent = jnp.tanh(upper * (0.7978845608028654 + (0.7978845608028654 * 0.044715) * square))
            gate = 0.5 * bent + 0.5
            hid = (upper * gate).astype(BF16)
            slope = gate + upper * (gate - gate * gate) * (
                2 * 0.7978845608028654 + (6 * 0.7978845608028654 * 0.044715) * square
            )
            d_upper = (d_hidden * slope).astype(BF16)
            result = result + dot_nn(hid, lines)
            a_down[chunk] += dot_nn(d_down_t, hid)
            a_up[chunk] += dot_nn(normed_t, d_upper)
            d_normed = d_normed + dot_nt(d_upper, w_up[chunk])
        layer_ref[...] = (second + jnp.where(valid, result, 0.0)).astype(BF16)
        g_norm_ref[0:8] += fold_rows(d_normed * unit)
        g_norm_ref[8:16] += fold_rows(d_normed)
        seconds[pair] = cotan.astype(F32) + norm_pull(d_normed, norms_ref[5:6, :], unit, inverse)

    def backward(pair):
        valid = valid_pair(pair)
        d_second = seconds[pair]
        d_out = jnp.where(valid, d_second, 0.0).astype(BF16)
        a_out[...] += dot_nn(both(attended[2 * pair], attended[2 * pair + 1]), d_out)
        line = lax.broadcasted_iota(jnp.int32, (128, ROWS), 0) // HDIM
        units = [(side, block) for side in range(2) for block in range(blocks)]

        def probe(side, block):
            image, lines = 2 * pair + side, slice(side * ROWS, (side + 1) * ROWS)
            columns = slice(block * 128, (block + 1) * 128)
            d_low = dot_nt(w_out[columns, :], d_out[lines]).astype(BF16).astype(F32)
            scaled = d_low * inverses[image, block]
            low = scaled.astype(BF16)
            inner = scaled * attended[image, columns].astype(F32)
            return low, inner, dot_nn(heads_apart(values[image, block]), low)

        ahead = probe(*units[0])
        for number, (side, block) in enumerate(units):
            low, inner, d_probs = ahead
            if number + 1 < len(units):
                ahead = probe(*units[number + 1])
            image, lines = 2 * pair + side, slice(side * ROWS, (side + 1) * ROWS)
            query = heads_apart(queries[image, block])
            d_value = jnp.zeros((ROWS, 128), F32)
            d_key = jnp.zeros((ROWS, 128), F32)
            steps = []
            for head in range(2):
                rows = slice(head * ROWS, (head + 1) * ROWS)
                delta = jnp.sum(inner[head * HDIM : (head + 1) * HDIM], axis=0, keepdims=True)
                power = expo[image, block, rows]
                d_score = (power.astype(F32) * (d_probs[rows] - delta)).astype(BF16)
                steps.append(d_score)
                own = jnp.where(line == head, low, jnp.zeros_like(low))
                d_value = d_value + dot_nt(power, own)
                d_key = d_key + dot_nn(d_score, query[rows])
            d_query_t = dot_tn(heads_apart(keys[image, block]), jnp.concatenate(steps, axis=0)) * (HDIM**-0.5)
            d_qkv[lines, block * 128 : (block + 1) * 128] = d_query_t.astype(BF16).T
            d_qkv[lines, width + block * 128 : width + (block + 1) * 128] = d_key.astype(BF16)
            d_qkv[lines, 2 * width + block * 128 : 2 * width + (block + 1) * 128] = d_value.astype(BF16)
        a_qkv[...] += dot_nn(normeds[pair].T, d_qkv[...])
        d_normed = dot_nt(d_qkv[...], w_qkv[...])
        unit, inverse = normalized(firsts[pair])
        g_norm_ref[16:24] += fold_rows(d_normed * unit)
        g_norm_ref[24:32] += fold_rows(d_normed)
        d_first = d_second + norm_pull(d_normed, norms_ref[3:4, :], unit, inverse)
        d_first_ref[...] = d_first
        unit, inverse = normalized(projected_ref[...])
        grad = jnp.where(valid, d_first, 0.0)
        g_norm_ref[32:40] += fold_rows(grad * unit)
        g_norm_ref[40:48] += fold_rows(grad)
        low = norm_pull(grad, norms_ref[1:2, :], unit, inverse).astype(BF16)
        d_proj_ref[...] = low
        d_proj_t_ref[0] = low.T

    pl.when(step < pairs)(lambda: forward(step))
    pl.when((step >= pairs) & (step < 2 * pairs))(lambda: feed(step - pairs))
    pl.when(step >= 2 * pairs)(lambda: backward(step - 2 * pairs))

    @pl.when(step == 3 * pairs - 1)
    def _():
        g_mixed_ref[:, :cut] = a_qkv[...].astype(BF16)
        g_mixed_ref[:, cut:] = a_out[...].astype(BF16)
        to_lines(a_down, g_down_ref.reshape(1, 1, hidden, width))
        for chunk in range(chunks):
            g_up_ref[:, chunk * CHUNK : (chunk + 1) * CHUNK] = a_up[chunk].astype(BF16)


def to_lines(blocks, target):
    layers, sides, share = target.shape[:3]
    for chunk in range(blocks.shape[0]):
        lines = blocks[chunk].astype(BF16).T
        for f in range(layers * sides):
            low, high = max(f * share, chunk * CHUNK), min((f + 1) * share, (chunk + 1) * CHUNK)
            if low < high:
                target[f // sides, f % sides, low - f * share : high - f * share] = lines[
                    low - chunk * CHUNK : high - chunk * CHUNK
                ]


def middle(grid, first, cotangent, projected, w_mixed, w_up, w_down, norms):
    rows, width = first.shape
    pairs, blocks = rows // (2 * ROWS), width // 128
    images = 2 * pairs
    hidden = w_up.shape[1]
    chunks = hidden // CHUNK
    cut = 3 * width

    def phase(number):
        return pl.BlockSpec((2 * ROWS, width), lambda i: (jnp.clip(i - number * pairs, 0, pairs - 1), 0))

    turned = pl.BlockSpec((1, width, 2 * ROWS), lambda i: (jnp.clip(i - 2 * pairs, 0, pairs - 1), 0, 0))
    anywhere = pl.BlockSpec(memory_space=pl.ANY)
    full_up, full_down = (width, hidden), (hidden, width)
    scratch = [
        pltpu.VMEM((width, cut), BF16),
        pltpu.VMEM((width, width), BF16),
        pltpu.VMEM((chunks, width, CHUNK), BF16),
        pltpu.VMEM(full_down, BF16),
        pltpu.SemaphoreType.DMA((3 + chunks,)),
        pltpu.VMEM((width, cut), F32),
        pltpu.VMEM((width, width), F32),
        pltpu.VMEM((chunks, width, CHUNK), F32),
        pltpu.VMEM((chunks, width, CHUNK), F32),
        pltpu.VMEM((pairs, 2 * ROWS, width), F32),
        pltpu.VMEM((pairs, 2 * ROWS, width), F32),
        pltpu.VMEM((pairs, 2 * ROWS, width), BF16),
        pltpu.VMEM((images, blocks, ROWS, 128), BF16),
        pltpu.VMEM((images, blocks, ROWS, 128), BF16),
        pltpu.VMEM((images, blocks, ROWS, 128), BF16),
        pltpu.VMEM((images, blocks, 2 * ROWS, ROWS), BF16),
        pltpu.VMEM((images, blocks, 128, ROWS), F32),
        pltpu.VMEM((images, width, ROWS), BF16),
        pltpu.VMEM((2 * ROWS, cut), BF16),
    ]
    grads = [jax.ShapeDtypeStruct(full_up, BF16), jax.ShapeDtypeStruct(full_down, BF16)]
    return pl.pallas_call(
        middle_kernel,
        grid=(3 * pairs,),
        in_specs=[pl.BlockSpec(memory_space=pltpu.SMEM), phase(0), phase(1), phase(2), whole(norms.shape)] + [anywhere] * 3,
        out_specs=[phase(1), phase(2), phase(2), turned, whole((48, width)), whole((width, cut + width))]
        + [whole(grad.shape) for grad in grads],
        out_shape=[
            jax.ShapeDtypeStruct((rows, width), BF16),
            jax.ShapeDtypeStruct((rows, width), F32),
            jax.ShapeDtypeStruct((rows, width), BF16),
            jax.ShapeDtypeStruct((pairs, width, 2 * ROWS), BF16),
            jax.ShapeDtypeStruct((48, width), F32),
            jax.ShapeDtypeStruct((width, cut + width), BF16),
        ]
        + grads,
        scratch_shapes=scratch,
        compiler_params=pltpu.CompilerParams(vmem_limit_bytes=VMEM_BYTES),
        name="middle",
    )(grid, first, cotangent, projected, norms, w_mixed, w_up, w_down)


class Reduce:
    def __init__(self, terms, mine, result, cross, buffers, sems, base, fetch_sem=None):
        sends, receives = sems
        self.terms, self.mine, self.result, self.cross = terms, mine, result, cross
        self.layers = terms.shape[0]
        self.x, self.core, self.z, self.y = places(2)
        self.along_devices, across, sibling, beyond = peers_of(self.layers)
        buffers = list(buffers)
        every = (slice(None), slice(None))
        self.from_core, self.chip = buffers[:2]
        other = part_of(terms, every, 1 - self.core)
        self.inside = remote(other, self.from_core, sends, receives, base, sibling)
        self.fetch = None
        if mine is not None:
            self.fetch = pltpu.make_async_copy(part_of(terms, every, self.core), mine, fetch_sem)
        rest = buffers[2:]
        if cross:
            self.from_cross, self.wide = rest[:2]
            self.over_x = remote(part_of(self.chip, every, 1 - self.x), self.from_cross, sends, receives, base + 1, beyond)
            rest = rest[2:]
        else:
            self.wide = self.chip
        self.from_side, self.line, self.from_along, self.own, self.from_x, self.total = rest
        self.over = remote(self.wide.at[:, 1 - self.y], self.from_side, sends, receives, base + 2, across)
        self.along = [
            remote(self.line.at[self.z ^ (step + 1)], self.from_along.at[step], sends, receives, base + 3 + step, device)
            for step, device in enumerate(self.along_devices)
        ]
        base += 3 + self.layers - 1
        half = part_of(result, (), self.core)
        if cross:
            self.spot = part_of(half, (), self.x)
            self.beyond = remote(self.total, self.spot, sends, receives, base, beyond)
            self.back = remote(half, half, sends, receives, base + 1, sibling)
        else:
            self.spot = half
            self.beyond = remote(self.own, self.from_x, sends, receives, base, beyond)
            self.back = remote(self.total, half, sends, receives, base + 1, sibling)

    def start(self):
        self.inside.start()

    def add_core(self):
        if self.fetch is not None:
            self.fetch.wait()
        self.inside.wait_recv()
        for z in range(self.layers):
            for y in range(2):
                if self.mine is not None:
                    own = self.mine[z, y]
                else:
                    own = part_of(self.terms, (z, y), self.core)[...]
                self.chip[z, y] = own + self.from_core[z, y]
        (self.over_x if self.cross else self.over).start()

    def add_cross(self):
        self.over_x.wait_recv()
        for z in range(self.layers):
            for y in range(2):
                self.wide[z, y] = part_of(self.chip, (z, y), self.x)[...] + self.from_cross[z, y]
        self.over.start()

    def add_side(self):
        self.over.wait_recv()
        for z in range(self.layers):
            self.line[z] = self.wide[z, self.y] + self.from_side[z]
        for copy in self.along:
            copy.start()

    def add_line(self):
        mine = self.line[self.z].astype(F32)
        for step, copy in enumerate(self.along):
            copy.wait_recv()
            mine = mine + self.from_along[step].astype(F32)
        if self.cross:
            self.total[...] = mine
            self.spot[...] = mine
        else:
            self.own[...] = mine.astype(self.own.dtype)
        self.beyond.start()

    def add_x(self):
        self.beyond.wait_recv()
        if not self.cross:
            mine = self.own[...].astype(F32) + self.from_x[...].astype(F32)
            self.total[...] = mine
            self.spot[...] = mine
        self.back.start()

    def finish(self):
        self.back.wait_recv()
        copies = [self.inside, self.over, self.beyond, self.back] + self.along
        if self.cross:
            copies.append(self.over_x)
        for copy in copies:
            copy.wait_send()


def reduce_buffers(shape, dtype, cross):
    layers, sides = shape[:2]
    half = part_shape(shape[2:])
    last = part_shape(half) if cross else half
    buffers = [(layers, sides) + half] * 2
    if cross:
        buffers += [(layers, sides) + last] * 2
    buffers += [(layers,) + last] * 2 + [(layers - 1,) + last, last, last]
    return [pltpu.VMEM(buffer, dtype) for buffer in buffers] + [pltpu.VMEM(last, F32)]


def conv_backward_kernel(layers, *refs):
    quick = layers > 0
    take = iter(refs)
    tokens_t_hbm, keep_hbm, d_first_hbm, d_proj_hbm, d_proj_t_hbm = [next(take) for _ in range(5)]
    field_hbm, act_hbm, pull_hbm, expand_hbm, taps_ref, project_hbm = [next(take) for _ in range(6)]
    if quick:
        late_norm_ref = next(take)
        late = [next(take) for _ in range(3)]
    d_tokens_ref = next(take)
    if quick:
        results = [next(take) for _ in range(6)]
    else:
        g_expand_ref, g_project_ref, g_taps_ref = [next(take) for _ in range(3)]
    (d_image, field, act, pull, expand, project, load_sems) = [next(take) for _ in range(7)]
    (d_proj, d_proj_t, tokens_t, keep, taps_b, a_expand, a_project, a_taps) = [next(take) for _ in range(8)]
    frames = next(take)
    pairs, _, width = d_image.shape
    images = 2 * pairs
    chunks = field.shape[0] // 2
    hidden = chunks * CHUNK
    items = pairs * chunks
    per = pairs // 2

    if quick:
        stage_project, stage_small = next(take), next(take)
        stage_expand = [next(take) for _ in range(chunks)]
        mines = [next(take) for _ in range(3)]
        fetch_sems = next(take)
    loads = []
    for number, (source, target) in enumerate(
        (
            (d_proj_hbm, d_proj), (project_hbm, project), (d_proj_t_hbm, d_proj_t), (keep_hbm, keep),
            (tokens_t_hbm, tokens_t.at[0:pairs]), (d_first_hbm, d_image), (expand_hbm, expand),
        )
    ):
        loads.append(pltpu.make_async_copy(source, target, load_sems.at[number]))
    base = 7

    def stream(kind, chunk):
        source, target = ((act_hbm, act), (pull_hbm, pull), (field_hbm, field))[kind]
        two = pl.ds(2 * chunk, 2)
        return pltpu.make_async_copy(source.at[two], target.at[two], load_sems.at[base + kind * chunks + chunk])

    if quick:
        x, core, z, y = places(2)
        for index, (ref, mine) in enumerate(zip(late, mines)):
            pltpu.make_async_copy(part_of(ref, (slice(None), slice(None)), core), mine, fetch_sems.at[index]).start()
    for load in loads[:3]:
        load.start()
    for kind in range(3):
        stream(kind, 0).start()
    stream(0, 1).start()
    for load in loads[3:]:
        load.start()

    plan = {}
    if quick:
        number = 0
        rest = list(take)
        sems = rest[-2:]
        rest = rest[:-2]
        span = 3 + layers + 1

        def reducer(terms, mine, result, cross, fetch_sem=None):
            nonlocal number, rest
            count = 10 if cross else 8
            made = Reduce(terms, mine, result, cross, rest[:count], sems, number * span, fetch_sem)
            rest = rest[count:]
            number += 1
            return made

        mixed = reducer(late[0], mines[0], results[3], True, fetch_sems.at[0])
        up = reducer(late[1], mines[1], results[4], False, fetch_sems.at[1])
        down = reducer(late[2], mines[2], results[5], True, fetch_sems.at[2])
        whole_project = reducer(stage_project, None, results[2], True)
        parts = [
            reducer(stage_expand[c], None, results[1].at[:, c * CHUNK : (c + 1) * CHUNK], False) for c in range(chunks)
        ]
        small = reducer(stage_small, None, results[0], False)
        along, across, sibling, beyond = peers_of(layers)
        greet(along + [across, sibling, beyond])
        for part in (up, down, mixed):
            part.inside.start()

        def send_project():
            to_lines(a_project, stage_project)
            whole_project.start()

        def send_part(chunk):
            stage_expand[chunk][...] = a_expand[chunk].astype(BF16).reshape(stage_expand[chunk].shape)
            parts[chunk].start()

        def at(segment, *works):
            plan.setdefault(segment, []).extend(works)

        at(1, up.add_core, down.add_core, mixed.add_core)
        at(3, lambda: send_part(0))
        at(4, parts[0].add_core)
        at(5, up.add_side, down.add_cross, lambda: send_part(1))
        at(6, send_project, parts[1].add_core, parts[0].add_side)
        at(7, down.add_side, whole_project.add_core, lambda: send_part(2), parts[1].add_side)
        at(8, mixed.add_cross, up.add_line, parts[2].add_core)
        at(9, parts[0].add_line, parts[1].add_line, lambda: send_part(3), parts[2].add_side)
        at(10, mixed.add_side, down.add_line, up.add_x, parts[3].add_core)
        at(
            11, whole_project.add_cross, lambda: send_part(4), parts[0].add_x, parts[1].add_x, parts[2].add_line,
            parts[3].add_side,
        )

    a_taps[...] = jnp.zeros_like(a_taps)
    a_expand[...] = jnp.zeros_like(a_expand)
    a_project[...] = jnp.zeros_like(a_project)
    frames[...] = jnp.zeros_like(frames)
    tokens_t[pairs] = jnp.zeros((width, 2 * ROWS), BF16)
    spread_taps(taps_ref, taps_b)
    for load in loads:
        load.wait()

    def item(t):
        t = jnp.clip(t, 0, items - 1)
        return t // pairs, t % pairs

    def step(t, lead, new=True, old=True):
        c2, p2 = item(t - 2)
        c1, p1 = item(t - 1)
        c0, p0 = item(t)
        spot = pl.ds(pl.multiple_of(p2 * 2 * ROWS, 2 * ROWS), 2 * ROWS)
        done = both(act[2 * c2, spot, :], act[2 * c2 + 1, spot, :])
        a_expand[c2] += dot_nn(tokens_t[jnp.where(t < 2, pairs, p2)], done)
        if lead:
            cp, pp = t // 2, 2 * (t % 2)
            total = a_project[cp]
            for more in range(2):
                rows = pl.ds(pl.multiple_of((pp + more) * 2 * ROWS, 2 * ROWS), 2 * ROWS)
                total = total + dot_nn(d_proj_t[pp + more], both(act[2 * cp, rows, :], act[2 * cp + 1, rows, :]))
            a_project[cp] = total
        block = 64
        rows = block // GRID
        for half in range(CHUNK // 128 if old else 0):
            lanes = slice(half * 128, (half + 1) * 128)
            taps = [taps_b[c1, k, :, lanes] for k in range(9)]
            totals = [jnp.zeros((8, 128), F32) for _ in range(9)]
            for side in range(2):
                for start in range(0, ROWS, block):
                    spot = pl.ds(pl.multiple_of((2 * p1 + side) * ROWS, ROWS) + start, block)
                    own = field[2 * c1 + half, spot, :].reshape(rows, GRID, 128)
                    lines = []
                    for a in range(3):
                        line = None
                        for b in range(3):
                            k = 3 * a + b
                            at = start + GRID * (2 - a)
                            near = frames[side, b, half, at : at + block].reshape(rows, GRID, 128)
                            term = taps[k] * near
                            line = term if line is None else line + term
                            prod = near * own
                            quad = ((prod[0] + prod[1]) + (prod[2] + prod[3])).astype(F32)
                            totals[k] = totals[k] + (quad[:8] + quad[8:])
                        lines.append(line)
                    grad = (lines[0] + lines[1] + lines[2]).reshape(block, 128)
                    act[2 * c1 + half, spot, :] = grad * keep[2 * p1 + side, start : start + block, :]
            for k in range(9):
                a_taps[c1, 8 * k : 8 * k + 8, lanes] += totals[k]
        if not new:
            return
        d_act = dot_nt(d_proj[p0], project[c0])
        for half in range(CHUNK // 128):
            lanes = slice(half * 128, (half + 1) * 128)
            for side in range(2):
                spot = pl.ds(pl.multiple_of((2 * p0 + side) * ROWS, ROWS), ROWS)
                d_conv = d_act[side * ROWS : (side + 1) * ROWS, lanes] * pull[2 * c0 + half, spot, :].astype(F32)
                frames[side, 0, half, GRID : GRID + ROWS] = move_cells(d_conv, -1).astype(BF16)
                frames[side, 1, half, GRID : GRID + ROWS] = d_conv.astype(BF16)
                frames[side, 2, half, GRID : GRID + ROWS] = move_cells(d_conv, 1).astype(BF16)

    def segment(s, lead):
        for key in plan:
            @pl.when(s == key)
            def _(works=plan[key]):
                for work in works:
                    work()

        if lead:
            stream(0, s).wait()

            @pl.when(s < chunks - 2)
            def _():
                stream(0, s + 2).start()

        @pl.when(s % 2 == 0)
        def _():
            stream(1, s // 2).wait()
            stream(2, s // 2).wait()

            @pl.when(s // 2 < chunks - 1)
            def _():
                stream(1, s // 2 + 1).start()
                stream(2, s // 2 + 1).start()

        @pl.loop(0, per)
        def _(turn):
            step(s * per + turn, lead)

    middle_segment = chunks
    pl.loop(0, middle_segment)(lambda s: segment(s, True))
    pl.loop(middle_segment, 2 * chunks)(lambda s: segment(s, False))
    step(items, False, new=False)
    step(items + 1, False, new=False, old=False)

    def finish_pair(pair):
        spot = slice(2 * pair * ROWS, 2 * (pair + 1) * ROWS)
        left = jnp.concatenate([act[line, spot, :] for line in range(2 * chunks)], axis=1)
        right = jnp.concatenate([expand[chunk] for chunk in range(chunks)], axis=1)
        d_tokens_ref[spot, :] = (d_image[pair] + dot_nt(left, right)).astype(BF16)


    if not quick:
        for chunk in range(chunks):
            g_expand_ref[:, chunk * CHUNK : (chunk + 1) * CHUNK] = a_expand[chunk].astype(BF16)
            g_project_ref[chunk * CHUNK : (chunk + 1) * CHUNK, :] = a_project[chunk].astype(BF16).T
            g_taps_ref[:, chunk * CHUNK : (chunk + 1) * CHUNK] = a_taps[chunk]
        for pair in range(pairs):
            finish_pair(pair)
        return

    whole_project.add_side()
    send_part(chunks - 1)
    lines = []
    for k in range(9):
        line = jnp.concatenate([a_taps[c, 8 * k : 8 * k + 8, :] for c in range(chunks)], axis=1)
        lines.append(jnp.sum(line, axis=0, keepdims=True))
    depth = jnp.concatenate(lines, axis=0)
    vectors = [late_norm_ref[8 * k : 8 * k + 8] for k in (4, 5, 2, 3, 0, 1)]
    vectors = jnp.concatenate([jnp.sum(vector, axis=0, keepdims=True) for vector in vectors], axis=0)
    share, thin = hidden // (2 * layers), width // (2 * layers)
    stage_small[...] = jnp.zeros_like(stage_small)
    for f in range(2 * layers):
        stage_small[f // 2, f % 2, 0:9, 0:share] = depth[:, f * share : (f + 1) * share]
        stage_small[f // 2, f % 2, 9:15, 0:thin] = vectors[:, f * thin : (f + 1) * thin]
    small.start()
    finish_pair(0)
    parts[4].add_core()
    parts[5].add_core()
    small.add_core()
    parts[3].add_line()
    parts[2].add_x()
    down.add_x()
    finish_pair(1)
    parts[4].add_side()
    parts[5].add_side()
    small.add_side()
    mixed.add_line()
    finish_pair(2)
    whole_project.add_line()
    parts[4].add_line()
    parts[5].add_line()
    small.add_line()
    parts[3].add_x()
    mixed.add_x()
    finish_pair(3)
    whole_project.add_x()
    parts[4].add_x()
    parts[5].add_x()
    small.add_x()
    for part in [up, down, mixed, whole_project, small] + parts:
        part.finish()


def conv_backward(tokens_t, keep, d_first, d_proj, d_proj_t, field, act, pull, w_expand, taps, w_project, late=None):
    rows, width = d_first.shape
    chunks = w_expand.shape[0]
    hidden = chunks * CHUNK
    images = rows // ROWS
    anywhere = pl.BlockSpec(memory_space=pl.ANY)
    here = pl.BlockSpec(memory_space=pltpu.VMEM)
    pairs = images // 2
    by_pair = (pairs, 2 * ROWS, width)
    wide = (2 * chunks, rows, 128)
    scratch = [
        pltpu.VMEM(by_pair, F32),
        pltpu.VMEM(wide, BF16),
        pltpu.VMEM(wide, BF16),
        pltpu.VMEM(wide, BF16),
        pltpu.VMEM((chunks, width, CHUNK), BF16),
        pltpu.VMEM((chunks, CHUNK, width), BF16),
        pltpu.SemaphoreType.DMA((7 + chunks * 3,)),
        pltpu.VMEM((pairs, 2 * ROWS, width), BF16),
        pltpu.VMEM((pairs, width, 2 * ROWS), BF16),
        pltpu.VMEM((pairs + 1, width, 2 * ROWS), BF16),
        pltpu.VMEM((images, ROWS, 128), BF16),
        pltpu.VMEM((chunks, 9, GRID, CHUNK), BF16),
        pltpu.VMEM((chunks, width, CHUNK), F32),
        pltpu.VMEM((chunks, width, CHUNK), F32),
        pltpu.VMEM((chunks, 72, CHUNK), F32),
    ]
    scratch += [pltpu.VMEM((2, 3, 2, ROWS + 2 * GRID, 128), BF16)]
    operands = [
        tokens_t, keep.reshape(images, ROWS, 128), d_first.reshape(by_pair), d_proj.reshape(by_pair), d_proj_t,
        field, act, pull, w_expand, taps, w_project.reshape(chunks, CHUNK, width),
    ]
    in_specs = [anywhere] * 9 + [here, anywhere]
    d_tokens = jax.ShapeDtypeStruct((rows, width), BF16)
    if late is None:
        layers, params = 0, {}
        out_shape = [
            d_tokens,
            jax.ShapeDtypeStruct((width, hidden), BF16),
            jax.ShapeDtypeStruct(w_project.shape, BF16),
            jax.ShapeDtypeStruct((72, hidden), F32),
        ]
    else:
        g_norm, g_mixed, g_up, g_down = late
        layers = g_up.shape[0]
        params = dict(collective_id=1, has_side_effects=True)
        operands += [g_norm, g_mixed, g_up, g_down]
        in_specs += [here] + [anywhere] * 3
        span = -(-hidden // (2 * layers) // 128) * 128
        b_small, b_expand, b_project = (16, span), (width // (2 * layers), hidden), (hidden // (2 * layers), width)
        blocks = (b_small, b_expand, b_project, g_mixed.shape[2:], g_up.shape[2:], g_down.shape[2:])
        out_shape = [d_tokens] + [jax.ShapeDtypeStruct(block, F32) for block in blocks]
        lead = (layers, 2)
        piece = (b_expand[0], CHUNK)
        scratch += [pltpu.VMEM(lead + b_project, BF16), pltpu.VMEM(lead + b_small, F32)]
        scratch += [pltpu.VMEM(lead + piece, BF16)] * chunks
        scratch += [pltpu.VMEM(lead + part_shape(block), BF16) for block in blocks[3:]]
        scratch += [pltpu.SemaphoreType.DMA((3,))]
        for shape, dtype, cross in (
            [(blocks[3], BF16, True), (blocks[4], BF16, False), (blocks[5], BF16, True), (blocks[2], BF16, True)]
            + [(piece, BF16, False)] * chunks
            + [(b_small, F32, False)]
        ):
            scratch += reduce_buffers(lead + shape, dtype, cross)
        copies = (5 + chunks) * (4 + layers)
        scratch += [pltpu.SemaphoreType.DMA((copies,))] * 2
    return pl.pallas_call(
        functools.partial(conv_backward_kernel, layers),
        in_specs=in_specs,
        out_specs=[here] * len(out_shape),
        out_shape=out_shape,
        scratch_shapes=scratch,
        compiler_params=pltpu.CompilerParams(vmem_limit_bytes=VMEM_BYTES, **params),
        name="conv_backward",
    )(*operands)


def deliver_kernel(*refs):
    tokens_in, small_ref, *blocks = refs[:7]
    tokens_out, depth_ref, *rest = refs[7:]
    vectors, outs = rest[:6], rest[6:]
    expand, project, mixed, up, down = blocks
    cut = outs[2].shape[1]
    pairs = [(tokens_in, tokens_out), (expand, outs[0]), (project, outs[1])]
    pairs += [(mixed.at[:, :cut], outs[2]), (mixed.at[:, cut:], outs[3]), (up, outs[4]), (down, outs[5])]
    for source, target in pairs:
        target[...] = source[...]
    depth_ref[...] = small_ref[0 : depth_ref.shape[0], 0 : depth_ref.shape[1]]
    for line, ref in enumerate(vectors):
        ref[...] = small_ref[9 + line, 0 : ref.shape[0]]


def deliver(d_tokens, small, s_expand, s_project, s_mixed, s_up, s_down, share, thin):
    rows, width = s_mixed.shape[0], s_project.shape[1]
    here = pl.BlockSpec(memory_space=pltpu.VMEM)
    blocks = [s_expand.shape, s_project.shape, (rows, 3 * width), (rows, width), s_up.shape, s_down.shape]
    return pl.pallas_call(
        deliver_kernel,
        in_specs=[here] * 7,
        out_specs=[here] * 14,
        out_shape=[jax.ShapeDtypeStruct(d_tokens.shape, BF16), jax.ShapeDtypeStruct((9, share), F32)]
        + [jax.ShapeDtypeStruct((thin,), F32)] * 6
        + [jax.ShapeDtypeStruct(block, F32) for block in blocks],
        compiler_params=pltpu.CompilerParams(vmem_limit_bytes=VMEM_BYTES),
        name="deliver",
    )(d_tokens, small, s_expand, s_project, s_mixed, s_up, s_down)


def reduce_plain(terms):
    results = []
    for term in terms:
        share = lax.psum_scatter(term, "fsdp", scatter_dimension=0, tiled=False)
        results.append(lax.psum(share, "dp").astype(F32))
    return results


def local(
    fsdp, quick,
    tokens, grid, w_expand, w_depth, w_project, gain_conv, bias_conv, gain_attend, bias_attend,
    w_qkv, w_out, gain_mlp, bias_mlp, w_up, w_down, cotangent,
):
    slots, rows, width = tokens.shape
    hidden = w_expand.shape[1]
    share, thin = w_depth.shape[1], gain_conv.shape[0]
    span = -(-share // 128) * 128
    vectors = (gain_conv, bias_conv, gain_attend, bias_attend, gain_mlp, bias_mlp)
    grid = grid.T
    flat, cotan = tokens.reshape(slots * rows, width), cotangent.reshape(slots * rows, width)
    if quick:
        field, act, pull, projected, first, tokens_t, keep, taps, norms, *fulls = gather_forward(
            grid, flat, w_depth, vectors, w_expand, w_project, w_qkv, w_out, w_up, w_down, fsdp // 2
        )
        f_expand = fulls[0]
        f_project, f_mixed, f_up, f_down = [full.reshape(-1, full.shape[3]) for full in fulls[1:]]
    else:
        mixed = jnp.concatenate((w_qkv, w_out), axis=1)
        f_expand, f_project, f_mixed, f_up, f_down = [
            lax.all_gather(shard, "fsdp", axis=0, tiled=True) for shard in (w_expand, w_project, mixed, w_up, w_down)
        ]
        f_expand = f_expand.reshape(width, hidden // CHUNK, CHUNK).transpose(1, 0, 2)
        taps = jnp.pad(lax.all_gather(w_depth, "fsdp", axis=1, tiled=True).astype(F32), ((0, 7), (0, 0)))
        lines = lax.all_gather(jnp.stack(vectors), "fsdp", axis=1, tiled=True).astype(F32)
        norms = jnp.pad(lines, ((1, 1), (0, 0)))
        field, act, pull, projected, first, tokens_t, keep = conv_forward(
            grid, flat, f_expand, taps, f_project, norms
        )
    layer_out, d_first, d_proj, d_proj_t, g_norm, g_mixed, g_up, g_down = middle(
        grid, first, cotan, projected, f_mixed, f_up, f_down, norms
    )
    inputs = (tokens_t, keep, d_first, d_proj, d_proj_t, field, act, pull, f_expand, taps, f_project)
    if quick:
        late = [term.reshape((fsdp // 2, 2, -1, term.shape[1])) for term in (g_mixed, g_up, g_down)]
        d_tokens, small, s_expand, s_project, s_mixed, s_up, s_down = conv_backward(*inputs, late=[g_norm] + late)
    else:
        d_tokens, g_expand, g_project, g_taps = conv_backward(*inputs)
        g_taps = jnp.sum(g_taps.reshape(9, 8, fsdp, share), axis=1)
        g_norm = jnp.concatenate((g_norm[32:], g_norm[16:32], g_norm[:16]), axis=0)
        g_norm = jnp.sum(g_norm.reshape(6, 8, fsdp, thin), axis=1)
        g_small = jnp.concatenate(
            (
                jnp.pad(g_taps, ((0, 0), (0, 0), (0, span - share))),
                jnp.pad(g_norm, ((0, 1), (0, 0), (0, span - thin))),
            ),
            axis=0,
        ).transpose(1, 0, 2)
        terms = [g_small] + [
            term.reshape((fsdp, -1, term.shape[1])) for term in (g_expand, g_project, g_mixed, g_up, g_down)
        ]
        small, s_expand, s_project, s_mixed, s_up, s_down = reduce_plain(terms)
    d_tokens, depth, *rest = deliver(d_tokens, small, s_expand, s_project, s_mixed, s_up, s_down, share, thin)
    vectors, (s_expand, s_project, s_qkv, s_out, s_up, s_down) = rest[:6], rest[6:]
    return (
        layer_out.reshape(tokens.shape),
        d_tokens.reshape(tokens.shape),
        s_expand,
        depth,
        s_project,
        *vectors[:4],
        s_qkv,
        s_out,
        *vectors[4:],
        s_up,
        s_down,
    )


def solution(mesh):
    fsdp, dp = mesh.shape["fsdp"], mesh.shape["dp"]
    quick = fsdp == 8 and dp == 4
    images, wide, tall, vector = P(("dp", "fsdp"), None, None), P("fsdp", None), P(None, "fsdp"), P("fsdp")
    in_specs = (
        images, P(("dp", "fsdp"), None), wide, tall, wide, vector, vector, vector, vector,
        wide, wide, vector, vector, wide, wide, images,
    )
    out_specs = (
        images, images, wide, tall, wide, vector, vector, vector, vector,
        wide, wide, vector, vector, wide, wide,
    )
    return jax.shard_map(
        functools.partial(local, fsdp, quick), mesh=mesh, in_specs=in_specs, out_specs=out_specs, check_vma=False
    )
```

```python
import functools

import jax
import jax.numpy as jnp
from jax import lax
from jax.experimental import pallas as pl
from jax.experimental.pallas import tpu as pltpu
from jax.sharding import PartitionSpec as P

HDIM = 64
GRID = 16
ROWS = GRID * GRID
CHUNK = 256
EPSILON = 1e-05
VMEM_BYTES = 62 * 1024 * 1024
F32 = jnp.float32
BF16 = jnp.bfloat16


def dot_nn(left, right):
    return jnp.dot(left, right, preferred_element_type=F32)


def dot_nt(left, right):
    return lax.dot_general(left, right, (((1,), (1,)), ((), ())), preferred_element_type=F32)


def dot_tn(left, right):
    return lax.dot_general(left, right, (((0,), (0,)), ((), ())), preferred_element_type=F32)


def valid_cells(high, wide, shape):
    place = lax.broadcasted_iota(jnp.int32, shape, 0)
    return (place // GRID < high) & (place % GRID < wide)


def normalized(values):
    center = jnp.mean(values, axis=-1, keepdims=True)
    shifted = values - center
    spread = jnp.mean(shifted * shifted, axis=-1, keepdims=True)
    inverse = lax.rsqrt(spread + EPSILON)
    return shifted * inverse, inverse


def norm_pull(grad, gain, unit, inverse):
    scaled = grad * gain
    mean_plain = jnp.mean(scaled, axis=-1, keepdims=True)
    mean_unit = jnp.mean(scaled * unit, axis=-1, keepdims=True)
    return (scaled - mean_plain - unit * mean_unit) * inverse


def both(left, right):
    return jnp.concatenate((left, right), axis=1)


def fold_rows(values):
    rows, width = values.shape
    return jnp.sum(values.reshape(rows // 8, 8, width), axis=0)


def move_cells(values, step):
    rows, width = values.shape
    parts = values.reshape(rows // GRID, 2, 8, width)
    turned = pltpu.roll(parts, step % 8, axis=2)
    first, last = turned[:, 0:1], turned[:, 1:2]
    line = lax.broadcasted_iota(jnp.int32, first.shape, 2)
    if step == 1:
        edge = line == 0
        moved = jnp.concatenate((jnp.where(edge, 0.0, first), jnp.where(edge, first, last)), axis=1)
    else:
        edge = line == 7
        moved = jnp.concatenate((jnp.where(edge, last, first), jnp.where(edge, 0.0, last)), axis=1)
    return moved.reshape(rows, width)


MESH = pl.DeviceIdType.MESH


def places(sides):
    dp, fsdp = lax.axis_index("dp"), lax.axis_index("fsdp")
    return dp // 2, dp % 2, fsdp // sides, fsdp % sides


def part_of(ref, lead, index, count=2):
    rows, columns = ref.shape[-2:]
    if columns > rows * 4:
        size = columns // count
        return ref.at[lead + (slice(None), pl.ds(pl.multiple_of(index * size, size), size))]
    size = rows // count
    return ref.at[lead + (pl.ds(pl.multiple_of(index * size, size), size), slice(None))]


def part_shape(shape, count=2):
    rows, columns = shape
    return (rows, columns // count) if columns > rows * 4 else (rows // count, columns)


def remote(source, target, sends, receives, index, device):
    return pltpu.make_async_remote_copy(
        src_ref=source,
        dst_ref=target,
        send_sem=sends.at[index],
        recv_sem=receives.at[index],
        device_id=device,
        device_id_type=MESH,
    )


def greet(devices):
    barrier = pltpu.get_barrier_semaphore()
    for device in devices:
        pl.semaphore_signal(barrier, inc=1, device_id=device, device_id_type=MESH)
    pl.semaphore_wait(barrier, len(devices))


def peers_of(layers):
    x, core, z, y = places(2)
    dp, fsdp = x * 2 + core, z * 2 + y
    along = [(dp, (z ^ step) * 2 + y) for step in range(1, layers)]
    return along, (dp, z * 2 + 1 - y), (x * 2 + 1 - core, fsdp), ((1 - x) * 2 + core, fsdp)


class Gather:
    def __init__(self, shard, full, cross, sems, number):
        sends, receives, locals_ = sems
        self.full, self.cross, self.layers = full, cross, full.shape[0]
        self.x, self.core, self.z, self.y = places(2)
        along, across, sibling, beyond = peers_of(self.layers)
        base = number * (2 * self.layers + 3)
        own = self.piece(shard, ())
        spot = self.piece(full, (self.z, self.y))
        self.local = pltpu.make_async_copy(own, spot, locals_.at[number])
        self.along = [remote(own, spot, sends, receives, base + step, device) for step, device in enumerate(along)]
        base += self.layers - 1
        self.over = []
        for step in range(self.layers):
            target = self.piece(full, (self.z ^ step, self.y))
            self.over.append(remote(own if step == 0 else target, target, sends, receives, base + step, across))
        base += self.layers
        self.beyond, self.inside = [], []
        for step, side in enumerate((self.y, 1 - self.y)):
            half = part_of(full, (slice(None), side), self.core)
            self.inside.append(remote(half, half, sends, receives, base + step, sibling))
            if cross:
                target = self.piece(full, (slice(None), side))
                self.beyond.append(remote(target, target, sends, receives, base + 2 + step, beyond))

    def piece(self, ref, lead):
        half = part_of(ref, lead, self.core)
        return part_of(half, (slice(None),) * (len(half.shape) - 2), self.x) if self.cross else half

    def start(self):
        for copy in self.along:
            copy.start()
        self.over[0].start()
        self.local.start()

    def forward(self):
        for step, copy in enumerate(self.along):
            copy.wait_recv()
            self.over[step + 1].start()
        self.local.wait()
        (self.beyond if self.cross else self.inside)[0].start()

    def side(self):
        for copy in self.over:
            copy.wait_recv()
        (self.beyond if self.cross else self.inside)[1].start()

    def share(self):
        for copy, after in zip(self.beyond, self.inside):
            copy.wait_recv()
            after.start()

    def finish(self):
        for copy in self.inside:
            copy.wait_recv()

    def drain(self):
        for copy in self.along + self.over + self.beyond + self.inside:
            copy.wait_send()


class Spread:
    def __init__(self, block, full, sems, base):
        sends, receives, local = sems
        layers = full.shape[0]
        x, core, z, y = places(2)
        spot = full.at[z, y]
        self.local = pltpu.make_async_copy(block, spot, local)
        self.copies = [
            remote(block, spot, sends, receives, base + 2 * up + over - 1, (x * 2 + core, (z ^ up) * 2 + (y ^ over)))
            for up in range(layers)
            for over in range(2)
            if up + over > 0
        ]

    def start(self):
        for copy in self.copies:
            copy.start()
        self.local.start()

    def finish(self):
        for copy in self.copies:
            copy.wait_recv()
        self.local.wait()

    def drain(self):
        for copy in self.copies:
            copy.wait_send()


def spread_taps(taps_ref, taps_b):
    for chunk in range(taps_b.shape[0]):
        for k in range(9):
            line = taps_ref[k : k + 1, chunk * CHUNK : (chunk + 1) * CHUNK]
            taps_b[chunk, k] = jnp.broadcast_to(line, (GRID, CHUNK)).astype(BF16)


def conv_chunk(chunk, kept, weights, taps_ref, frames, field_ref, act_ref, pull_ref, acts, slot):
    expanded = dot_nn(kept, weights)
    block = 64
    for half in range(CHUNK // 128):
        lanes = slice(half * 128, (half + 1) * 128)
        field_ref[chunk * 2 + half] = expanded[:, lanes].astype(BF16)
        frames[chunk % 2, half, GRID : GRID + ROWS] = expanded[:, lanes]
        whole = slice(chunk * CHUNK + half * 128, chunk * CHUNK + (half + 1) * 128)
        taps = [taps_ref[k : k + 1, whole] for k in range(9)]
        for start in range(0, ROWS, block):
            near = [frames[chunk % 2, half, start + GRID * a : start + GRID * a + block] for a in range(3)]
            sums = [sum(taps[3 * a + b] * near[a] for a in range(3)) for b in range(3)]
            conv = sums[1] + move_cells(sums[0], 1) + move_cells(sums[2], -1)
            gate = 0.5 * jnp.tanh(0.5 * conv) + 0.5
            act = conv * gate
            low = act.astype(BF16)
            act_ref[chunk * 2 + half, start : start + block] = low
            acts[slot, chunk * 2 + half, start : start + block] = low
            pull_ref[chunk * 2 + half, start : start + block] = (gate + act * (1.0 - gate)).astype(BF16)


def project_chunks(chunk, acts, slot, project):
    left = jnp.concatenate([acts[slot, 2 * chunk + part] for part in range(4)], axis=1)
    return dot_nn(left, project[chunk * CHUNK : (chunk + 2) * CHUNK, :])


def end_forward(projected, tokens, valid, norms_ref, projected_ref, first_ref):
    projected_ref[...] = projected
    unit, _ = normalized(projected)
    shift = unit * norms_ref[1:2, :] + norms_ref[2:3, :]
    first_ref[...] = tokens.astype(F32) + jnp.where(valid, shift, 0.0)


def conv_forward_body(
    step, before, middle_of_first, grid_ref, tokens_ref, late_tokens_ref, weights, project, norms_ref, taps_ref,
    field_ref, act_ref, pull_ref, projected_ref, first_ref, tokens_t_ref, keep_ref, frames, acts,
):
    width = tokens_ref.shape[1]
    chunks = weights.shape[0]
    images = pl.num_programs(0) - 2
    slot = lax.rem(step, 2)

    def start_image():
        valid = valid_cells(grid_ref[0, step], grid_ref[1, step], (ROWS, width))
        tokens = tokens_ref[...]
        tokens_t_ref[0] = tokens.T
        keep_ref[...] = jnp.where(valid[:, :128], 1.0, 0.0).astype(BF16)
        return jnp.where(valid, tokens, jnp.zeros_like(tokens))

    def convolve(chunk, kept):
        conv_chunk(chunk, kept, weights[chunk], taps_ref, frames, field_ref, act_ref, pull_ref, acts, slot)

    def end_image(projected):
        high, wide = grid_ref[0, step - 2], grid_ref[1, step - 2]
        valid = valid_cells(high, wide, (ROWS, width))
        end_forward(projected, late_tokens_ref[...], valid, norms_ref, projected_ref, first_ref)

    @pl.when(step == 0)
    def _():
        before()
        frames[...] = jnp.zeros_like(frames)
        kept = start_image()
        for chunk in range(chunks):
            middle_of_first(chunk)
            convolve(chunk, kept)

    @pl.when(step == 1)
    def _():
        kept = start_image()
        for chunk in range(chunks):
            convolve(chunk, kept)

    @pl.when((step > 1) & (step < images))
    def _():
        kept = start_image()
        projected = jnp.zeros((ROWS, width), F32)
        for chunk in range(0, chunks, 2):
            projected = projected + project_chunks(chunk, acts, slot, project)
            convolve(chunk, kept)
            convolve(chunk + 1, kept)
        end_image(projected)

    @pl.when(step >= images)
    def _():
        projected = jnp.zeros((ROWS, width), F32)
        for chunk in range(0, chunks, 2):
            projected = projected + project_chunks(chunk, acts, slot, project)
        end_image(projected)


def conv_forward_kernel(
    grid_ref, tokens_ref, late_tokens_ref, weights, taps_ref, project_ref, norms_ref,
    field_ref, act_ref, pull_ref, projected_ref, first_ref, tokens_t_ref, keep_ref, frames, acts,
):
    conv_forward_body(
        pl.program_id(0), lambda: None, lambda chunk: None,
        grid_ref, tokens_ref, late_tokens_ref, weights, project_ref, norms_ref, taps_ref,
        field_ref, act_ref, pull_ref, projected_ref, first_ref, tokens_t_ref, keep_ref, frames, acts,
    )


def gather_forward_kernel(
    grid_ref, tokens_ref, late_tokens_ref, depth_ref, gain1_ref, bias1_ref, gain2_ref, bias2_ref, gain3_ref, bias3_ref,
    s_expand, s_project, s_qkv, s_out, s_up, s_down,
    field_ref, act_ref, pull_ref, projected_ref, first_ref, tokens_t_ref, keep_ref,
    taps_ref, norms_ref, f_expand, f_project, f_mixed, f_up, f_down,
    frames, acts, weights, v_expand, v_project, v_small, own_small, own_mixed, sends, receives, locals_,
):
    step = pl.program_id(0)
    last = pl.num_programs(0) - 1
    sems = (sends, receives, locals_)
    layers = v_small.shape[0]
    hidden, width = taps_ref.shape[1], tokens_ref.shape[1]
    wide = v_expand.shape[-1]
    pieces = v_expand.shape[0]
    expand = [
        Gather(s_expand.at[:, piece * wide : (piece + 1) * wide], v_expand.at[piece], True, sems, piece)
        for piece in range(pieces)
    ]
    project = Gather(s_project, v_project, False, sems, pieces)
    mixed = Gather(own_mixed, f_mixed, True, sems, pieces + 1)
    up = Gather(s_up, f_up, True, sems, pieces + 2)
    down = Gather(s_down, f_down, False, sems, pieces + 3)
    count = pieces + 4
    small = Spread(own_small, v_small, (sends, receives, locals_.at[count]), count * (2 * layers + 3))
    share, thin = depth_ref.shape[1], gain1_ref.shape[0]
    cut = s_qkv.shape[1]
    joins = [
        pltpu.make_async_copy(s_qkv, own_mixed.at[:, :cut], locals_.at[count + 1]),
        pltpu.make_async_copy(s_out, own_mixed.at[:, cut:], locals_.at[count + 2]),
    ]
    save_expand = pltpu.make_async_copy(weights, f_expand, locals_.at[count + 3])
    save_project = pltpu.make_async_copy(v_project, f_project, locals_.at[count + 4])

    @pl.when(step == 0)
    def _():
        for join in joins:
            join.start()
        own_small[...] = jnp.zeros_like(own_small)
        own_small[0:9, 0:share] = depth_ref[...].astype(F32)
        for line, ref in enumerate((gain1_ref, bias1_ref, gain2_ref, bias2_ref, gain3_ref, bias3_ref)):
            own_small[9 + line : 10 + line, 0:thin] = ref[...].astype(F32).reshape(1, thin)
        x, core, z, y = places(2)
        _, _, sibling, beyond = peers_of(layers)
        others = [
            (x * 2 + core, (z ^ more) * 2 + (y ^ over)) for more in range(layers) for over in range(2) if more + over > 0
        ]
        greet(others + [sibling, beyond])
        for part in expand:
            part.start()
        small.start()

    def before():
        for join in joins:
            join.wait()
        for part in expand:
            part.forward()
        project.start()
        small.finish()
        blocks = [v_small[z, y] for z in range(layers) for y in range(2)]
        taps_ref[...] = jnp.concatenate([block[:, :share] for block in blocks], axis=1)
        norms_ref[...] = jnp.concatenate([block[8:, :thin] for block in blocks], axis=1)
        for part in expand:
            part.side()
        mixed.start()

    def middle_of_first(chunk):
        per = wide // CHUNK
        piece, place = chunk // per, chunk % per
        if place == 0:
            expand[piece].share()
            expand[piece].finish()
        weights[chunk] = v_expand[piece, :, :, :, place * CHUNK : (place + 1) * CHUNK].reshape(width, CHUNK)

    def at(number, *works):
        @pl.when(step == number)
        def _():
            for work in works:
                work()

    at(1, project.forward, save_expand.start, up.start)
    at(2, project.side, project.finish, save_project.start, mixed.forward, down.start)
    at(3, mixed.side, up.forward)
    at(4, up.side)
    at(5, mixed.share, down.forward)
    at(6, down.side)
    at(7, up.share)

    conv_forward_body(
        step, before, middle_of_first,
        grid_ref, tokens_ref, late_tokens_ref, weights, v_project.reshape(hidden, width), norms_ref, taps_ref,
        field_ref, act_ref, pull_ref, projected_ref, first_ref, tokens_t_ref, keep_ref, frames, acts,
    )

    @pl.when(step == last)
    def _():
        for part in (mixed, up, down):
            part.finish()
        for part in expand + [small, project, mixed, up, down]:
            part.drain()
        save_expand.wait()
        save_project.wait()


def whole(shape):
    return pl.BlockSpec(shape, lambda *_: (0,) * len(shape), pipeline_mode=pl.Buffered(1))


def forward_specs(rows, width, hidden):
    images, chunks = rows // ROWS, hidden // CHUNK
    here = lambda i: jnp.minimum(i, images - 1)
    late = lambda i: jnp.maximum(i - 2, 0)
    by_image = pl.BlockSpec((ROWS, width), lambda i: (here(i), 0))
    by_late = pl.BlockSpec((ROWS, width), lambda i: (late(i), 0))
    by_chunk = pl.BlockSpec((2 * chunks, ROWS, 128), lambda i: (0, here(i), 0))
    turned = pl.BlockSpec((1, width, ROWS), lambda i: (here(i) // 2, 0, here(i) % 2))
    cells = pl.BlockSpec((ROWS, 128), lambda i: (here(i), 0))
    wide = jax.ShapeDtypeStruct((2 * chunks, rows, 128), BF16)
    tall = jax.ShapeDtypeStruct((rows, width), F32)
    return (
        [pl.BlockSpec(memory_space=pltpu.SMEM), by_image, by_late],
        [by_chunk, by_chunk, by_chunk, by_late, by_late, turned, cells],
        [
            wide, wide, wide, tall, tall,
            jax.ShapeDtypeStruct((images // 2, width, 2 * ROWS), BF16), jax.ShapeDtypeStruct((rows, 128), BF16),
        ],
        [
            pltpu.VMEM((2, 2, ROWS + 2 * GRID, 128), F32),
            pltpu.VMEM((2, 2 * chunks, ROWS, 128), BF16),
        ],
    )


def conv_forward(grid, tokens, w_expand, taps, w_project, norms):
    rows, width = tokens.shape
    in_specs, out_specs, out_shape, scratch = forward_specs(rows, width, taps.shape[1])
    return pl.pallas_call(
        conv_forward_kernel,
        grid=(rows // ROWS + 2,),
        in_specs=in_specs + [whole(w_expand.shape), whole(taps.shape), whole(w_project.shape), whole(norms.shape)],
        out_specs=out_specs,
        out_shape=out_shape,
        scratch_shapes=scratch,
        compiler_params=pltpu.CompilerParams(vmem_limit_bytes=VMEM_BYTES),
        name="conv_forward",
    )(grid, tokens, tokens, w_expand, taps, w_project, norms)


def gather_forward(grid, tokens, w_depth, vectors, w_expand, w_project, w_qkv, w_out, w_up, w_down, layers):
    rows, width = tokens.shape
    hidden = w_expand.shape[1]
    chunks = hidden // CHUNK
    in_specs, out_specs, out_shape, scratch = forward_specs(rows, width, hidden)
    anywhere = pl.BlockSpec(memory_space=pl.ANY)
    here = pl.BlockSpec(memory_space=pltpu.VMEM)
    span = -(-w_depth.shape[1] // 128) * 128
    mixed = (w_qkv.shape[0], w_qkv.shape[1] + w_out.shape[1])
    pieces = 3
    lead = (layers, 2)
    fulls = [(chunks, width, CHUNK)] + [lead + shape for shape in (w_project.shape, mixed, w_up.shape, w_down.shape)]
    copies = (pieces + 4) * (2 * layers + 3) + 2 * layers
    return pl.pallas_call(
        gather_forward_kernel,
        grid=(rows // ROWS + 2,),
        in_specs=in_specs + [here] * 7 + [anywhere] * 6,
        out_specs=out_specs + [whole((16, hidden)), whole((8, width))] + [anywhere] * 5,
        out_shape=out_shape
        + [jax.ShapeDtypeStruct((16, hidden), F32), jax.ShapeDtypeStruct((8, width), F32)]
        + [jax.ShapeDtypeStruct(full, BF16) for full in fulls],
        scratch_shapes=scratch
        + [
            pltpu.VMEM((chunks, width, CHUNK), BF16),
            pltpu.VMEM((pieces,) + lead + (w_expand.shape[0], hidden // pieces), BF16),
            pltpu.VMEM(fulls[1], BF16),
            pltpu.VMEM(lead + (16, span), F32),
            pltpu.VMEM((16, span), F32),
            pltpu.VMEM(mixed, BF16),
            pltpu.SemaphoreType.DMA((copies,)),
            pltpu.SemaphoreType.DMA((copies,)),
            pltpu.SemaphoreType.DMA((pieces + 9,)),
        ],
        compiler_params=pltpu.CompilerParams(
            vmem_limit_bytes=VMEM_BYTES, collective_id=0, has_side_effects=True
        ),
        name="gather_forward",
    )(grid, tokens, tokens, w_depth, *vectors, w_expand, w_project, w_qkv, w_out, w_up, w_down)


def heads_apart(pair):
    lane = lax.broadcasted_iota(jnp.int32, pair.shape, 1) // HDIM
    zero = jnp.zeros_like(pair)
    return jnp.concatenate((jnp.where(lane == 0, pair, zero), jnp.where(lane == 1, pair, zero)), axis=0)


def middle_kernel(*refs):
    take = iter(refs)
    grid_ref, first_ref, cotan_ref, projected_ref, norms_ref = [next(take) for _ in range(5)]
    mixed_hbm, up_hbm, down_hbm = [next(take) for _ in range(3)]
    layer_ref, d_first_ref, d_proj_ref, d_proj_t_ref, g_norm_ref, g_mixed_ref = [next(take) for _ in range(6)]
    g_up_ref, g_down_ref = next(take), next(take)
    w_qkv, w_out, w_up, w_down, load_sems = [next(take) for _ in range(5)]
    a_qkv, a_out, a_up, a_down = [next(take) for _ in range(4)]
    firsts, seconds, normeds, queries, keys, values, expo, inverses, attended, d_qkv = [next(take) for _ in range(10)]
    step = pl.program_id(0)
    pairs = firsts.shape[0]
    width = firsts.shape[2]
    chunks = w_up.shape[0]
    hidden = chunks * CHUNK
    blocks = width // 128
    cut = 3 * width

    loads = [
        pltpu.make_async_copy(mixed_hbm.at[:, :cut], w_qkv, load_sems.at[0]),
        pltpu.make_async_copy(mixed_hbm.at[:, cut:], w_out, load_sems.at[1]),
    ]
    loads.append(pltpu.make_async_copy(down_hbm, w_down, load_sems.at[2]))
    for chunk in range(chunks):
        source = up_hbm.at[:, chunk * CHUNK : (chunk + 1) * CHUNK]
        loads.append(pltpu.make_async_copy(source, w_up.at[chunk], load_sems.at[3 + chunk]))

    @pl.when(step == 0)
    def _():
        for load in loads:
            load.start()
        for ref in (a_qkv, a_out, a_up, a_down, g_norm_ref):
            ref[...] = jnp.zeros_like(ref)
        for load in loads[:2]:
            load.wait()

    @pl.when(step == pairs)
    def _():
        for load in loads[2:]:
            load.wait()

    def sizes(pair, side):
        return grid_ref[0, 2 * pair + side], grid_ref[1, 2 * pair + side]

    def valid_pair(pair):
        return jnp.concatenate([valid_cells(*sizes(pair, side), (ROWS, width)) for side in range(2)], axis=0)

    def forward(pair):
        first = first_ref[...]
        firsts[pair] = first
        unit, _ = normalized(first)
        normed = (unit * norms_ref[3:4, :] + norms_ref[4:5, :]).astype(BF16)
        normeds[pair] = normed
        packed = dot_nn(normed, w_qkv[...]).astype(BF16)
        line = lax.broadcasted_iota(jnp.int32, (128, ROWS), 0) // HDIM
        biases = [jnp.where(valid_cells(*sizes(pair, side), (ROWS, ROWS)), 0.0, -1e9) for side in range(2)]
        units = [(side, block) for side in range(2) for block in range(blocks)]

        def score(side, block):
            image, lines = 2 * pair + side, slice(side * ROWS, (side + 1) * ROWS)
            query = packed[lines, block * 128 : (block + 1) * 128] * jnp.asarray(HDIM**-0.5, BF16)
            key = packed[lines, width + block * 128 : width + (block + 1) * 128]
            value = packed[lines, 2 * width + block * 128 : 2 * width + (block + 1) * 128]
            queries[image, block], keys[image, block], values[image, block] = query, key, value
            return dot_nt(heads_apart(key), query), heads_apart(value)

        ahead = score(*units[0])
        for number, (side, block) in enumerate(units):
            scores, value = ahead
            if number + 1 < len(units):
                ahead = score(*units[number + 1])
            image = 2 * pair + side
            columns = slice(block * 128, (block + 1) * 128)
            totals, powers = [], []
            for head in range(2):
                rows = slice(head * ROWS, (head + 1) * ROWS)
                part = scores[rows] + biases[side]
                power = jnp.exp(part - jnp.max(part, axis=0, keepdims=True))
                totals.append(1.0 / jnp.sum(power, axis=0, keepdims=True))
                powers.append(power.astype(BF16))
                expo[image, block, rows] = powers[-1]
            inverse = jnp.where(line == 0, totals[0], totals[1])
            inverses[image, block] = inverse
            attended[image, columns] = (dot_tn(value, jnp.concatenate(powers, axis=0)) * inverse).astype(BF16)
            if block == blocks - 1:
                lines = slice(side * ROWS, (side + 1) * ROWS)
                valid = valid_cells(*sizes(pair, side), (ROWS, width))
                seconds[pair, lines] = first[lines] + jnp.where(valid, dot_tn(attended[image], w_out[...]), 0.0)

    def feed(pair):
        valid = valid_pair(pair)
        second, cotan = seconds[pair], cotan_ref[...]
        unit, inverse = normalized(second)
        normed = (unit * norms_ref[5:6, :] + norms_ref[6:7, :]).astype(BF16)
        d_down = jnp.where(valid, cotan, jnp.zeros_like(cotan))
        normed_t, d_down_t = normed.T, d_down.T
        result = jnp.zeros((2 * ROWS, width), F32)
        d_normed = jnp.zeros((2 * ROWS, width), F32)

        def begin(chunk):
            lines = w_down[chunk * CHUNK : (chunk + 1) * CHUNK, :]
            return dot_nn(normed, w_up[chunk]), dot_nt(d_down, lines), lines

        ahead = begin(0)
        for chunk in range(chunks):
            upper, d_hidden, lines = ahead
            if chunk + 1 < chunks:
                ahead = begin(chunk + 1)
            square = upper * upper
            bent = jnp.tanh(upper * (0.7978845608028654 + (0.7978845608028654 * 0.044715) * square))
            gate = 0.5 * bent + 0.5
            hid = (upper * gate).astype(BF16)
            slope = gate + upper * (gate - gate * gate) * (
                2 * 0.7978845608028654 + (6 * 0.7978845608028654 * 0.044715) * square
            )
            d_upper = (d_hidden * slope).astype(BF16)
            result = result + dot_nn(hid, lines)
            a_down[chunk] += dot_nn(d_down_t, hid)
            a_up[chunk] += dot_nn(normed_t, d_upper)
            d_normed = d_normed + dot_nt(d_upper, w_up[chunk])
        layer_ref[...] = (second + jnp.where(valid, result, 0.0)).astype(BF16)
        g_norm_ref[0:8] += fold_rows(d_normed * unit)
        g_norm_ref[8:16] += fold_rows(d_normed)
        seconds[pair] = cotan.astype(F32) + norm_pull(d_normed, norms_ref[5:6, :], unit, inverse)

    def backward(pair):
        valid = valid_pair(pair)
        d_second = seconds[pair]
        d_out = jnp.where(valid, d_second, 0.0).astype(BF16)
        a_out[...] += dot_nn(both(attended[2 * pair], attended[2 * pair + 1]), d_out)
        line = lax.broadcasted_iota(jnp.int32, (128, ROWS), 0) // HDIM
        units = [(side, block) for side in range(2) for block in range(blocks)]

        def probe(side, block):
            image, lines = 2 * pair + side, slice(side * ROWS, (side + 1) * ROWS)
            columns = slice(block * 128, (block + 1) * 128)
            d_low = dot_nt(w_out[columns, :], d_out[lines]).astype(BF16).astype(F32)
            scaled = d_low * inverses[image, block]
            low = scaled.astype(BF16)
            inner = scaled * attended[image, columns].astype(F32)
            return low, inner, dot_nn(heads_apart(values[image, block]), low)

        ahead = probe(*units[0])
        for number, (side, block) in enumerate(units):
            low, inner, d_probs = ahead
            if number + 1 < len(units):
                ahead = probe(*units[number + 1])
            image, lines = 2 * pair + side, slice(side * ROWS, (side + 1) * ROWS)
            query = heads_apart(queries[image, block])
            d_value = jnp.zeros((ROWS, 128), F32)
            d_key = jnp.zeros((ROWS, 128), F32)
            steps = []
            for head in range(2):
                rows = slice(head * ROWS, (head + 1) * ROWS)
                delta = jnp.sum(inner[head * HDIM : (head + 1) * HDIM], axis=0, keepdims=True)
                power = expo[image, block, rows]
                d_score = (power.astype(F32) * (d_probs[rows] - delta)).astype(BF16)
                steps.append(d_score)
                own = jnp.where(line == head, low, jnp.zeros_like(low))
                d_value = d_value + dot_nt(power, own)
                d_key = d_key + dot_nn(d_score, query[rows])
            d_query_t = dot_tn(heads_apart(keys[image, block]), jnp.concatenate(steps, axis=0)) * (HDIM**-0.5)
            d_qkv[lines, block * 128 : (block + 1) * 128] = d_query_t.astype(BF16).T
            d_qkv[lines, width + block * 128 : width + (block + 1) * 128] = d_key.astype(BF16)
            d_qkv[lines, 2 * width + block * 128 : 2 * width + (block + 1) * 128] = d_value.astype(BF16)
        a_qkv[...] += dot_nn(normeds[pair].T, d_qkv[...])
        d_normed = dot_nt(d_qkv[...], w_qkv[...])
        unit, inverse = normalized(firsts[pair])
        g_norm_ref[16:24] += fold_rows(d_normed * unit)
        g_norm_ref[24:32] += fold_rows(d_normed)
        d_first = d_second + norm_pull(d_normed, norms_ref[3:4, :], unit, inverse)
        d_first_ref[...] = d_first
        unit, inverse = normalized(projected_ref[...])
        grad = jnp.where(valid, d_first, 0.0)
        g_norm_ref[32:40] += fold_rows(grad * unit)
        g_norm_ref[40:48] += fold_rows(grad)
        low = norm_pull(grad, norms_ref[1:2, :], unit, inverse).astype(BF16)
        d_proj_ref[...] = low
        d_proj_t_ref[0] = low.T

    pl.when(step < pairs)(lambda: forward(step))
    pl.when((step >= pairs) & (step < 2 * pairs))(lambda: feed(step - pairs))
    pl.when(step >= 2 * pairs)(lambda: backward(step - 2 * pairs))

    @pl.when(step == 3 * pairs - 1)
    def _():
        g_mixed_ref[:, :cut] = a_qkv[...].astype(BF16)
        g_mixed_ref[:, cut:] = a_out[...].astype(BF16)
        to_lines(a_down, g_down_ref.reshape(1, 1, hidden, width))
        for chunk in range(chunks):
            g_up_ref[:, chunk * CHUNK : (chunk + 1) * CHUNK] = a_up[chunk].astype(BF16)


def to_lines(blocks, target):
    layers, sides, share = target.shape[:3]
    for chunk in range(blocks.shape[0]):
        lines = blocks[chunk].astype(BF16).T
        for f in range(layers * sides):
            low, high = max(f * share, chunk * CHUNK), min((f + 1) * share, (chunk + 1) * CHUNK)
            if low < high:
                target[f // sides, f % sides, low - f * share : high - f * share] = lines[
                    low - chunk * CHUNK : high - chunk * CHUNK
                ]


def middle(grid, first, cotangent, projected, w_mixed, w_up, w_down, norms):
    rows, width = first.shape
    pairs, blocks = rows // (2 * ROWS), width // 128
    images = 2 * pairs
    hidden = w_up.shape[1]
    chunks = hidden // CHUNK
    cut = 3 * width

    def phase(number):
        return pl.BlockSpec((2 * ROWS, width), lambda i: (jnp.clip(i - number * pairs, 0, pairs - 1), 0))

    turned = pl.BlockSpec((1, width, 2 * ROWS), lambda i: (jnp.clip(i - 2 * pairs, 0, pairs - 1), 0, 0))
    anywhere = pl.BlockSpec(memory_space=pl.ANY)
    full_up, full_down = (width, hidden), (hidden, width)
    scratch = [
        pltpu.VMEM((width, cut), BF16),
        pltpu.VMEM((width, width), BF16),
        pltpu.VMEM((chunks, width, CHUNK), BF16),
        pltpu.VMEM(full_down, BF16),
        pltpu.SemaphoreType.DMA((3 + chunks,)),
        pltpu.VMEM((width, cut), F32),
        pltpu.VMEM((width, width), F32),
        pltpu.VMEM((chunks, width, CHUNK), F32),
        pltpu.VMEM((chunks, width, CHUNK), F32),
        pltpu.VMEM((pairs, 2 * ROWS, width), F32),
        pltpu.VMEM((pairs, 2 * ROWS, width), F32),
        pltpu.VMEM((pairs, 2 * ROWS, width), BF16),
        pltpu.VMEM((images, blocks, ROWS, 128), BF16),
        pltpu.VMEM((images, blocks, ROWS, 128), BF16),
        pltpu.VMEM((images, blocks, ROWS, 128), BF16),
        pltpu.VMEM((images, blocks, 2 * ROWS, ROWS), BF16),
        pltpu.VMEM((images, blocks, 128, ROWS), F32),
        pltpu.VMEM((images, width, ROWS), BF16),
        pltpu.VMEM((2 * ROWS, cut), BF16),
    ]
    grads = [jax.ShapeDtypeStruct(full_up, BF16), jax.ShapeDtypeStruct(full_down, BF16)]
    return pl.pallas_call(
        middle_kernel,
        grid=(3 * pairs,),
        in_specs=[pl.BlockSpec(memory_space=pltpu.SMEM), phase(0), phase(1), phase(2), whole(norms.shape)] + [anywhere] * 3,
        out_specs=[phase(1), phase(2), phase(2), turned, whole((48, width)), whole((width, cut + width))]
        + [whole(grad.shape) for grad in grads],
        out_shape=[
            jax.ShapeDtypeStruct((rows, width), BF16),
            jax.ShapeDtypeStruct((rows, width), F32),
            jax.ShapeDtypeStruct((rows, width), BF16),
            jax.ShapeDtypeStruct((pairs, width, 2 * ROWS), BF16),
            jax.ShapeDtypeStruct((48, width), F32),
            jax.ShapeDtypeStruct((width, cut + width), BF16),
        ]
        + grads,
        scratch_shapes=scratch,
        compiler_params=pltpu.CompilerParams(vmem_limit_bytes=VMEM_BYTES),
        name="middle",
    )(grid, first, cotangent, projected, norms, w_mixed, w_up, w_down)


class Reduce:
    def __init__(self, terms, mine, result, cross, buffers, sems, base, fetch_sem=None):
        sends, receives = sems
        self.terms, self.mine, self.result, self.cross = terms, mine, result, cross
        self.layers = terms.shape[0]
        self.x, self.core, self.z, self.y = places(2)
        self.along_devices, across, sibling, beyond = peers_of(self.layers)
        buffers = list(buffers)
        every = (slice(None), slice(None))
        self.from_core, self.chip = buffers[:2]
        other = part_of(terms, every, 1 - self.core)
        self.inside = remote(other, self.from_core, sends, receives, base, sibling)
        self.fetch = None
        if mine is not None:
            self.fetch = pltpu.make_async_copy(part_of(terms, every, self.core), mine, fetch_sem)
        rest = buffers[2:]
        if cross:
            self.from_cross, self.wide = rest[:2]
            self.over_x = remote(part_of(self.chip, every, 1 - self.x), self.from_cross, sends, receives, base + 1, beyond)
            rest = rest[2:]
        else:
            self.wide = self.chip
        self.from_side, self.line, self.from_along, self.own, self.from_x, self.total = rest
        self.over = remote(self.wide.at[:, 1 - self.y], self.from_side, sends, receives, base + 2, across)
        self.along = [
            remote(self.line.at[self.z ^ (step + 1)], self.from_along.at[step], sends, receives, base + 3 + step, device)
            for step, device in enumerate(self.along_devices)
        ]
        base += 3 + self.layers - 1
        half = part_of(result, (), self.core)
        if cross:
            self.spot = part_of(half, (), self.x)
            self.beyond = remote(self.total, self.spot, sends, receives, base, beyond)
            self.back = remote(half, half, sends, receives, base + 1, sibling)
        else:
            self.spot = half
            self.beyond = remote(self.own, self.from_x, sends, receives, base, beyond)
            self.back = remote(self.total, half, sends, receives, base + 1, sibling)

    def start(self):
        self.inside.start()

    def add_core(self):
        if self.fetch is not None:
            self.fetch.wait()
        self.inside.wait_recv()
        for z in range(self.layers):
            for y in range(2):
                if self.mine is not None:
                    own = self.mine[z, y]
                else:
                    own = part_of(self.terms, (z, y), self.core)[...]
                self.chip[z, y] = own + self.from_core[z, y]
        (self.over_x if self.cross else self.over).start()

    def add_cross(self):
        self.over_x.wait_recv()
        for z in range(self.layers):
            for y in range(2):
                self.wide[z, y] = part_of(self.chip, (z, y), self.x)[...] + self.from_cross[z, y]
        self.over.start()

    def add_side(self):
        self.over.wait_recv()
        for z in range(self.layers):
            self.line[z] = self.wide[z, self.y] + self.from_side[z]
        for copy in self.along:
            copy.start()

    def add_line(self):
        mine = self.line[self.z].astype(F32)
        for step, copy in enumerate(self.along):
            copy.wait_recv()
            mine = mine + self.from_along[step].astype(F32)
        if self.cross:
            self.total[...] = mine
            self.spot[...] = mine
        else:
            self.own[...] = mine.astype(self.own.dtype)
        self.beyond.start()

    def add_x(self):
        self.beyond.wait_recv()
        if not self.cross:
            mine = self.own[...].astype(F32) + self.from_x[...].astype(F32)
            self.total[...] = mine
            self.spot[...] = mine
        self.back.start()

    def finish(self):
        self.back.wait_recv()
        copies = [self.inside, self.over, self.beyond, self.back] + self.along
        if self.cross:
            copies.append(self.over_x)
        for copy in copies:
            copy.wait_send()


def reduce_buffers(shape, dtype, cross):
    layers, sides = shape[:2]
    half = part_shape(shape[2:])
    last = part_shape(half) if cross else half
    buffers = [(layers, sides) + half] * 2
    if cross:
        buffers += [(layers, sides) + last] * 2
    buffers += [(layers,) + last] * 2 + [(layers - 1,) + last, last, last]
    return [pltpu.VMEM(buffer, dtype) for buffer in buffers] + [pltpu.VMEM(last, F32)]


def conv_backward_kernel(layers, *refs):
    quick = layers > 0
    take = iter(refs)
    tokens_t_hbm, keep_hbm, d_first_hbm, d_proj_hbm, d_proj_t_hbm = [next(take) for _ in range(5)]
    field_hbm, act_hbm, pull_hbm, expand_hbm, taps_ref, project_hbm = [next(take) for _ in range(6)]
    if quick:
        late_norm_ref = next(take)
        late = [next(take) for _ in range(3)]
    d_tokens_ref = next(take)
    if quick:
        results = [next(take) for _ in range(6)]
    else:
        g_expand_ref, g_project_ref, g_taps_ref = [next(take) for _ in range(3)]
    (d_image, field, act, pull, expand, project, load_sems) = [next(take) for _ in range(7)]
    (d_proj, d_proj_t, tokens_t, keep, taps_b, a_expand, a_project, a_taps) = [next(take) for _ in range(8)]
    frames = next(take)
    pairs, _, width = d_image.shape
    images = 2 * pairs
    chunks = field.shape[0] // 2
    hidden = chunks * CHUNK
    items = pairs * chunks
    per = pairs // 2

    if quick:
        stage_project, stage_small = next(take), next(take)
        stage_expand = [next(take) for _ in range(chunks)]
        mines = [next(take) for _ in range(3)]
        fetch_sems = next(take)
    loads = []
    for number, (source, target) in enumerate(
        (
            (d_proj_hbm, d_proj), (project_hbm, project), (d_proj_t_hbm, d_proj_t), (keep_hbm, keep),
            (tokens_t_hbm, tokens_t.at[0:pairs]), (d_first_hbm, d_image), (expand_hbm, expand),
        )
    ):
        loads.append(pltpu.make_async_copy(source, target, load_sems.at[number]))
    base = 7

    def stream(kind, chunk):
        source, target = ((act_hbm, act), (pull_hbm, pull), (field_hbm, field))[kind]
        two = pl.ds(2 * chunk, 2)
        return pltpu.make_async_copy(source.at[two], target.at[two], load_sems.at[base + kind * chunks + chunk])

    if quick:
        x, core, z, y = places(2)
        for index, (ref, mine) in enumerate(zip(late, mines)):
            pltpu.make_async_copy(part_of(ref, (slice(None), slice(None)), core), mine, fetch_sems.at[index]).start()
    for load in loads[:3]:
        load.start()
    for kind in range(3):
        stream(kind, 0).start()
    stream(0, 1).start()
    for load in loads[3:]:
        load.start()

    plan = {}
    if quick:
        number = 0
        rest = list(take)
        sems = rest[-2:]
        rest = rest[:-2]
        span = 3 + layers + 1

        def reducer(terms, mine, result, cross, fetch_sem=None):
            nonlocal number, rest
            count = 10 if cross else 8
            made = Reduce(terms, mine, result, cross, rest[:count], sems, number * span, fetch_sem)
            rest = rest[count:]
            number += 1
            return made

        mixed = reducer(late[0], mines[0], results[3], True, fetch_sems.at[0])
        up = reducer(late[1], mines[1], results[4], False, fetch_sems.at[1])
        down = reducer(late[2], mines[2], results[5], True, fetch_sems.at[2])
        whole_project = reducer(stage_project, None, results[2], True)
        parts = [
            reducer(stage_expand[c], None, results[1].at[:, c * CHUNK : (c + 1) * CHUNK], False) for c in range(chunks)
        ]
        small = reducer(stage_small, None, results[0], False)
        along, across, sibling, beyond = peers_of(layers)
        greet(along + [across, sibling, beyond])
        for part in (up, down, mixed):
            part.inside.start()

        def send_project():
            to_lines(a_project, stage_project)
            whole_project.start()

        def send_part(chunk):
            stage_expand[chunk][...] = a_expand[chunk].astype(BF16).reshape(stage_expand[chunk].shape)
            parts[chunk].start()

        def at(segment, *works):
            plan.setdefault(segment, []).extend(works)

        at(1, up.add_core, down.add_core, mixed.add_core)
        at(3, lambda: send_part(0))
        at(4, parts[0].add_core)
        at(5, up.add_side, down.add_cross, lambda: send_part(1))
        at(6, send_project, parts[1].add_core, parts[0].add_side)
        at(7, down.add_side, whole_project.add_core, lambda: send_part(2), parts[1].add_side)
        at(8, mixed.add_cross, up.add_line, parts[2].add_core)
        at(9, parts[0].add_line, parts[1].add_line, lambda: send_part(3), parts[2].add_side)
        at(10, mixed.add_side, down.add_line, up.add_x, parts[3].add_core)
        at(
            11, whole_project.add_cross, lambda: send_part(4), parts[0].add_x, parts[1].add_x, parts[2].add_line,
            parts[3].add_side,
        )

    a_taps[...] = jnp.zeros_like(a_taps)
    a_expand[...] = jnp.zeros_like(a_expand)
    a_project[...] = jnp.zeros_like(a_project)
    frames[...] = jnp.zeros_like(frames)
    tokens_t[pairs] = jnp.zeros((width, 2 * ROWS), BF16)
    spread_taps(taps_ref, taps_b)
    for load in loads:
        load.wait()

    def item(t):
        t = jnp.clip(t, 0, items - 1)
        return t // pairs, t % pairs

    def step(t, lead, new=True, old=True):
        c2, p2 = item(t - 2)
        c1, p1 = item(t - 1)
        c0, p0 = item(t)
        spot = pl.ds(pl.multiple_of(p2 * 2 * ROWS, 2 * ROWS), 2 * ROWS)
        done = both(act[2 * c2, spot, :], act[2 * c2 + 1, spot, :])
        a_expand[c2] += dot_nn(tokens_t[jnp.where(t < 2, pairs, p2)], done)
        if lead:
            cp, pp = t // 2, 2 * (t % 2)
            total = a_project[cp]
            for more in range(2):
                rows = pl.ds(pl.multiple_of((pp + more) * 2 * ROWS, 2 * ROWS), 2 * ROWS)
                total = total + dot_nn(d_proj_t[pp + more], both(act[2 * cp, rows, :], act[2 * cp + 1, rows, :]))
            a_project[cp] = total
        block = 64
        rows = block // GRID
        for half in range(CHUNK // 128 if old else 0):
            lanes = slice(half * 128, (half + 1) * 128)
            taps = [taps_b[c1, k, :, lanes] for k in range(9)]
            totals = [jnp.zeros((8, 128), F32) for _ in range(9)]
            for side in range(2):
                for start in range(0, ROWS, block):
                    spot = pl.ds(pl.multiple_of((2 * p1 + side) * ROWS, ROWS) + start, block)
                    own = field[2 * c1 + half, spot, :].reshape(rows, GRID, 128)
                    lines = []
                    for a in range(3):
                        line = None
                        for b in range(3):
                            k = 3 * a + b
                            at = start + GRID * (2 - a)
                            near = frames[side, b, half, at : at + block].reshape(rows, GRID, 128)
                            term = taps[k] * near
                            line = term if line is None else line + term
                            prod = near * own
                            quad = ((prod[0] + prod[1]) + (prod[2] + prod[3])).astype(F32)
                            totals[k] = totals[k] + (quad[:8] + quad[8:])
                        lines.append(line)
                    grad = (lines[0] + lines[1] + lines[2]).reshape(block, 128)
                    act[2 * c1 + half, spot, :] = grad * keep[2 * p1 + side, start : start + block, :]
            for k in range(9):
                a_taps[c1, 8 * k : 8 * k + 8, lanes] += totals[k]
        if not new:
            return
        d_act = dot_nt(d_proj[p0], project[c0])
        for half in range(CHUNK // 128):
            lanes = slice(half * 128, (half + 1) * 128)
            for side in range(2):
                spot = pl.ds(pl.multiple_of((2 * p0 + side) * ROWS, ROWS), ROWS)
                d_conv = d_act[side * ROWS : (side + 1) * ROWS, lanes] * pull[2 * c0 + half, spot, :].astype(F32)
                frames[side, 0, half, GRID : GRID + ROWS] = move_cells(d_conv, -1).astype(BF16)
                frames[side, 1, half, GRID : GRID + ROWS] = d_conv.astype(BF16)
                frames[side, 2, half, GRID : GRID + ROWS] = move_cells(d_conv, 1).astype(BF16)

    def segment(s, lead):
        for key in plan:
            @pl.when(s == key)
            def _(works=plan[key]):
                for work in works:
                    work()

        if lead:
            stream(0, s).wait()

            @pl.when(s < chunks - 2)
            def _():
                stream(0, s + 2).start()

        @pl.when(s % 2 == 0)
        def _():
            stream(1, s // 2).wait()
            stream(2, s // 2).wait()

            @pl.when(s // 2 < chunks - 1)
            def _():
                stream(1, s // 2 + 1).start()
                stream(2, s // 2 + 1).start()

        @pl.loop(0, per)
        def _(turn):
            step(s * per + turn, lead)

    middle_segment = chunks
    pl.loop(0, middle_segment)(lambda s: segment(s, True))
    pl.loop(middle_segment, 2 * chunks)(lambda s: segment(s, False))
    step(items, False, new=False)
    step(items + 1, False, new=False, old=False)

    def finish_pair(pair):
        spot = slice(2 * pair * ROWS, 2 * (pair + 1) * ROWS)
        left = jnp.concatenate([act[line, spot, :] for line in range(2 * chunks)], axis=1)
        right = jnp.concatenate([expand[chunk] for chunk in range(chunks)], axis=1)
        d_tokens_ref[spot, :] = (d_image[pair] + dot_nt(left, right)).astype(BF16)


    if not quick:
        for chunk in range(chunks):
            g_expand_ref[:, chunk * CHUNK : (chunk + 1) * CHUNK] = a_expand[chunk].astype(BF16)
            g_project_ref[chunk * CHUNK : (chunk + 1) * CHUNK, :] = a_project[chunk].astype(BF16).T
            g_taps_ref[:, chunk * CHUNK : (chunk + 1) * CHUNK] = a_taps[chunk]
        for pair in range(pairs):
            finish_pair(pair)
        return

    whole_project.add_side()
    send_part(chunks - 1)
    parts[4].add_core()
    lines = []
    for k in range(9):
        line = jnp.concatenate([a_taps[c, 8 * k : 8 * k + 8, :] for c in range(chunks)], axis=1)
        lines.append(jnp.sum(line, axis=0, keepdims=True))
    depth = jnp.concatenate(lines, axis=0)
    vectors = [late_norm_ref[8 * k : 8 * k + 8] for k in (4, 5, 2, 3, 0, 1)]
    vectors = jnp.concatenate([jnp.sum(vector, axis=0, keepdims=True) for vector in vectors], axis=0)
    share, thin = hidden // (2 * layers), width // (2 * layers)
    stage_small[...] = jnp.zeros_like(stage_small)
    for f in range(2 * layers):
        stage_small[f // 2, f % 2, 0:9, 0:share] = depth[:, f * share : (f + 1) * share]
        stage_small[f // 2, f % 2, 9:15, 0:thin] = vectors[:, f * thin : (f + 1) * thin]
    small.start()
    parts[5].add_core()
    finish_pair(0)
    small.add_core()
    parts[4].add_side()
    parts[3].add_line()
    parts[2].add_x()
    down.add_x()
    finish_pair(1)
    parts[5].add_side()
    small.add_side()
    mixed.add_line()
    finish_pair(2)
    whole_project.add_line()
    parts[4].add_line()
    parts[5].add_line()
    small.add_line()
    parts[3].add_x()
    mixed.add_x()
    finish_pair(3)
    whole_project.add_x()
    parts[4].add_x()
    parts[5].add_x()
    small.add_x()
    for part in [up, down, mixed, whole_project, small] + parts:
        part.finish()


def conv_backward(tokens_t, keep, d_first, d_proj, d_proj_t, field, act, pull, w_expand, taps, w_project, late=None):
    rows, width = d_first.shape
    chunks = w_expand.shape[0]
    hidden = chunks * CHUNK
    images = rows // ROWS
    anywhere = pl.BlockSpec(memory_space=pl.ANY)
    here = pl.BlockSpec(memory_space=pltpu.VMEM)
    pairs = images // 2
    by_pair = (pairs, 2 * ROWS, width)
    wide = (2 * chunks, rows, 128)
    scratch = [
        pltpu.VMEM(by_pair, F32),
        pltpu.VMEM(wide, BF16),
        pltpu.VMEM(wide, BF16),
        pltpu.VMEM(wide, BF16),
        pltpu.VMEM((chunks, width, CHUNK), BF16),
        pltpu.VMEM((chunks, CHUNK, width), BF16),
        pltpu.SemaphoreType.DMA((7 + chunks * 3,)),
        pltpu.VMEM((pairs, 2 * ROWS, width), BF16),
        pltpu.VMEM((pairs, width, 2 * ROWS), BF16),
        pltpu.VMEM((pairs + 1, width, 2 * ROWS), BF16),
        pltpu.VMEM((images, ROWS, 128), BF16),
        pltpu.VMEM((chunks, 9, GRID, CHUNK), BF16),
        pltpu.VMEM((chunks, width, CHUNK), F32),
        pltpu.VMEM((chunks, width, CHUNK), F32),
        pltpu.VMEM((chunks, 72, CHUNK), F32),
    ]
    scratch += [pltpu.VMEM((2, 3, 2, ROWS + 2 * GRID, 128), BF16)]
    operands = [
        tokens_t, keep.reshape(images, ROWS, 128), d_first.reshape(by_pair), d_proj.reshape(by_pair), d_proj_t,
        field, act, pull, w_expand, taps, w_project.reshape(chunks, CHUNK, width),
    ]
    in_specs = [anywhere] * 9 + [here, anywhere]
    d_tokens = jax.ShapeDtypeStruct((rows, width), BF16)
    if late is None:
        layers, params = 0, {}
        out_shape = [
            d_tokens,
            jax.ShapeDtypeStruct((width, hidden), BF16),
            jax.ShapeDtypeStruct(w_project.shape, BF16),
            jax.ShapeDtypeStruct((72, hidden), F32),
        ]
    else:
        g_norm, g_mixed, g_up, g_down = late
        layers = g_up.shape[0]
        params = dict(collective_id=1, has_side_effects=True)
        operands += [g_norm, g_mixed, g_up, g_down]
        in_specs += [here] + [anywhere] * 3
        span = -(-hidden // (2 * layers) // 128) * 128
        b_small, b_expand, b_project = (16, span), (width // (2 * layers), hidden), (hidden // (2 * layers), width)
        blocks = (b_small, b_expand, b_project, g_mixed.shape[2:], g_up.shape[2:], g_down.shape[2:])
        out_shape = [d_tokens] + [jax.ShapeDtypeStruct(block, F32) for block in blocks]
        lead = (layers, 2)
        piece = (b_expand[0], CHUNK)
        scratch += [pltpu.VMEM(lead + b_project, BF16), pltpu.VMEM(lead + b_small, F32)]
        scratch += [pltpu.VMEM(lead + piece, BF16)] * chunks
        scratch += [pltpu.VMEM(lead + part_shape(block), BF16) for block in blocks[3:]]
        scratch += [pltpu.SemaphoreType.DMA((3,))]
        for shape, dtype, cross in (
            [(blocks[3], BF16, True), (blocks[4], BF16, False), (blocks[5], BF16, True), (blocks[2], BF16, True)]
            + [(piece, BF16, False)] * chunks
            + [(b_small, F32, False)]
        ):
            scratch += reduce_buffers(lead + shape, dtype, cross)
        copies = (5 + chunks) * (4 + layers)
        scratch += [pltpu.SemaphoreType.DMA((copies,))] * 2
    return pl.pallas_call(
        functools.partial(conv_backward_kernel, layers),
        in_specs=in_specs,
        out_specs=[here] * len(out_shape),
        out_shape=out_shape,
        scratch_shapes=scratch,
        compiler_params=pltpu.CompilerParams(vmem_limit_bytes=VMEM_BYTES, **params),
        name="conv_backward",
    )(*operands)


def deliver_kernel(*refs):
    tokens_in, small_ref, *blocks = refs[:7]
    tokens_out, depth_ref, *rest = refs[7:]
    vectors, outs = rest[:6], rest[6:]
    expand, project, mixed, up, down = blocks
    cut = outs[2].shape[1]
    pairs = [(tokens_in, tokens_out), (expand, outs[0]), (project, outs[1])]
    pairs += [(mixed.at[:, :cut], outs[2]), (mixed.at[:, cut:], outs[3]), (up, outs[4]), (down, outs[5])]
    for source, target in pairs:
        target[...] = source[...]
    depth_ref[...] = small_ref[0 : depth_ref.shape[0], 0 : depth_ref.shape[1]]
    for line, ref in enumerate(vectors):
        ref[...] = small_ref[9 + line, 0 : ref.shape[0]]


def deliver(d_tokens, small, s_expand, s_project, s_mixed, s_up, s_down, share, thin):
    rows, width = s_mixed.shape[0], s_project.shape[1]
    here = pl.BlockSpec(memory_space=pltpu.VMEM)
    blocks = [s_expand.shape, s_project.shape, (rows, 3 * width), (rows, width), s_up.shape, s_down.shape]
    return pl.pallas_call(
        deliver_kernel,
        in_specs=[here] * 7,
        out_specs=[here] * 14,
        out_shape=[jax.ShapeDtypeStruct(d_tokens.shape, BF16), jax.ShapeDtypeStruct((9, share), F32)]
        + [jax.ShapeDtypeStruct((thin,), F32)] * 6
        + [jax.ShapeDtypeStruct(block, F32) for block in blocks],
        compiler_params=pltpu.CompilerParams(vmem_limit_bytes=VMEM_BYTES),
        name="deliver",
    )(d_tokens, small, s_expand, s_project, s_mixed, s_up, s_down)


def reduce_plain(terms):
    results = []
    for term in terms:
        share = lax.psum_scatter(term, "fsdp", scatter_dimension=0, tiled=False)
        results.append(lax.psum(share, "dp").astype(F32))
    return results


def local(
    fsdp, quick,
    tokens, grid, w_expand, w_depth, w_project, gain_conv, bias_conv, gain_attend, bias_attend,
    w_qkv, w_out, gain_mlp, bias_mlp, w_up, w_down, cotangent,
):
    slots, rows, width = tokens.shape
    hidden = w_expand.shape[1]
    share, thin = w_depth.shape[1], gain_conv.shape[0]
    span = -(-share // 128) * 128
    vectors = (gain_conv, bias_conv, gain_attend, bias_attend, gain_mlp, bias_mlp)
    grid = grid.T
    flat, cotan = tokens.reshape(slots * rows, width), cotangent.reshape(slots * rows, width)
    if quick:
        field, act, pull, projected, first, tokens_t, keep, taps, norms, *fulls = gather_forward(
            grid, flat, w_depth, vectors, w_expand, w_project, w_qkv, w_out, w_up, w_down, fsdp // 2
        )
        f_expand = fulls[0]
        f_project, f_mixed, f_up, f_down = [full.reshape(-1, full.shape[3]) for full in fulls[1:]]
    else:
        mixed = jnp.concatenate((w_qkv, w_out), axis=1)
        f_expand, f_project, f_mixed, f_up, f_down = [
            lax.all_gather(shard, "fsdp", axis=0, tiled=True) for shard in (w_expand, w_project, mixed, w_up, w_down)
        ]
        f_expand = f_expand.reshape(width, hidden // CHUNK, CHUNK).transpose(1, 0, 2)
        taps = jnp.pad(lax.all_gather(w_depth, "fsdp", axis=1, tiled=True).astype(F32), ((0, 7), (0, 0)))
        lines = lax.all_gather(jnp.stack(vectors), "fsdp", axis=1, tiled=True).astype(F32)
        norms = jnp.pad(lines, ((1, 1), (0, 0)))
        field, act, pull, projected, first, tokens_t, keep = conv_forward(
            grid, flat, f_expand, taps, f_project, norms
        )
    layer_out, d_first, d_proj, d_proj_t, g_norm, g_mixed, g_up, g_down = middle(
        grid, first, cotan, projected, f_mixed, f_up, f_down, norms
    )
    inputs = (tokens_t, keep, d_first, d_proj, d_proj_t, field, act, pull, f_expand, taps, f_project)
    if quick:
        late = [term.reshape((fsdp // 2, 2, -1, term.shape[1])) for term in (g_mixed, g_up, g_down)]
        d_tokens, small, s_expand, s_project, s_mixed, s_up, s_down = conv_backward(*inputs, late=[g_norm] + late)
    else:
        d_tokens, g_expand, g_project, g_taps = conv_backward(*inputs)
        g_taps = jnp.sum(g_taps.reshape(9, 8, fsdp, share), axis=1)
        g_norm = jnp.concatenate((g_norm[32:], g_norm[16:32], g_norm[:16]), axis=0)
        g_norm = jnp.sum(g_norm.reshape(6, 8, fsdp, thin), axis=1)
        g_small = jnp.concatenate(
            (
                jnp.pad(g_taps, ((0, 0), (0, 0), (0, span - share))),
                jnp.pad(g_norm, ((0, 1), (0, 0), (0, span - thin))),
            ),
            axis=0,
        ).transpose(1, 0, 2)
        terms = [g_small] + [
            term.reshape((fsdp, -1, term.shape[1])) for term in (g_expand, g_project, g_mixed, g_up, g_down)
        ]
        small, s_expand, s_project, s_mixed, s_up, s_down = reduce_plain(terms)
    d_tokens, depth, *rest = deliver(d_tokens, small, s_expand, s_project, s_mixed, s_up, s_down, share, thin)
    vectors, (s_expand, s_project, s_qkv, s_out, s_up, s_down) = rest[:6], rest[6:]
    return (
        layer_out.reshape(tokens.shape),
        d_tokens.reshape(tokens.shape),
        s_expand,
        depth,
        s_project,
        *vectors[:4],
        s_qkv,
        s_out,
        *vectors[4:],
        s_up,
        s_down,
    )


def solution(mesh):
    fsdp, dp = mesh.shape["fsdp"], mesh.shape["dp"]
    quick = fsdp == 8 and dp == 4
    images, wide, tall, vector = P(("dp", "fsdp"), None, None), P("fsdp", None), P(None, "fsdp"), P("fsdp")
    in_specs = (
        images, P(("dp", "fsdp"), None), wide, tall, wide, vector, vector, vector, vector,
        wide, wide, vector, vector, wide, wide, images,
    )
    out_specs = (
        images, images, wide, tall, wide, vector, vector, vector, vector,
        wide, wide, vector, vector, wide, wide,
    )
    return jax.shard_map(
        functools.partial(local, fsdp, quick), mesh=mesh, in_specs=in_specs, out_specs=out_specs, check_vma=False
    )
```
